32 devices in a mesh: groups: 2 (over x), ex: 4 (over y, core), layer: 4 (over z).
Axes of the slice: x: 2, y: 2, z: 4, core: 2. Of those that a mesh axis runs over, the one named last changes fastest.
Arguments:
- queries: bfloat16 [512, 4, 4096], P(None, 'layer', 'ex'), may hold values from -6 to 6
- hessian: bfloat16 [4, 4096, 4096], P('layer', 'ex'), as said below
- store: bfloat16 [10240, 4, 4096], P(('groups', 'ex'), 'layer'), parts along dimension 0, may hold values from -0.09375 to 0.09375
Outputs:
- scores: float32 [10240, 512], P(('groups', 'ex', 'layer')), parts along dimension 0
The draws below stay inside these ranges and needn't reach their ends.
There are 2 independent parts, one for each index of `groups`. The reference program is written for one: setup_inputs(seed, part) draws one part's arguments, and reference() takes and returns one part's arrays. A program takes and returns all parts, laid end to end along the dimension named above; an argument that names none is the same for every part. Nothing has to cross between parts.
Inputs may be any that keep to these rules, and one draw needn't show every extreme that they name: `hessian`: each layer's block is symmetric with a positive diagonal and full-rank off-diagonal part.
All inputs are finite; a program needn't handle non-finite values.
Results may differ from the reference program's by a relative error of at most 0.0029.
Values may be sent and summed in bfloat16 or wider, within the bound.
No kernel may reach another device: no remote copies, remote signals or barrier semaphores. Data moves between devices by JAX's collectives and lax.ppermute only.
A program may use at most 128 MiB of HBM per device.

```python
import jax
import jax.numpy as jnp
from jax import lax

P_SIZE = 4096
QUERIES = 512
LAYERS = 4
EXAMPLES = 5120


def draw_hessian(key, part):
    key = jax.random.fold_in(key, 11)
    key_diag, key_off = jax.random.split(key)
    diag_vals = jnp.exp(jax.random.uniform(key_diag, (LAYERS, P_SIZE, 1), jnp.float32, jnp.log(0.5), jnp.log(2.0)))
    off_part = jax.random.normal(key_off, (LAYERS, P_SIZE, P_SIZE), jnp.float32)
    off_part = off_part * (0.5 / jnp.sqrt(jnp.float32(P_SIZE)))
    off_part = (off_part + jnp.swapaxes(off_part, 1, 2)) * 0.70710678
    rows_idx = jnp.arange(P_SIZE)[:, None]
    cols_idx = jnp.arange(P_SIZE)[None, :]
    eye_mask = (rows_idx == cols_idx).astype(jnp.float32)[None]
    return (off_part * (1.0 - eye_mask) + eye_mask * diag_vals).astype(jnp.bfloat16)


def steps_of(key, dims, cuts, least, high):
    def one(axis_at, parts):
        heights = jax.random.uniform(jax.random.fold_in(jax.random.fold_in(key, 6), axis_at), (parts,), jnp.float32, least / len(cuts), high / len(cuts))
        return jnp.repeat(jnp.exp(heights), dims[axis_at] // parts).reshape((-1,) + (1,) * (len(dims) - axis_at - 1))

    gain = one(*cuts[0])
    for cut in cuts[1:]:
        gain = gain * one(*cut)
    return gain


def bell_draw(key, extent, spread, reach, cuts=(), held_as=jnp.bfloat16):
    entries = spread * jax.random.normal(key, extent, jnp.float32)
    if cuts:
        entries = entries * steps_of(key, extent, cuts, -0.22, 0.18)
    return jnp.clip(entries, -reach, reach).astype(held_as)


def setup_inputs(seed: int = 0, part: int = 0) -> dict:
    splits = jax.random.split(jax.random.key(seed), 4)
    part_splits = jax.random.split(jax.random.fold_in(splits[3], part), 4)
    return {
        "queries": bell_draw(splits[0], (QUERIES, LAYERS, P_SIZE), 1.0, 6.0, ((1, 4), (2, 4))),
        "hessian": draw_hessian(jax.random.fold_in(splits[3], 71), part),
        "store": bell_draw(part_splits[2], (EXAMPLES, LAYERS, P_SIZE), P_SIZE ** -0.5, 0.09375, ((0, 4), (1, 4))),
    }


def reference(queries, hessian, store):
    total = jnp.zeros((store.shape[0], queries.shape[0]), jnp.float32)
    for index in range(LAYERS):
        query_rows = queries[:, index, :].astype(jnp.float32)
        block = hessian[index].astype(jnp.float32)
        conditioned = jnp.dot(query_rows, block, precision=lax.Precision.HIGHEST)
        conditioned = conditioned.T.astype(jnp.bfloat16).astype(jnp.float32)
        store_rows = store[:, index, :].astype(jnp.float32)
        total = total + jnp.dot(store_rows, conditioned, precision=lax.Precision.HIGHEST)
    return total
```

```python
import functools

import jax
import jax.numpy as jnp
from jax import lax
from jax.experimental import pallas as pl
from jax.experimental.pallas import tpu as pltpu
from jax.sharding import PartitionSpec as P

F32, BF16 = jnp.float32, jnp.bfloat16
CORES = 2
CHUNKS = 2
MIB = 1 << 20
VMEM = pl.BlockSpec(memory_space=pltpu.VMEM)
SMEM = pl.BlockSpec(memory_space=pltpu.SMEM)
ANY = pl.BlockSpec(memory_space=pl.ANY)


def load_kernel(hess_hbm, store_hbm, hess_ref, store_ref, sems):
    copies = [
        pltpu.make_async_copy(hess_hbm, hess_ref, sems.at[0]),
        pltpu.make_async_copy(store_hbm, store_ref, sems.at[1]),
    ]
    for copy in copies:
        copy.start()
    for copy in copies:
        copy.wait()


def load(hess, store):
    return pl.pallas_call(
        load_kernel,
        out_shape=(pltpu.VMEM(hess.shape, BF16), pltpu.VMEM(store.shape, BF16)),
        in_specs=[ANY, ANY],
        out_specs=(VMEM, VMEM),
        scratch_shapes=[pltpu.SemaphoreType.DMA((2,))],
        compiler_params=pltpu.CompilerParams(vmem_limit_bytes=2 * MIB),
    )(hess, store)


def condition_kernel(count, ids, hess, *rest):
    pieces, out, total = rest[:count], rest[count], rest[count + 1]
    width = hess.shape[1] // count
    for t, piece in enumerate(pieces):
        columns = pl.ds(pl.multiple_of(ids[t] * width, width), width)
        part = lax.dot_general(
            hess[:, columns], piece[...], (((1,), (1,)), ((), ())), preferred_element_type=F32
        )
        if t:
            total[...] += part
        else:
            total[...] = part
    out[...] = total[...].astype(BF16)


def condition(ids, hess, pieces):
    rows, queries = hess.shape[0], pieces[0].shape[0]
    return pl.pallas_call(
        functools.partial(condition_kernel, len(pieces)),
        out_shape=jax.ShapeDtypeStruct((rows, queries), BF16),
        in_specs=[SMEM] + [VMEM] * (1 + len(pieces)),
        out_specs=VMEM,
        scratch_shapes=[pltpu.VMEM((rows, queries), F32)],
        compiler_params=pltpu.CompilerParams(vmem_limit_bytes=16 * MIB),
    )(ids, hess, *pieces)


def score_kernel(groups, count, ids, blocks, store, *rest):
    pieces = rest[: groups * count]
    send, keep, right = rest[groups * count :]
    rows = send.shape[1]
    depth, width = pieces[0].shape
    for t in range(count):
        at = pl.ds(pl.multiple_of(ids[t] * depth, depth), depth)
        for j in range(groups):
            right[at, j * width : (j + 1) * width] = pieces[t * groups + j][...]
    for r in range(2 * send.shape[0]):
        at = pl.ds(pl.multiple_of(blocks[r] * rows, rows), rows)
        part = jnp.dot(store[at, :], right[...], preferred_element_type=F32)
        if r % 2:
            send[r // 2] = part.astype(BF16)
        else:
            keep[r // 2] = part


def score(ids, blocks, store, pieces, groups):
    count = len(pieces) // groups
    depth, width = pieces[0].shape
    layers = blocks.shape[0]
    shape = (layers // 2, store.shape[0] // layers, groups * width)
    return pl.pallas_call(
        functools.partial(score_kernel, groups, count),
        out_shape=(jax.ShapeDtypeStruct(shape, BF16), jax.ShapeDtypeStruct(shape, F32)),
        in_specs=[SMEM, SMEM] + [VMEM] * (1 + len(pieces)),
        out_specs=(VMEM, VMEM),
        scratch_shapes=[pltpu.VMEM((count * depth, groups * width), BF16)],
        compiler_params=pltpu.CompilerParams(vmem_limit_bytes=24 * MIB),
    )(ids, blocks, store, *pieces)


def fold_kernel(keep, got, send, left):
    for r in range(keep.shape[0]):
        total = keep[r] + got[r].astype(F32)
        if r % 2:
            send[r // 2] = total.astype(BF16)
        else:
            left[r // 2] = total


def fold(keep, got):
    shape = (keep.shape[0] // 2,) + keep.shape[1:]
    return pl.pallas_call(
        fold_kernel,
        out_shape=(jax.ShapeDtypeStruct(shape, BF16), jax.ShapeDtypeStruct(shape, F32)),
        in_specs=[VMEM, VMEM],
        out_specs=(VMEM, VMEM),
        compiler_params=pltpu.CompilerParams(vmem_limit_bytes=16 * MIB),
    )(keep, got)


def finish_kernel(chunks, groups, place, *refs):
    out = refs[2 * chunks]
    span = out.shape[1] // groups
    width = span // chunks
    for c in range(chunks):
        keep, got = refs[2 * c], refs[2 * c + 1]
        total = keep[0] + got[0].astype(F32)
        for j in range(groups):
            at = pl.multiple_of(place[j] * span + c * width, width)
            out[:, pl.ds(at, width)] = total[:, j * width : (j + 1) * width]


def finish(place, pairs, queries):
    groups = place.shape[0]
    rows = pairs[0][0].shape[1]
    return pl.pallas_call(
        functools.partial(finish_kernel, len(pairs), groups),
        out_shape=jax.ShapeDtypeStruct((rows, queries), F32),
        in_specs=[SMEM] + [VMEM] * (2 * len(pairs)),
        out_specs=VMEM,
        compiler_params=pltpu.CompilerParams(vmem_limit_bytes=16 * MIB),
    )(place, *[a for pair in pairs for a in pair])


def shards(groups, ex, layers, queries, hessian, store):
    chips = ex // CORES
    at_group, at_ex, at_layer = (lax.axis_index(a) for a in ("groups", "ex", "layer"))
    chip, core = at_ex // CORES, at_ex % CORES
    ids = jnp.stack(
        [(chip + k) % chips * CORES + (core ^ s) for k in range(chips) for s in range(CORES)]
    ).astype(jnp.int32)
    blocks = jnp.stack([at_layer ^ r for r in range(layers)]).astype(jnp.int32)
    place = jnp.stack([(at_group + j) % groups for j in range(groups)]).astype(jnp.int32)

    def from_chip(x, k):
        perm = [(e, (e - k * CORES) % ex) for e in range(ex)]
        return lax.ppermute(x, "ex", perm)

    def from_core(x):
        return lax.ppermute(x, "ex", [(e, e ^ 1) for e in range(ex)])

    def from_group(x, j):
        return lax.ppermute(x, "groups", [(g, (g - j) % groups) for g in range(groups)])

    def from_layer(x, b):
        return lax.ppermute(x, "layer", [(z, z ^ b) for z in range(layers)])

    hess, rows = load(hessian[0], store[:, 0, :])
    total = queries.shape[0]
    span = total // groups
    width = span // CHUNKS
    pairs = []
    last = None
    for c in range(CHUNKS):
        mine = lax.dynamic_slice_in_dim(queries[:, 0, :], at_group * span + c * width, width, 0)
        if last is not None:
            mine, last = lax.optimization_barrier((mine, last))
        pieces = []
        for k in range(chips):
            here = from_chip(mine, k) if k else mine
            pieces += [here, from_core(here)]
            last = here
        share = condition(ids, hess, pieces)
        held = []
        for k in range(chips):
            here = from_chip(share, k) if k else share
            across = [from_group(here, j) if j else here for j in range(groups)]
            held += across + [from_core(x) for x in across]
        send, keep = score(ids, blocks, rows, held, groups)
        step = 1
        while True:
            got = from_layer(send, step)
            if keep.shape[0] == 1:
                break
            send, keep = fold(keep, got)
            step *= 2
        pairs.append((keep, got))
    return finish(place, pairs, total)


def solution(mesh):
    groups, ex, layers = (mesh.shape[a] for a in ("groups", "ex", "layer"))
    in_specs = (P(None, "layer", "ex"), P("layer", "ex", None), P(("groups", "ex"), "layer", None))
    out_specs = P(("groups", "ex", "layer"), None)
    return jax.shard_map(
        functools.partial(shards, groups, ex, layers),
        mesh=mesh,
        in_specs=in_specs,
        out_specs=out_specs,
        check_vma=False,
    )
```

```python
import functools

import jax
import jax.numpy as jnp
from jax import lax
from jax.experimental import pallas as pl
from jax.experimental.pallas import tpu as pltpu
from jax.sharding import PartitionSpec as P

F32, BF16 = jnp.float32, jnp.bfloat16
CORES = 2
CHUNKS = 2
MIB = 1 << 20
VMEM = pl.BlockSpec(memory_space=pltpu.VMEM)
SMEM = pl.BlockSpec(memory_space=pltpu.SMEM)
ANY = pl.BlockSpec(memory_space=pl.ANY)


HBM = pl.BlockSpec(memory_space=pltpu.HBM)


def load_kernel(source, after, out, sem):
    copy = pltpu.make_async_copy(source, out, sem)
    copy.start()
    copy.wait()


def load(source, after):
    return pl.pallas_call(
        load_kernel,
        out_shape=pltpu.VMEM(source.shape, BF16),
        in_specs=[HBM, ANY],
        out_specs=VMEM,
        scratch_shapes=[pltpu.SemaphoreType.DMA],
        compiler_params=pltpu.CompilerParams(vmem_limit_bytes=2 * MIB),
        cost_estimate=pl.CostEstimate(flops=0, bytes_accessed=source.size * 2, transcendentals=0),
    )(pltpu.with_memory_space_constraint(source, pltpu.HBM), after)


def take_kernel(start, source, after, out, sem):
    at = pl.ds(pl.multiple_of(start[0], out.shape[0]), out.shape[0])
    copy = pltpu.make_async_copy(source.at[at, :], out, sem)
    copy.start()
    copy.wait()


def take(start, source, after, rows):
    return pl.pallas_call(
        take_kernel,
        out_shape=pltpu.VMEM((rows, source.shape[1]), BF16),
        in_specs=[SMEM, HBM, ANY],
        out_specs=VMEM,
        scratch_shapes=[pltpu.SemaphoreType.DMA],
        compiler_params=pltpu.CompilerParams(vmem_limit_bytes=2 * MIB),
        cost_estimate=pl.CostEstimate(flops=0, bytes_accessed=2 * rows * source.shape[1], transcendentals=0),
    )(start, pltpu.with_memory_space_constraint(source, pltpu.HBM), after)


def condition_kernel(count, ids, hess, *rest):
    pieces, out, right = rest[:count], rest[count], rest[count + 1]
    width = hess.shape[1] // count
    for t, piece in enumerate(pieces):
        right[:, pl.ds(pl.multiple_of(ids[t] * width, width), width)] = piece[...]
    out[...] = lax.dot_general(
        hess[...], right[...], (((1,), (1,)), ((), ())), preferred_element_type=F32
    ).astype(BF16)


def condition(ids, hess, pieces):
    rows, queries = hess.shape[0], pieces[0].shape[0]
    return pl.pallas_call(
        functools.partial(condition_kernel, len(pieces)),
        out_shape=jax.ShapeDtypeStruct((rows, queries), BF16),
        in_specs=[SMEM] + [VMEM] * (1 + len(pieces)),
        out_specs=VMEM,
        scratch_shapes=[pltpu.VMEM((queries, hess.shape[1]), BF16)],
        compiler_params=pltpu.CompilerParams(vmem_limit_bytes=12 * MIB),
        cost_estimate=pl.CostEstimate(
            flops=2 * queries * hess.size, bytes_accessed=hess.size * 2, transcendentals=0
        ),
    )(ids, hess, *pieces)


def score_kernel(groups, count, ids, blocks, store, *rest):
    pieces = rest[: groups * count]
    keep, *send, right = rest[groups * count :]
    rows = keep.shape[0]
    depth, width = pieces[0].shape
    for t in range(count):
        at = pl.ds(pl.multiple_of(ids[t] * depth, depth), depth)
        for j in range(groups):
            right[at, j * width : (j + 1) * width] = pieces[t * groups + j][...]
    for r in range(blocks.shape[0]):
        at = pl.ds(pl.multiple_of(blocks[r] * rows, rows), rows)
        part = jnp.dot(store[at, :], right[...], preferred_element_type=F32)
        if r:
            send[r - 1][...] = part.astype(BF16)
        else:
            keep[...] = part


def score(ids, blocks, store, pieces, groups):
    count = len(pieces) // groups
    depth, width = pieces[0].shape
    layers = blocks.shape[0]
    shape = (store.shape[0] // layers, groups * width)
    return pl.pallas_call(
        functools.partial(score_kernel, groups, count),
        out_shape=(jax.ShapeDtypeStruct(shape, F32),)
        + (jax.ShapeDtypeStruct(shape, BF16),) * (layers - 1),
        in_specs=[SMEM, SMEM] + [VMEM] * (1 + len(pieces)),
        out_specs=(VMEM,) * layers,
        scratch_shapes=[pltpu.VMEM((count * depth, groups * width), BF16)],
        compiler_params=pltpu.CompilerParams(vmem_limit_bytes=12 * MIB),
        cost_estimate=pl.CostEstimate(
            flops=2 * groups * width * store.size, bytes_accessed=store.size * 2, transcendentals=0
        ),
    )(ids, blocks, store, *pieces)


def finish_kernel(chunks, groups, place, *refs):
    *refs, out = refs
    span = out.shape[1] // groups
    width = span // chunks
    count = len(refs) // chunks
    for c in range(chunks):
        total = refs[c * count][...]
        for got in refs[c * count + 1 : (c + 1) * count]:
            total = total + got[...].astype(F32)
        for j in range(groups):
            at = pl.multiple_of(place[j] * span + c * width, width)
            out[:, pl.ds(at, width)] = total[:, j * width : (j + 1) * width]


def finish(place, parts, queries):
    groups = place.shape[0]
    rows = parts[0][0].shape[0]
    return pl.pallas_call(
        functools.partial(finish_kernel, len(parts), groups),
        out_shape=jax.ShapeDtypeStruct((rows, queries), F32),
        in_specs=[SMEM] + [VMEM] * sum(map(len, parts)),
        out_specs=VMEM,
        compiler_params=pltpu.CompilerParams(vmem_limit_bytes=12 * MIB),
    )(place, *[a for part in parts for a in part])


def shards(groups, ex, layers, queries, hessian, store):
    chips = ex // CORES
    at_group, at_ex, at_layer = (lax.axis_index(a) for a in ("groups", "ex", "layer"))
    chip, core = at_ex // CORES, at_ex % CORES
    ids = jnp.stack(
        [(chip + k) % chips * CORES + (core ^ s) for k in range(chips) for s in range(CORES)]
    ).astype(jnp.int32)
    blocks = jnp.stack([at_layer ^ r for r in range(layers)]).astype(jnp.int32)
    place = jnp.stack([(at_group + j) % groups for j in range(groups)]).astype(jnp.int32)

    def from_chip(x, k):
        perm = [(e, (e - k * CORES) % ex) for e in range(ex)]
        return lax.ppermute(x, "ex", perm)

    def from_core(x):
        return lax.ppermute(x, "ex", [(e, e ^ 1) for e in range(ex)])

    def from_group(x, j):
        return lax.ppermute(x, "groups", [(g, (g - j) % groups) for g in range(groups)])

    def from_layer(x, r):
        return lax.ppermute(x, "layer", [(z, z ^ r) for z in range(layers)])

    def tie(x, *others):
        return lax.optimization_barrier((x, *others))[0]

    total = queries.shape[0]
    span = total // groups
    width = span // CHUNKS

    pieces, last = [], ids
    for c in range(CHUNKS):
        start = (at_group * span + c * width).astype(jnp.int32)[None]
        mine = take(start, queries[:, 0, :], last, width)
        there = [from_chip(mine, k) for k in range(1, chips)]
        last = there[-1]
        pieces.append([p for x in [mine] + there for p in (x, from_core(x))])

    hess = load(hessian[0], ids)
    shares, held, last = [], [], ()
    for c in range(CHUNKS):
        share = condition(ids, hess, pieces[c])
        shares.append(share)
        share = tie(share, *last)
        columns = [share] + [from_chip(share, k) for k in range(1, chips)]
        first = [from_group(share, j) for j in range(1, groups)]
        last = columns[1:] + first
        held.append(
            [[columns[0]] + first]
            + [[x] + [from_group(x, j) for j in range(1, groups)] for x in columns[1:]]
        )

    rows = load(store[:, 0, :], shares[-1])
    parts, last = [], ()
    for c in range(CHUNKS):
        ready = [x for row in held[c] for x in row]
        flip = [from_core(tie(x, *last)) for x in ready]
        both = []
        for k in range(chips):
            at = slice(k * groups, (k + 1) * groups)
            both += ready[at] + flip[at]
        keep, *send = score(ids, blocks, rows, both, groups)
        last = [keep]
        parts.append([keep] + [from_layer(x, r + 1) for r, x in enumerate(send)])
    return finish(place, parts, total)


def solution(mesh):
    groups, ex, layers = (mesh.shape[a] for a in ("groups", "ex", "layer"))
    in_specs = (P(None, "layer", "ex"), P("layer", "ex", None), P(("groups", "ex"), "layer", None))
    out_specs = P(("groups", "ex", "layer"), None)
    return jax.shard_map(
        functools.partial(shards, groups, ex, layers),
        mesh=mesh,
        in_specs=in_specs,
        out_specs=out_specs,
        check_vma=False,
    )
```

```python
import functools

import jax
import jax.numpy as jnp
from jax import lax
from jax.experimental import pallas as pl
from jax.experimental.pallas import tpu as pltpu
from jax.sharding import PartitionSpec as P

F32, BF16 = jnp.float32, jnp.bfloat16
CORES = 2
CHUNKS = 2
MIB = 1 << 20
VMEM = pl.BlockSpec(memory_space=pltpu.VMEM)
SMEM = pl.BlockSpec(memory_space=pltpu.SMEM)
ANY = pl.BlockSpec(memory_space=pl.ANY)


HBM = pl.BlockSpec(memory_space=pltpu.HBM)


def load_kernel(source, after, out, sem):
    copy = pltpu.make_async_copy(source, out, sem)
    copy.start()
    copy.wait()


def load(source, after):
    return pl.pallas_call(
        load_kernel,
        out_shape=pltpu.VMEM(source.shape, BF16),
        in_specs=[HBM, ANY],
        out_specs=VMEM,
        scratch_shapes=[pltpu.SemaphoreType.DMA],
        compiler_params=pltpu.CompilerParams(vmem_limit_bytes=2 * MIB),
    )(pltpu.with_memory_space_constraint(source, pltpu.HBM), after)


def take_kernel(start, source, after, out, sem):
    at = pl.ds(pl.multiple_of(start[0], out.shape[0]), out.shape[0])
    copy = pltpu.make_async_copy(source.at[at, :], out, sem)
    copy.start()
    copy.wait()


def take(start, source, after, rows):
    return pl.pallas_call(
        take_kernel,
        out_shape=pltpu.VMEM((rows, source.shape[1]), BF16),
        in_specs=[SMEM, HBM, ANY],
        out_specs=VMEM,
        scratch_shapes=[pltpu.SemaphoreType.DMA],
        compiler_params=pltpu.CompilerParams(vmem_limit_bytes=2 * MIB),
    )(start, pltpu.with_memory_space_constraint(source, pltpu.HBM), after)


def condition_kernel(count, ids, hess, *rest):
    pieces, (_, out, right) = rest[:count], rest[count:]
    width = hess.shape[1] // count
    for t, piece in enumerate(pieces):
        right[:, pl.ds(pl.multiple_of(ids[t] * width, width), width)] = piece[...]
    out[...] = lax.dot_general(
        hess[...], right[...], (((1,), (1,)), ((), ())), preferred_element_type=F32
    ).astype(BF16)


def condition(ids, hess, pieces, after):
    rows, queries = hess.shape[0], pieces[0].shape[0]
    return pl.pallas_call(
        functools.partial(condition_kernel, len(pieces)),
        out_shape=jax.ShapeDtypeStruct((rows, queries), BF16),
        in_specs=[SMEM] + [VMEM] * (1 + len(pieces)) + [ANY],
        out_specs=VMEM,
        scratch_shapes=[pltpu.VMEM((queries, hess.shape[1]), BF16)],
        compiler_params=pltpu.CompilerParams(vmem_limit_bytes=12 * MIB),
    )(ids, hess, *pieces, after)


def score_kernel(count, ids, blocks, store, *rest):
    pieces, (_, send, keep, right) = rest[:count], rest[count:]
    rows = keep.shape[1]
    depth = pieces[0].shape[0]
    for t, piece in enumerate(pieces):
        right[pl.ds(pl.multiple_of(ids[t] * depth, depth), depth), :] = piece[...]
    for r in [*range(1, blocks.shape[0], 2), *range(0, blocks.shape[0], 2)]:
        at = pl.ds(pl.multiple_of(blocks[r] * rows, rows), rows)
        part = jnp.dot(store[at, :], right[...], preferred_element_type=F32)
        if r % 2:
            send[r // 2] = part.astype(BF16)
        else:
            keep[r // 2] = part


def score(ids, blocks, store, pieces, after):
    depth, width = pieces[0].shape
    layers = blocks.shape[0]
    shape = (layers // 2, store.shape[0] // layers, width)
    return pl.pallas_call(
        functools.partial(score_kernel, len(pieces)),
        out_shape=(jax.ShapeDtypeStruct(shape, BF16), jax.ShapeDtypeStruct(shape, F32)),
        in_specs=[SMEM, SMEM] + [VMEM] * (1 + len(pieces)) + [ANY],
        out_specs=(VMEM, VMEM),
        scratch_shapes=[pltpu.VMEM((len(pieces) * depth, width), BF16)],
        compiler_params=pltpu.CompilerParams(vmem_limit_bytes=12 * MIB),
    )(ids, blocks, store, *pieces, after)


def fold_kernel(keep, got, _, send, left):
    for r in range(keep.shape[0]):
        total = keep[r] + got[r].astype(F32)
        if r % 2:
            send[r // 2] = total.astype(BF16)
        else:
            left[r // 2] = total


def fold(keep, got, after):
    shape = (keep.shape[0] // 2,) + keep.shape[1:]
    return pl.pallas_call(
        fold_kernel,
        out_shape=(jax.ShapeDtypeStruct(shape, BF16), jax.ShapeDtypeStruct(shape, F32)),
        in_specs=[VMEM, VMEM, ANY],
        out_specs=(VMEM, VMEM),
        compiler_params=pltpu.CompilerParams(vmem_limit_bytes=4 * MIB),
    )(keep, got, after)


def finish_kernel(groups, place, *refs):
    *refs, out = refs
    width = refs[0].shape[2]
    pieces = out.shape[1] // width
    for c in range(pieces // groups):
        for j in range(groups):
            keep, got = refs[2 * (c * groups + j) : 2 * (c * groups + j + 1)]
            at = place[j] * (out.shape[1] // groups) + c * width
            out[:, pl.ds(pl.multiple_of(at, width), width)] = keep[0] + got[0].astype(F32)


def finish(place, parts, queries):
    groups = place.shape[0]
    rows = parts[0][0].shape[1]
    return pl.pallas_call(
        functools.partial(finish_kernel, groups),
        out_shape=jax.ShapeDtypeStruct((rows, queries), F32),
        in_specs=[SMEM] + [VMEM] * sum(map(len, parts)),
        out_specs=VMEM,
        compiler_params=pltpu.CompilerParams(vmem_limit_bytes=12 * MIB),
    )(place, *[a for part in parts for a in part])


def shards(groups, ex, layers, queries, hessian, store):
    chips = ex // CORES
    at_group, at_ex, at_layer = (lax.axis_index(a) for a in ("groups", "ex", "layer"))
    chip, core = at_ex // CORES, at_ex % CORES
    ids = jnp.stack(
        [(chip + k) % chips * CORES + (core ^ s) for k in range(chips) for s in range(CORES)]
    ).astype(jnp.int32)
    blocks = jnp.stack([at_layer ^ r for r in range(layers)]).astype(jnp.int32)
    place = jnp.stack([(at_group + j) % groups for j in range(groups)]).astype(jnp.int32)

    def from_chip(x, k):
        perm = [(e, (e - k * CORES) % ex) for e in range(ex)]
        return lax.ppermute(x, "ex", perm)

    def from_core(x):
        return lax.ppermute(x, "ex", [(e, e ^ 1) for e in range(ex)])

    def from_group(x, j):
        return lax.ppermute(x, "groups", [(g, (g - j) % groups) for g in range(groups)])

    def from_layer(x, r):
        return lax.ppermute(x, "layer", [(z, z ^ r) for z in range(layers)])

    def tie(x, *others):
        return lax.optimization_barrier((x, *others))[0]

    total = queries.shape[0]
    span = total // groups
    width = span // CHUNKS

    def part_of_queries(c, after):
        start = (at_group * span + c * width).astype(jnp.int32)[None]
        return take(start, queries[:, 0, :], after, width)

    def gather_chip(x):
        return [from_chip(x, k) for k in range(1, chips)]

    def gather_group(x):
        return [from_group(x, j) for j in range(1, groups)]

    def with_cores(ours, theirs):
        return [x for pair in zip(ours, theirs) for x in pair]

    def flip(xs):
        return [from_core(x) for x in xs]

    def after(token, xs):
        return [tie(x, token) for x in xs]

    scored = functools.partial(score, ids, blocks)
    parts = []

    def advance(token, chain=False):
        for i, part in enumerate(parts):
            if part[0].shape[0] > 1:
                if chain and i and parts[i - 1][0].shape[0] == 1:
                    token = tie(token, parts[i - 1][1])
                send, keep = fold(part[0], part[1], token)
                step = layers // keep.shape[0] // 2
                part[:] = keep, from_layer(send, step)

    def send_parts(made):
        send, keep = made
        advance(keep, chain=True)
        parts.append([keep, from_layer(send, 1)])
        return parts[-2][0] if parts[1:] else keep

    q0 = part_of_queries(0, ids)
    q0_there, q0_core = gather_chip(q0), from_core(q0)
    hess = load(hessian[0], ids)
    q0_there = after(hess, q0_there)
    q0_cores = [q0_core] + flip(q0_there)
    q1 = part_of_queries(1, q0_there[-1])
    q1_there, q1_core = gather_chip(q1), from_core(q1)
    s0 = condition(ids, hess, with_cores([q0] + q0_there, q0_cores), q1)
    s0_there, s0_across, s0_core = gather_chip(s0), gather_group(s0), from_core(s0)
    rows = load(store[:, 0, :], s0)
    q1_there = after(rows, q1_there)
    q1_cores = [q1_core] + flip(q1_there)
    s0_there = after(rows, s0_there)
    s0_diagonal = [gather_group(x) for x in s0_there]
    s0_cores = [s0_core] + flip(s0_there)
    s1 = condition(ids, hess, with_cores([q1] + q1_there, q1_cores), s0_there[-1])
    s1_there, s1_core = gather_chip(s1), from_core(s1)
    s0_across = after(s1, s0_across)
    s0_across_cores = flip(s0_across)
    last = send_parts(scored(rows, with_cores([s0] + s0_there, s0_cores), s1))
    s0_diagonal = [after(last, xs) for xs in s0_diagonal]
    s0_diagonal_cores = [flip(xs) for xs in s0_diagonal]
    s1_across = gather_group(tie(s1, s0_diagonal[-1][-1]))
    s1_there = after(last, s1_there)
    s1_diagonal = [gather_group(x) for x in s1_there]
    s1_cores = [s1_core] + flip(s1_there)
    for j in range(groups - 1):
        ours = [s0_across[j]] + [xs[j] for xs in s0_diagonal]
        theirs = [s0_across_cores[j]] + [xs[j] for xs in s0_diagonal_cores]
        last = send_parts(scored(rows, with_cores(ours, theirs), last))
    last = send_parts(scored(rows, with_cores([s1] + s1_there, s1_cores), last))
    s1_across = after(last, s1_across)
    s1_across_cores = flip(s1_across)
    s1_diagonal = [after(last, xs) for xs in s1_diagonal]
    s1_diagonal_cores = [flip(xs) for xs in s1_diagonal]
    last = tie(last, parts[-2][1])
    for j in range(groups - 1):
        ours = [s1_across[j]] + [xs[j] for xs in s1_diagonal]
        theirs = [s1_across_cores[j]] + [xs[j] for xs in s1_diagonal_cores]
        last = send_parts(scored(rows, with_cores(ours, theirs), last))
    while any(part[0].shape[0] > 1 for part in parts):
        advance(last)
    return finish(place, parts, total)


def solution(mesh):
    groups, ex, layers = (mesh.shape[a] for a in ("groups", "ex", "layer"))
    in_specs = (P(None, "layer", "ex"), P("layer", "ex", None), P(("groups", "ex"), "layer", None))
    out_specs = P(("groups", "ex", "layer"), None)
    return jax.shard_map(
        functools.partial(shards, groups, ex, layers),
        mesh=mesh,
        in_specs=in_specs,
        out_specs=out_specs,
        check_vma=False,
    )
```

```python
import functools

import jax
import jax.numpy as jnp
from jax import lax
from jax.experimental import pallas as pl
from jax.experimental.pallas import tpu as pltpu
from jax.sharding import PartitionSpec as P

F32, BF16 = jnp.float32, jnp.bfloat16
CORES = 2
CHUNKS = 2
MIB = 1 << 20
VMEM = pl.BlockSpec(memory_space=pltpu.VMEM)
SMEM = pl.BlockSpec(memory_space=pltpu.SMEM)
ANY = pl.BlockSpec(memory_space=pl.ANY)


HBM = pl.BlockSpec(memory_space=pltpu.HBM)


def load_kernel(source, after, out, sem):
    copy = pltpu.make_async_copy(source, out, sem)
    copy.start()
    copy.wait()


def load(source, after):
    return pl.pallas_call(
        load_kernel,
        out_shape=pltpu.VMEM(source.shape, BF16),
        in_specs=[HBM, ANY],
        out_specs=VMEM,
        scratch_shapes=[pltpu.SemaphoreType.DMA],
        compiler_params=pltpu.CompilerParams(vmem_limit_bytes=2 * MIB),
    )(pltpu.with_memory_space_constraint(source, pltpu.HBM), after)


def take_kernel(where, facts, source, after, out, sem):
    at = pl.ds(pl.multiple_of(facts[where], out.shape[0]), out.shape[0])
    copy = pltpu.make_async_copy(source.at[at, :], out, sem)
    copy.start()
    copy.wait()


def take(where, facts, source, after, rows):
    return pl.pallas_call(
        functools.partial(take_kernel, where),
        out_shape=pltpu.VMEM((rows, source.shape[1]), BF16),
        in_specs=[SMEM, HBM, ANY],
        out_specs=VMEM,
        scratch_shapes=[pltpu.SemaphoreType.DMA],
        compiler_params=pltpu.CompilerParams(vmem_limit_bytes=2 * MIB),
    )(facts, pltpu.with_memory_space_constraint(source, pltpu.HBM), after)


def condition_kernel(count, facts, hess, *rest):
    pieces, (_, out, right) = rest[:count], rest[count:]
    width = hess.shape[1] // count
    for t, piece in enumerate(pieces):
        right[:, pl.ds(pl.multiple_of(facts[t] * width, width), width)] = piece[...]
    out[...] = lax.dot_general(
        hess[...], right[...], (((1,), (1,)), ((), ())), preferred_element_type=F32
    ).astype(BF16)


def condition(facts, hess, pieces, after):
    rows, queries = hess.shape[0], pieces[0].shape[0]
    return pl.pallas_call(
        functools.partial(condition_kernel, len(pieces)),
        out_shape=jax.ShapeDtypeStruct((rows, queries), BF16),
        in_specs=[SMEM] + [VMEM] * (1 + len(pieces)) + [ANY],
        out_specs=VMEM,
        scratch_shapes=[pltpu.VMEM((queries, hess.shape[1]), BF16)],
        compiler_params=pltpu.CompilerParams(vmem_limit_bytes=12 * MIB),
    )(facts, hess, *pieces, after)


def score_kernel(count, layers, facts, store, *rest):
    pieces, (_, send, keep, right) = rest[:count], rest[count:]
    rows = keep.shape[1]
    depth = pieces[0].shape[0]
    for t, piece in enumerate(pieces):
        right[pl.ds(pl.multiple_of(facts[t] * depth, depth), depth), :] = piece[...]
    for r in [*range(1, layers, 2), *range(0, layers, 2)]:
        at = pl.ds(pl.multiple_of(facts[count + r] * rows, rows), rows)
        part = jnp.dot(store[at, :], right[...], preferred_element_type=F32)
        if r % 2:
            send[r // 2] = part.astype(BF16)
        else:
            keep[r // 2] = part


def score(layers, facts, store, pieces, after):
    depth, width = pieces[0].shape
    shape = (layers // 2, store.shape[0] // layers, width)
    return pl.pallas_call(
        functools.partial(score_kernel, len(pieces), layers),
        out_shape=(jax.ShapeDtypeStruct(shape, BF16), jax.ShapeDtypeStruct(shape, F32)),
        in_specs=[SMEM] + [VMEM] * (1 + len(pieces)) + [ANY],
        out_specs=(VMEM, VMEM),
        scratch_shapes=[pltpu.VMEM((len(pieces) * depth, width), BF16)],
        compiler_params=pltpu.CompilerParams(vmem_limit_bytes=12 * MIB),
    )(facts, store, *pieces, after)


def fold_kernel(keep, got, _, send, left):
    for r in range(keep.shape[0]):
        total = keep[r] + got[r].astype(F32)
        if r % 2:
            send[r // 2] = total.astype(BF16)
        else:
            left[r // 2] = total


def fold(keep, got, after):
    shape = (keep.shape[0] // 2,) + keep.shape[1:]
    return pl.pallas_call(
        fold_kernel,
        out_shape=(jax.ShapeDtypeStruct(shape, BF16), jax.ShapeDtypeStruct(shape, F32)),
        in_specs=[VMEM, VMEM, ANY],
        out_specs=(VMEM, VMEM),
        compiler_params=pltpu.CompilerParams(vmem_limit_bytes=4 * MIB),
    )(keep, got, after)


def finish_kernel(groups, base, facts, *refs):
    *refs, out = refs
    width = refs[0].shape[2]
    pieces = out.shape[1] // width
    for c in range(pieces // groups):
        for j in range(groups):
            keep, got = refs[2 * (c * groups + j) : 2 * (c * groups + j + 1)]
            at = facts[base + j] * (out.shape[1] // groups) + c * width
            out[:, pl.ds(pl.multiple_of(at, width), width)] = keep[0] + got[0].astype(F32)


def finish(groups, base, facts, parts, queries):
    rows = parts[0][0].shape[1]
    return pl.pallas_call(
        functools.partial(finish_kernel, groups, base),
        out_shape=jax.ShapeDtypeStruct((rows, queries), F32),
        in_specs=[SMEM] + [VMEM] * sum(map(len, parts)),
        out_specs=VMEM,
        compiler_params=pltpu.CompilerParams(vmem_limit_bytes=12 * MIB),
    )(facts, *[a for part in parts for a in part])


def shards(groups, ex, layers, queries, hessian, store):
    chips = ex // CORES
    at_group, at_ex, at_layer = (lax.axis_index(a) for a in ("groups", "ex", "layer"))
    chip, core = at_ex // CORES, at_ex % CORES
    total = queries.shape[0]
    span = total // groups
    width = span // CHUNKS
    facts = [(chip + k) % chips * CORES + (core ^ s) for k in range(chips) for s in range(CORES)]
    facts += [at_layer ^ r for r in range(layers)]
    facts += [(at_group + j) % groups for j in range(groups)]
    facts += [at_group * span + c * width for c in range(CHUNKS)]
    facts = jnp.stack(facts).astype(jnp.int32)

    def from_chip(x, k):
        perm = [(e, (e - k * CORES) % ex) for e in range(ex)]
        return lax.ppermute(x, "ex", perm)

    def from_core(x):
        return lax.ppermute(x, "ex", [(e, e ^ 1) for e in range(ex)])

    def from_group(x, j):
        return lax.ppermute(x, "groups", [(g, (g - j) % groups) for g in range(groups)])

    def from_layer(x, r):
        return lax.ppermute(x, "layer", [(z, z ^ r) for z in range(layers)])

    def tie(x, *others):
        return lax.optimization_barrier((x, *others))[0]

    def part_of_queries(c, after):
        return take(ex + layers + groups + c, facts, queries[:, 0, :], after, width)

    def gather_chip(x):
        return [from_chip(x, k) for k in range(1, chips)]

    def gather_group(x):
        return [from_group(x, j) for j in range(1, groups)]

    def with_cores(ours, theirs):
        return [x for pair in zip(ours, theirs) for x in pair]

    def flip(xs):
        return [from_core(x) for x in xs]

    def after(token, xs):
        return [tie(x, token) for x in xs]

    scored = functools.partial(score, layers, facts)
    parts = []

    def advance(token, chain=False):
        for i, part in enumerate(parts):
            if part[0].shape[0] > 1:
                if chain and i and parts[i - 1][0].shape[0] == 1:
                    token = tie(token, parts[i - 1][1])
                send, keep = fold(part[0], part[1], token)
                step = layers // keep.shape[0] // 2
                part[:] = keep, from_layer(send, step)

    def send_parts(made):
        send, keep = made
        advance(keep, chain=True)
        parts.append([keep, from_layer(send, 1)])
        return parts[-2][0] if parts[1:] else keep

    q0 = part_of_queries(0, facts)
    q0_there, q0_core = gather_chip(q0), from_core(q0)
    hess = load(hessian[0], facts)
    q0_there = after(hess, q0_there)
    q0_cores = [q0_core] + flip(q0_there)
    q1 = part_of_queries(1, q0_there[-1])
    q1_there, q1_core = gather_chip(q1), from_core(q1)
    s0 = condition(facts, hess, with_cores([q0] + q0_there, q0_cores), q1)
    s0_there, s0_across, s0_core = gather_chip(s0), gather_group(s0), from_core(s0)
    rows = load(store[:, 0, :], s0)
    q1_there = after(rows, q1_there)
    q1_cores = [q1_core] + flip(q1_there)
    s0_there = after(rows, s0_there)
    s0_diagonal = [gather_group(x) for x in s0_there]
    s0_cores = [s0_core] + flip(s0_there)
    s1 = condition(facts, hess, with_cores([q1] + q1_there, q1_cores), s0_there[-1])
    s1_there, s1_core = gather_chip(s1), from_core(s1)
    s0_across = after(s1, s0_across)
    s0_across_cores = flip(s0_across)
    last = send_parts(scored(rows, with_cores([s0] + s0_there, s0_cores), s1))
    s0_diagonal = [after(last, xs) for xs in s0_diagonal]
    s0_diagonal_cores = [flip(xs) for xs in s0_diagonal]
    s1_across = gather_group(tie(s1, s0_diagonal[-1][-1]))
    s1_there = after(last, s1_there)
    s1_diagonal = [gather_group(x) for x in s1_there]
    s1_cores = [s1_core] + flip(s1_there)
    for j in range(groups - 1):
        ours = [s0_across[j]] + [xs[j] for xs in s0_diagonal]
        theirs = [s0_across_cores[j]] + [xs[j] for xs in s0_diagonal_cores]
        last = send_parts(scored(rows, with_cores(ours, theirs), last))
    last = send_parts(scored(rows, with_cores([s1] + s1_there, s1_cores), last))
    s1_across = after(last, s1_across)
    s1_across_cores = flip(s1_across)
    s1_diagonal = [after(last, xs) for xs in s1_diagonal]
    s1_diagonal_cores = [flip(xs) for xs in s1_diagonal]
    last = tie(last, parts[-2][1])
    for j in range(groups - 1):
        ours = [s1_across[j]] + [xs[j] for xs in s1_diagonal]
        theirs = [s1_across_cores[j]] + [xs[j] for xs in s1_diagonal_cores]
        last = send_parts(scored(rows, with_cores(ours, theirs), last))
    while any(part[0].shape[0] > 1 for part in parts):
        advance(last)
    return finish(groups, ex + layers, facts, parts, total)


def solution(mesh):
    groups, ex, layers = (mesh.shape[a] for a in ("groups", "ex", "layer"))
    in_specs = (P(None, "layer", "ex"), P("layer", "ex", None), P(("groups", "ex"), "layer", None))
    out_specs = P(("groups", "ex", "layer"), None)
    return jax.shard_map(
        functools.partial(shards, groups, ex, layers),
        mesh=mesh,
        in_specs=in_specs,
        out_specs=out_specs,
        check_vma=False,
    )
```

```python
import functools

import jax
import jax.numpy as jnp
from jax import lax
from jax.experimental import pallas as pl
from jax.experimental.pallas import tpu as pltpu
from jax.sharding import PartitionSpec as P

F32, BF16 = jnp.float32, jnp.bfloat16
CORES = 2
COSTS = {
    "load_hessian": 1_000_000_000_000,
    "condition_here": 1_000_000_000_000,
    "own_here": 3_000_000_000,
    "other_here": 1_000_000_000_000,
    "sum0": 1_000_000_000_000,
    "sum1": 3_000_000_000,
    "sum2": 3_000_000_000,
}
MIB = 1 << 20
VMEM = pl.BlockSpec(memory_space=pltpu.VMEM)
SMEM = pl.BlockSpec(memory_space=pltpu.SMEM)
ANY = pl.BlockSpec(memory_space=pl.ANY)


HBM = pl.BlockSpec(memory_space=pltpu.HBM)


def positions(groups, ex, layers):
    chips = ex // CORES
    chip, core = lax.axis_index("ex") // CORES, lax.axis_index("ex") % CORES
    ids = [lax.rem(chip + k, chips) * CORES + (core ^ s) for k in range(chips) for s in range(CORES)]
    blocks = [lax.axis_index("layer") ^ r for r in range(layers)]
    place = [lax.rem(lax.axis_index("groups") + j, groups) for j in range(groups)]
    return ids, blocks, place


def take_kernel(source, out, sem):
    rows = out.shape[0]
    at = pl.ds(pl.multiple_of(lax.axis_index("groups") * rows, rows), rows)
    copy = pltpu.make_async_copy(source.at[at, :], out, sem)
    copy.start()
    copy.wait()


def take(source, rows):
    return pl.pallas_call(
        take_kernel,
        out_shape=pltpu.VMEM((rows, source.shape[1]), BF16),
        in_specs=[HBM],
        out_specs=VMEM,
        scratch_shapes=[pltpu.SemaphoreType.DMA],
        compiler_params=pltpu.CompilerParams(vmem_limit_bytes=2 * MIB),
        name="take",
    )(pltpu.with_memory_space_constraint(source, pltpu.HBM))


def cost(name):
    return pl.CostEstimate(flops=COSTS.get(name, 0), bytes_accessed=1, transcendentals=0)


def load_kernel(source, after, out, sem):
    copy = pltpu.make_async_copy(source, out, sem)
    copy.start()
    copy.wait()


def load(name, source, after):
    return pl.pallas_call(
        load_kernel,
        out_shape=pltpu.VMEM(source.shape, BF16),
        in_specs=[HBM, ANY],
        out_specs=VMEM,
        scratch_shapes=[pltpu.SemaphoreType.DMA],
        compiler_params=pltpu.CompilerParams(vmem_limit_bytes=2 * MIB),
        cost_estimate=cost(name),
        name=name,
    )(pltpu.with_memory_space_constraint(source, pltpu.HBM), after)


def runs_of(ids, at_ids, depth):
    if len(at_ids) == len(ids):
        return [ids[t] * depth for t in at_ids], [(0, 0, len(ids) * depth)]
    span = CORES * depth
    at = [(i // CORES * CORES + ids[t] % CORES) * depth for i, t in enumerate(at_ids)]
    return at, [(i * span, ids[t] // CORES * span, span) for i, t in enumerate(at_ids[::CORES])]


def condition_kernel(sizes, at_ids, more, hess, *rest):
    ids, _, _ = positions(*sizes)
    pieces, rest = rest[: len(at_ids)], rest[len(at_ids) + 1 :]
    before, (out, right) = rest[0] if more else None, rest[more:]
    depth = pieces[0].shape[1]
    places, runs = runs_of(ids, at_ids, depth)
    for at, piece in zip(places, pieces):
        right[:, pl.ds(pl.multiple_of(at, depth), depth)] = piece[...]
    total = before[...] if more else None
    for low, column, span in runs:
        term = lax.dot_general(
            hess[:, pl.ds(pl.multiple_of(column, depth), span)],
            right[:, low : low + span],
            (((1,), (1,)), ((), ())),
            preferred_element_type=F32,
        )
        total = term if total is None else total + term
    out[...] = total.astype(out.dtype)


def condition(name, sizes, hess, at_ids, pieces, after, before=None):
    queries, depth = pieces[0].shape
    more = [] if before is None else [before]
    return pl.pallas_call(
        functools.partial(condition_kernel, sizes, at_ids, len(more)),
        out_shape=jax.ShapeDtypeStruct((hess.shape[0], queries), BF16 if more else F32),
        in_specs=[VMEM] * (1 + len(pieces)) + [ANY] + [VMEM] * len(more),
        out_specs=VMEM,
        scratch_shapes=[pltpu.VMEM((queries, len(pieces) * depth), BF16)],
        compiler_params=pltpu.CompilerParams(vmem_limit_bytes=12 * MIB),
        cost_estimate=cost(name),
        name=name,
    )(hess, *pieces, after, *more)


def score_kernel(sizes, at_ids, offsets, more, store, *rest):
    ids, blocks, _ = positions(*sizes)
    layers = len(blocks)
    pieces, rest = rest[: len(offsets)], rest[len(offsets) + 1 :]
    before, (*outs, right) = rest[0] if more else None, rest[more:]
    depth = right.shape[0] // len(at_ids)
    rows = store.shape[0] // layers
    places, runs = runs_of(ids, at_ids, depth)
    for (i, offset), piece in zip(offsets, pieces):
        count = piece.shape[0]
        right[pl.ds(pl.multiple_of(places[i] + offset, count), count), :] = piece[...]
    for r in [*range(1, layers, 2), *range(0, layers, 2)]:
        at = pl.ds(pl.multiple_of(blocks[r] * rows, rows), rows)
        part = before[r] if more else None
        for low, column, span in runs:
            columns = pl.ds(pl.multiple_of(column, depth), span)
            term = jnp.dot(store[at, columns], right[low : low + span, :], preferred_element_type=F32)
            part = term if part is None else part + term
        if len(outs) == 1:
            outs[0][r] = part
            continue
        cut = 2 * part.shape[1] // len(outs)
        for i in range(len(outs) // 2):
            out = outs[2 * i + 1 - r % 2]
            out[r // 2] = part[:, i * cut : (i + 1) * cut].astype(out.dtype)


def score(name, sizes, store, at_ids, pieces, after, before=None, cuts=0):
    width = pieces[0][0].shape[1]
    layers = sizes[2]
    rows = store.shape[0] // layers
    shapes = [((layers, rows, width), F32)]
    if cuts:
        shapes = [((layers // 2, rows, width // cuts), t) for t in (BF16, F32)] * cuts
    more = [] if before is None else [before]
    offsets, flat = [], []
    for i, xs in enumerate(pieces):
        low = 0
        for x in xs:
            offsets.append((i, low))
            flat.append(x)
            low += x.shape[0]
    return pl.pallas_call(
        functools.partial(score_kernel, sizes, at_ids, tuple(offsets), len(more)),
        out_shape=[jax.ShapeDtypeStruct(*shape) for shape in shapes],
        in_specs=[VMEM] * (1 + len(flat)) + [ANY] + [VMEM] * len(more),
        out_specs=[VMEM] * len(shapes),
        scratch_shapes=[pltpu.VMEM((len(at_ids) * low, width), BF16)],
        compiler_params=pltpu.CompilerParams(vmem_limit_bytes=12 * MIB),
        cost_estimate=cost(name),
        name=name,
    )(store, *flat, after, *more)


def fold_kernel(keep, got, _, send, left):
    for r in range(keep.shape[0]):
        total = keep[r] + got[r].astype(F32)
        if r % 2:
            send[r // 2] = total.astype(BF16)
        else:
            left[r // 2] = total


def fold(name, keep, got, after):
    shape = (keep.shape[0] // 2,) + keep.shape[1:]
    return pl.pallas_call(
        fold_kernel,
        out_shape=(jax.ShapeDtypeStruct(shape, BF16), jax.ShapeDtypeStruct(shape, F32)),
        in_specs=[VMEM, VMEM, ANY],
        out_specs=(VMEM, VMEM),
        compiler_params=pltpu.CompilerParams(vmem_limit_bytes=4 * MIB),
        cost_estimate=cost(name),
        name=name,
    )(keep, got, after)


def finish_kernel(sizes, places, *refs):
    _, _, place = positions(*sizes)
    *refs, out = refs
    span = out.shape[1] // len(place)
    for i, (j, column) in enumerate(places):
        keep, got = refs[2 * i : 2 * i + 2]
        at = pl.multiple_of(place[j] * span + column, keep.shape[2])
        out[:, pl.ds(at, keep.shape[2])] = keep[0] + got[0].astype(F32)


def finish(sizes, parts, queries):
    rows = parts[0][1][0].shape[1]
    return pl.pallas_call(
        functools.partial(finish_kernel, sizes, tuple(place for place, _ in parts)),
        out_shape=jax.ShapeDtypeStruct((rows, queries), F32),
        in_specs=[VMEM] * (2 * len(parts)),
        out_specs=VMEM,
        compiler_params=pltpu.CompilerParams(vmem_limit_bytes=12 * MIB),
        name="finish",
    )(*[a for _, part in parts for a in part])


def shards(groups, ex, layers, queries, hessian, store):
    chips = ex // CORES
    sizes = groups, ex, layers
    total = queries.shape[0]

    def permute(x, axis, perm, what):
        with jax.named_scope(what):
            return lax.ppermute(x, axis, perm)

    def from_chip(x, k, what):
        perm = [(e, (e - k * CORES) % ex) for e in range(ex)]
        return permute(x, "ex", perm, what + "_from_chip")

    def from_core(x, what):
        return permute(x, "ex", [(e, e ^ 1) for e in range(ex)], what + "_from_core")

    def from_group(x, j, what):
        perm = [(g, (g - j) % groups) for g in range(groups)]
        return permute(x, "groups", perm, what + "_from_group")

    def from_layer(x, r, what):
        return permute(x, "layer", [(z, z ^ r) for z in range(layers)], f"{what}_from_layer_{r}")

    def tie(x, *others):
        return lax.optimization_barrier((x, *others))[0]

    def gather_chip(x, what):
        return [from_chip(x, k, what) for k in range(1, chips)]

    def gather_group(x, what):
        return [from_group(x, j, what) for j in range(1, groups)]

    def with_cores(ours, theirs):
        return [x for pair in zip(ours, theirs) for x in pair]

    def flip(xs, what):
        return [from_core(x, what) for x in xs]

    def after(token, xs):
        return [tie(x, token) for x in xs]

    everywhere = tuple(range(ex))
    here, there = everywhere[:CORES], everywhere[CORES:]

    def step(name, keep, got, token):
        if keep.shape[0] == 1:
            return keep, got
        send, keep = fold(name, keep, got, token)
        return keep, from_layer(send, layers // keep.shape[0] // 2, name)

    hess = load("load_hessian", hessian[0], queries)
    rows = pltpu.with_memory_space_constraint(store[:, 0, :], pltpu.VMEM)
    mine = take(queries[:, 0, :], total // groups)
    mine_there, mine_core = gather_chip(mine, "queries"), from_core(mine, "queries")
    part = condition("condition_here", sizes, hess, here, [mine, mine_core], queries)
    mine_there = after(part, mine_there)
    pieces = with_cores(mine_there, flip(mine_there, "queries_there"))
    share = condition("condition_there", sizes, hess, there, pieces, part, part)
    by_chip, by_group = gather_chip(share, "share"), gather_group(share, "share")
    share_core = from_core(share, "share")
    part = score("own_here", sizes, rows, here, [[share], [share_core]], share)[0]
    by_chip, by_group = after(part, by_chip), after(part, by_group)
    half = share.shape[0] // 2
    by_chip_cores, by_group_cores = flip(by_chip, "by_chip"), flip(by_group, "by_group")
    upper = [[from_group(x[:half], j, "upper") for x in by_chip] for j in range(1, groups)]
    lower = [[from_chip(x[half:], k, "lower") for k in range(1, chips)] for x in by_group]
    pieces = [[x] for x in with_cores(by_chip, by_chip_cores)]
    send, keep = score("own_there", sizes, rows, there, pieces, part, part, 1)
    parts = [((0, 0), (keep, from_layer(send, 1, "own")))]
    token = keep
    for j in range(groups - 1):
        pieces = [[by_group[j]], [by_group_cores[j]]]
        part = score("other_here", sizes, rows, here, pieces, token)[0]
        halves = [after(part, pair) for pair in zip(upper[j], lower[j])]
        flips = [flip(pair, "diagonal") for pair in halves]
        pieces = [x for pair in zip(halves, flips) for x in pair]
        made = score("other_there", sizes, rows, there, pieces, part, part, 2)
        cut = made[0].shape[2]
        for c in range(2):
            send, token = made[2 * c : 2 * c + 2]
            parts.append(((j + 1, c * cut), (token, from_layer(send, 1, f"other{c}"))))
    while any(part[0].shape[0] > 1 for _, part in parts):
        parts = [(at, step(f"sum{i}", *part, token)) for i, (at, part) in enumerate(parts)]
    return finish(sizes, parts, total)


def solution(mesh):
    groups, ex, layers = (mesh.shape[a] for a in ("groups", "ex", "layer"))
    in_specs = (P(None, "layer", "ex"), P("layer", "ex", None), P(("groups", "ex"), "layer", None))
    out_specs = P(("groups", "ex", "layer"), None)
    return jax.shard_map(
        functools.partial(shards, groups, ex, layers),
        mesh=mesh,
        in_specs=in_specs,
        out_specs=out_specs,
        check_vma=False,
    )
```

```python
import functools

import jax
import jax.numpy as jnp
from jax import lax
from jax.experimental import pallas as pl
from jax.experimental.pallas import tpu as pltpu
from jax.sharding import PartitionSpec as P

F32, BF16 = jnp.float32, jnp.bfloat16
CORES = 2
COSTS = {
    "load_hessian": 1_000_000_000_000,
    "condition_here": 1_000_000_000_000,
    "own_here": 1_000_000_000_000,
    "other_here": 1_000_000_000_000,
}
MIB = 1 << 20
VMEM = pl.BlockSpec(memory_space=pltpu.VMEM)
SMEM = pl.BlockSpec(memory_space=pltpu.SMEM)
ANY = pl.BlockSpec(memory_space=pl.ANY)


HBM = pl.BlockSpec(memory_space=pltpu.HBM)


def positions(groups, ex, layers):
    chips = ex // CORES
    chip, core = lax.axis_index("ex") // CORES, lax.axis_index("ex") % CORES
    ids = [lax.rem(chip + k, chips) * CORES + (core ^ s) for k in range(chips) for s in range(CORES)]
    blocks = [lax.axis_index("layer") ^ r for r in range(layers)]
    place = [lax.rem(lax.axis_index("groups") + j, groups) for j in range(groups)]
    return ids, blocks, place


def take_kernel(source, out, sems):
    parts = sems.shape[0]
    rows = out.shape[0] // parts
    first = lax.axis_index("groups") * out.shape[0]
    copies = []
    for i in range(parts):
        at = pl.ds(pl.multiple_of(first + i * rows, rows), rows)
        copies.append(
            pltpu.make_async_copy(source.at[at, :], out.at[i * rows : (i + 1) * rows, :], sems.at[i])
        )
    for copy in copies:
        copy.start()
    for copy in copies:
        copy.wait()


def take(source, rows):
    return pl.pallas_call(
        take_kernel,
        out_shape=pltpu.VMEM((rows, source.shape[1]), BF16),
        in_specs=[HBM],
        out_specs=VMEM,
        scratch_shapes=[pltpu.SemaphoreType.DMA((8,))],
        compiler_params=pltpu.CompilerParams(vmem_limit_bytes=2 * MIB),
        name="take",
    )(pltpu.with_memory_space_constraint(source, pltpu.HBM))


def cost(name):
    return pl.CostEstimate(flops=COSTS.get(name, 0), bytes_accessed=1, transcendentals=0)


def load_kernel(source, after, out, sem):
    copy = pltpu.make_async_copy(source, out, sem)
    copy.start()
    copy.wait()


def load(name, source, after):
    return pl.pallas_call(
        load_kernel,
        out_shape=pltpu.VMEM(source.shape, BF16),
        in_specs=[HBM, ANY],
        out_specs=VMEM,
        scratch_shapes=[pltpu.SemaphoreType.DMA],
        compiler_params=pltpu.CompilerParams(vmem_limit_bytes=2 * MIB),
        cost_estimate=cost(name),
        name=name,
    )(pltpu.with_memory_space_constraint(source, pltpu.HBM), after)


def condition_kernel(sizes, at_ids, more, hess, *rest):
    ids, _, _ = positions(*sizes)
    pieces, rest = rest[: len(at_ids)], rest[len(at_ids) + 1 :]
    total, outs = rest[0][...] if more else None, rest[more:]
    depth = pieces[0].shape[1]
    for t, piece in zip(at_ids, pieces):
        columns = pl.ds(pl.multiple_of(ids[t] * depth, depth), depth)
        term = lax.dot_general(
            hess[:, columns], piece[...], (((1,), (1,)), ((), ())), preferred_element_type=F32
        )
        total = term if total is None else total + term
    outs[0][...] = total.astype(outs[0].dtype)
    for i, out in enumerate(outs[1:]):
        out[...] = outs[0][i * out.shape[0] : (i + 1) * out.shape[0], :]


def condition(name, sizes, hess, at_ids, pieces, after, before=None):
    queries = pieces[0].shape[0]
    height = hess.shape[0]
    shapes = [((height, queries), F32)]
    if before is not None:
        shapes = [((height, queries), BF16)] + [((height // 2, queries), BF16)] * 2
    more = [] if before is None else [before]
    return pl.pallas_call(
        functools.partial(condition_kernel, sizes, at_ids, len(more)),
        out_shape=[pltpu.VMEM(*shape) for shape in shapes],
        in_specs=[VMEM] * (1 + len(pieces)) + [ANY] + [VMEM] * len(more),
        out_specs=[VMEM] * len(shapes),
        compiler_params=pltpu.CompilerParams(vmem_limit_bytes=12 * MIB),
        cost_estimate=cost(name),
        name=name,
    )(hess, *pieces, after, *more)


def score_kernel(sizes, at_ids, more, store, *rest):
    ids, blocks, _ = positions(*sizes)
    layers = len(blocks)
    pieces, rest = rest[: len(at_ids)], rest[len(at_ids) + 1 :]
    before, outs = rest[0] if more else None, rest[more:]
    depth = store.shape[1] // len(ids)
    rows = store.shape[0] // layers
    for r in [*range(1, layers, 2), *range(0, layers, 2)]:
        at = pl.ds(pl.multiple_of(blocks[r] * rows, rows), rows)
        part = before[r] if more else None
        for (t, half), piece in zip(at_ids, pieces):
            height = piece.shape[0]
            column = ids[t] * depth + half * height
            columns = pl.ds(pl.multiple_of(column, height), height)
            term = jnp.dot(store[at, columns], piece[...], preferred_element_type=F32)
            part = term if part is None else part + term
        if len(outs) == 1:
            outs[0][r] = part
            continue
        cut = 2 * part.shape[1] // len(outs)
        for i in range(len(outs) // 2):
            out = outs[2 * i + 1 - r % 2]
            out[r // 2] = part[:, i * cut : (i + 1) * cut].astype(out.dtype)


def score(name, sizes, store, pieces, after, before=None, cuts=0):
    flat = list(pieces.values())
    width = flat[0].shape[1]
    layers = sizes[2]
    rows = store.shape[0] // layers
    shapes = [((layers, rows, width), F32)]
    if cuts:
        shapes = [((layers // 2, rows, width // cuts), t) for t in (BF16, F32)] * cuts
    more = [] if before is None else [before]
    return pl.pallas_call(
        functools.partial(score_kernel, sizes, tuple(pieces), len(more)),
        out_shape=[pltpu.VMEM(*shape) for shape in shapes],
        in_specs=[VMEM] * (1 + len(flat)) + [ANY] + [VMEM] * len(more),
        out_specs=[VMEM] * len(shapes),
        compiler_params=pltpu.CompilerParams(vmem_limit_bytes=12 * MIB),
        cost_estimate=cost(name),
        name=name,
    )(store, *flat, after, *more)


def fold_kernel(keep, got, _, send, left):
    for r in range(keep.shape[0]):
        total = keep[r] + got[r].astype(F32)
        if r % 2:
            send[r // 2] = total.astype(BF16)
        else:
            left[r // 2] = total


def fold(name, keep, got, after):
    shape = (keep.shape[0] // 2,) + keep.shape[1:]
    return pl.pallas_call(
        fold_kernel,
        out_shape=(pltpu.VMEM(shape, BF16), pltpu.VMEM(shape, F32)),
        in_specs=[VMEM, VMEM, ANY],
        out_specs=(VMEM, VMEM),
        compiler_params=pltpu.CompilerParams(vmem_limit_bytes=4 * MIB),
        cost_estimate=cost(name),
        name=name,
    )(keep, got, after)


def finish_kernel(sizes, places, *refs):
    _, _, place = positions(*sizes)
    *refs, out = refs
    span = out.shape[1] // len(place)
    for i, (j, column) in enumerate(places):
        keep, got = refs[2 * i : 2 * i + 2]
        at = pl.multiple_of(place[j] * span + column, keep.shape[2])
        out[:, pl.ds(at, keep.shape[2])] = keep[0] + got[0].astype(F32)


def finish(sizes, parts, queries):
    rows = parts[0][1][0].shape[1]
    return pl.pallas_call(
        functools.partial(finish_kernel, sizes, tuple(place for place, _ in parts)),
        out_shape=jax.ShapeDtypeStruct((rows, queries), F32),
        in_specs=[VMEM] * (2 * len(parts)),
        out_specs=VMEM,
        compiler_params=pltpu.CompilerParams(vmem_limit_bytes=12 * MIB),
        name="finish",
    )(*[a for _, part in parts for a in part])


def shards(groups, ex, layers, queries, hessian, store):
    chips = ex // CORES
    sizes = groups, ex, layers
    total = queries.shape[0]

    def permute(x, axis, perm, what):
        with jax.named_scope(what):
            return lax.ppermute(x, axis, perm)

    def from_chip(x, k, what):
        perm = [(e, (e - k * CORES) % ex) for e in range(ex)]
        return permute(x, "ex", perm, what + "_from_chip")

    def from_core(x, what):
        return permute(x, "ex", [(e, e ^ 1) for e in range(ex)], what + "_from_core")

    def from_group(x, j, what):
        perm = [(g, (g - j) % groups) for g in range(groups)]
        return permute(x, "groups", perm, what + "_from_group")

    def from_layer(x, r, what):
        return permute(x, "layer", [(z, z ^ r) for z in range(layers)], f"{what}_from_layer_{r}")

    def tie(x, *others):
        return lax.optimization_barrier((x, *others))[0]

    def gather_chip(x, what):
        return [from_chip(x, k, what) for k in range(1, chips)]

    def gather_group(x, what):
        return [from_group(x, j, what) for j in range(1, groups)]

    def with_cores(ours, theirs):
        return [x for pair in zip(ours, theirs) for x in pair]

    def flip(xs, what):
        return [from_core(x, what) for x in xs]

    def after(token, xs):
        return [tie(x, token) for x in xs]

    here, there = range(CORES), range(CORES, ex)

    def step(name, keep, got, token):
        if keep.shape[0] == 1:
            return keep, got
        send, keep = fold(name, keep, got, token)
        return keep, from_layer(send, layers // keep.shape[0] // 2, name)

    mine = take(queries[:, 0, :], total // groups)
    hess = load("load_hessian", hessian[0], mine)
    rows = pltpu.with_memory_space_constraint(store[:, 0, :], pltpu.VMEM)
    mine_there, mine_core = gather_chip(mine, "queries"), from_core(mine, "queries")
    part = condition("condition_here", sizes, hess, here, [mine, mine_core], hess)[0]
    mine_there = after(part, mine_there)
    pieces = with_cores(mine_there, flip(mine_there, "queries_there"))
    share, upper, lower = condition("condition_there", sizes, hess, there, pieces, part, part)
    share_core = from_core(share, "share")
    by_chip = [gather_chip(upper, "upper"), gather_chip(lower, "lower")]
    by_group = [gather_group(tie(upper, share_core), "upper"), gather_group(tie(lower, share_core), "lower")]
    part = score("own_here", sizes, rows, {(0, 0): share, (1, 0): share_core}, share)[0]
    by_chip[0], by_group[1] = after(part, by_chip[0]), after(part, by_group[1])
    diagonal = [
        [[from_group(x, j, "chips_upper") for x in by_chip[0]] for j in range(1, groups)],
        [gather_chip(x, "groups_lower") for x in by_group[1]],
    ]

    def spread(xs, half, what):
        return {(t, half): x for t, x in zip(there, with_cores(xs, flip(xs, what)))}

    by_chip[1] = after(part, by_chip[1])
    pieces = spread(by_chip[0], 0, "chips_upper") | spread(by_chip[1], 1, "chips_lower")
    send, keep = score("own_there", sizes, rows, pieces, part, part, 1)
    parts = [((0, 0), (keep, from_layer(send, 1, "own")))]
    token = keep
    by_group[0] = after(part, by_group[0])
    for j in range(groups - 1):
        pieces = {}
        for half in range(2):
            x = by_group[half][j]
            pieces |= {(0, half): x, (1, half): from_core(x, "groups")}
        part = score("other_here", sizes, rows, pieces, token)[0]
        pieces = {}
        for half in range(2):
            pieces |= spread(after(part, diagonal[half][j]), half, "diagonal")
        made = score("other_there", sizes, rows, pieces, part, part, 2)
        cut = made[0].shape[2]
        for c in range(2):
            send, token = made[2 * c : 2 * c + 2]
            parts.append(((j + 1, c * cut), (token, from_layer(send, 1, f"other{c}"))))
    while any(part[0].shape[0] > 1 for _, part in parts):
        parts = [(at, step(f"sum{i}", *part, token)) for i, (at, part) in enumerate(parts)]
    return finish(sizes, parts, total)


def solution(mesh):
    groups, ex, layers = (mesh.shape[a] for a in ("groups", "ex", "layer"))
    in_specs = (P(None, "layer", "ex"), P("layer", "ex", None), P(("groups", "ex"), "layer", None))
    out_specs = P(("groups", "ex", "layer"), None)
    return jax.shard_map(
        functools.partial(shards, groups, ex, layers),
        mesh=mesh,
        in_specs=in_specs,
        out_specs=out_specs,
        check_vma=False,
    )
```

```python
import functools

import jax
import jax.numpy as jnp
from jax import lax
from jax.experimental import pallas as pl
from jax.experimental.pallas import tpu as pltpu
from jax.sharding import PartitionSpec as P

F32, BF16 = jnp.float32, jnp.bfloat16
CORES = 2
COSTS = {
    "load_hessian": 1_000_000_000_000,
    "condition_here": 1_000_000_000_000,
    "own_here": 3_000_000_000,
    "other_here": 1_000_000_000_000,
    "sum0": 1_000_000_000_000,
    "sum1": 3_000_000_000,
    "sum2": 3_000_000_000,
}
CHUNKS = 2
MIB = 1 << 20
VMEM = pl.BlockSpec(memory_space=pltpu.VMEM)
SMEM = pl.BlockSpec(memory_space=pltpu.SMEM)
ANY = pl.BlockSpec(memory_space=pl.ANY)


HBM = pl.BlockSpec(memory_space=pltpu.HBM)


def positions(groups, ex, layers):
    chips = ex // CORES
    chip, core = lax.axis_index("ex") // CORES, lax.axis_index("ex") % CORES
    ids = [lax.rem(chip + k, chips) * CORES + (core ^ s) for k in range(chips) for s in range(CORES)]
    blocks = [lax.axis_index("layer") ^ r for r in range(layers)]
    place = [lax.rem(lax.axis_index("groups") + j, groups) for j in range(groups)]
    return ids, blocks, place


def take_kernel(chunk, source, after, out, sem):
    rows = out.shape[0]
    at = pl.multiple_of((lax.axis_index("groups") * CHUNKS + chunk) * rows, rows)
    copy = pltpu.make_async_copy(source.at[pl.ds(at, rows), :], out, sem)
    copy.start()
    copy.wait()


def take(name, chunk, source, after, rows):
    return pl.pallas_call(
        functools.partial(take_kernel, chunk),
        out_shape=pltpu.VMEM((rows, source.shape[1]), BF16),
        in_specs=[HBM, VMEM if chunk else ANY],
        out_specs=VMEM,
        scratch_shapes=[pltpu.SemaphoreType.DMA],
        compiler_params=pltpu.CompilerParams(vmem_limit_bytes=2 * MIB),
        cost_estimate=cost(name),
        name=name,
    )(pltpu.with_memory_space_constraint(source, pltpu.HBM), after)


def cut_kernel(half, source, out):
    rows = out.shape[0]
    out[...] = source[half * rows : (half + 1) * rows, :]


def cut(name, half, source):
    shape = (source.shape[0] // 2, source.shape[1])
    return pl.pallas_call(
        functools.partial(cut_kernel, half),
        out_shape=pltpu.VMEM(shape, BF16),
        in_specs=[VMEM],
        out_specs=VMEM,
        compiler_params=pltpu.CompilerParams(vmem_limit_bytes=4 * MIB),
        cost_estimate=cost(name),
        name=name,
    )(source)


def cost(name):
    return pl.CostEstimate(flops=COSTS.get(name, 0), bytes_accessed=1, transcendentals=0)


def load_kernel(source, after, out, sem):
    copy = pltpu.make_async_copy(source, out, sem)
    copy.start()
    copy.wait()


def load(name, source, after):
    return pl.pallas_call(
        load_kernel,
        out_shape=pltpu.VMEM(source.shape, BF16),
        in_specs=[HBM, ANY],
        out_specs=VMEM,
        scratch_shapes=[pltpu.SemaphoreType.DMA],
        compiler_params=pltpu.CompilerParams(vmem_limit_bytes=2 * MIB),
        cost_estimate=cost(name),
        name=name,
    )(pltpu.with_memory_space_constraint(source, pltpu.HBM), after)


def runs_of(ids, at_ids, depth):
    if len(at_ids) == len(ids):
        return [ids[t] * depth for t in at_ids], [(0, 0, len(ids) * depth)]
    span = CORES * depth
    at = [(i // CORES * CORES + ids[t] % CORES) * depth for i, t in enumerate(at_ids)]
    return at, [(i * span, ids[t] // CORES * span, span) for i, t in enumerate(at_ids[::CORES])]


def condition_kernel(sizes, at_ids, more, hess, *rest):
    ids, _, _ = positions(*sizes)
    count = CHUNKS * len(at_ids)
    pieces, rest = rest[:count], rest[count + 1 :]
    before, (out, right) = rest[0] if more else None, rest[more:]
    rows, depth = pieces[0].shape
    places, runs = runs_of(ids, at_ids, depth)
    for i, piece in enumerate(pieces):
        at = pl.multiple_of(places[i // CHUNKS], depth)
        low = i % CHUNKS * rows
        right[low : low + rows, pl.ds(at, depth)] = piece[...]
    total = before[...] if more else None
    for low, column, span in runs:
        term = lax.dot_general(
            hess[:, pl.ds(pl.multiple_of(column, depth), span)],
            right[:, low : low + span],
            (((1,), (1,)), ((), ())),
            preferred_element_type=F32,
        )
        total = term if total is None else total + term
    out[...] = total.astype(out.dtype)


def condition(name, sizes, hess, at_ids, pieces, after, before=None):
    queries, depth = CHUNKS * pieces[0][0].shape[0], pieces[0][0].shape[1]
    flat = [x for xs in pieces for x in xs]
    more = [] if before is None else [before]
    return pl.pallas_call(
        functools.partial(condition_kernel, sizes, at_ids, len(more)),
        out_shape=pltpu.VMEM((hess.shape[0], queries), BF16 if more else F32),
        in_specs=[VMEM] * (1 + len(flat)) + [ANY] + [VMEM] * len(more),
        out_specs=VMEM,
        scratch_shapes=[pltpu.VMEM((queries, len(pieces) * depth), BF16)],
        compiler_params=pltpu.CompilerParams(vmem_limit_bytes=12 * MIB),
        cost_estimate=cost(name),
        name=name,
    )(hess, *flat, after, *more)


def score_kernel(sizes, at_ids, offsets, more, store, *rest):
    ids, blocks, _ = positions(*sizes)
    layers = len(blocks)
    pieces, rest = rest[: len(offsets)], rest[len(offsets) + 1 :]
    before, (*outs, right) = rest[0] if more else None, rest[more:]
    depth = right.shape[0] // len(at_ids)
    rows = store.shape[0] // layers
    places, runs = runs_of(ids, at_ids, depth)
    for (i, offset), piece in zip(offsets, pieces):
        count = piece.shape[0]
        right[pl.ds(pl.multiple_of(places[i] + offset, count), count), :] = piece[...]
    for r in [*range(1, layers, 2), *range(0, layers, 2)]:
        at = pl.ds(pl.multiple_of(blocks[r] * rows, rows), rows)
        part = before[r] if more else None
        for low, column, span in runs:
            columns = pl.ds(pl.multiple_of(column, depth), span)
            term = jnp.dot(store[at, columns], right[low : low + span, :], preferred_element_type=F32)
            part = term if part is None else part + term
        if len(outs) == 1:
            outs[0][r] = part
            continue
        cut = 2 * part.shape[1] // len(outs)
        for i in range(len(outs) // 2):
            out = outs[2 * i + 1 - r % 2]
            out[r // 2] = part[:, i * cut : (i + 1) * cut].astype(out.dtype)


def score(name, sizes, store, at_ids, pieces, after, before=None, cuts=0):
    width = pieces[0][0].shape[1]
    layers = sizes[2]
    rows = store.shape[0] // layers
    shapes = [((layers, rows, width), F32)]
    if cuts:
        shapes = [((layers // 2, rows, width // cuts), t) for t in (BF16, F32)] * cuts
    more = [] if before is None else [before]
    offsets, flat = [], []
    for i, xs in enumerate(pieces):
        low = 0
        for x in xs:
            offsets.append((i, low))
            flat.append(x)
            low += x.shape[0]
    return pl.pallas_call(
        functools.partial(score_kernel, sizes, at_ids, tuple(offsets), len(more)),
        out_shape=[pltpu.VMEM(*shape) for shape in shapes],
        in_specs=[VMEM] * (1 + len(flat)) + [ANY] + [VMEM] * len(more),
        out_specs=[VMEM] * len(shapes),
        scratch_shapes=[pltpu.VMEM((len(at_ids) * low, width), BF16)],
        compiler_params=pltpu.CompilerParams(vmem_limit_bytes=12 * MIB),
        cost_estimate=cost(name),
        name=name,
    )(store, *flat, after, *more)


def fold_kernel(keep, got, _, send, left):
    for r in range(keep.shape[0]):
        total = keep[r] + got[r].astype(F32)
        if r % 2:
            send[r // 2] = total.astype(BF16)
        else:
            left[r // 2] = total


def fold(name, keep, got, after):
    shape = (keep.shape[0] // 2,) + keep.shape[1:]
    return pl.pallas_call(
        fold_kernel,
        out_shape=(pltpu.VMEM(shape, BF16), pltpu.VMEM(shape, F32)),
        in_specs=[VMEM, VMEM, ANY],
        out_specs=(VMEM, VMEM),
        compiler_params=pltpu.CompilerParams(vmem_limit_bytes=4 * MIB),
        cost_estimate=cost(name),
        name=name,
    )(keep, got, after)


def finish_kernel(sizes, places, *refs):
    _, _, place = positions(*sizes)
    *refs, out = refs
    span = out.shape[1] // len(place)
    for i, (j, column) in enumerate(places):
        keep, got = refs[2 * i : 2 * i + 2]
        at = pl.multiple_of(place[j] * span + column, keep.shape[2])
        out[:, pl.ds(at, keep.shape[2])] = keep[0] + got[0].astype(F32)


def finish(sizes, parts, queries):
    rows = parts[0][1][0].shape[1]
    return pl.pallas_call(
        functools.partial(finish_kernel, sizes, tuple(place for place, _ in parts)),
        out_shape=jax.ShapeDtypeStruct((rows, queries), F32),
        in_specs=[VMEM] * (2 * len(parts)),
        out_specs=VMEM,
        compiler_params=pltpu.CompilerParams(vmem_limit_bytes=12 * MIB),
        name="finish",
    )(*[a for _, part in parts for a in part])


def shards(groups, ex, layers, queries, hessian, store):
    chips = ex // CORES
    sizes = groups, ex, layers
    total = queries.shape[0]

    def permute(x, axis, perm, what):
        with jax.named_scope(what):
            return lax.ppermute(x, axis, perm)

    def from_chip(x, k, what):
        perm = [(e, (e - k * CORES) % ex) for e in range(ex)]
        return permute(x, "ex", perm, what + "_from_chip")

    def from_core(x, what):
        return permute(x, "ex", [(e, e ^ 1) for e in range(ex)], what + "_from_core")

    def from_group(x, j, what):
        perm = [(g, (g - j) % groups) for g in range(groups)]
        return permute(x, "groups", perm, what + "_from_group")

    def from_layer(x, r, what):
        return permute(x, "layer", [(z, z ^ r) for z in range(layers)], f"{what}_from_layer_{r}")

    def tie(x, *others):
        return lax.optimization_barrier((x, *others))[0]

    def gather_chip(x, what):
        return [from_chip(x, k, what) for k in range(1, chips)]

    def gather_group(x, what):
        return [from_group(x, j, what) for j in range(1, groups)]

    def with_cores(ours, theirs):
        return [x for pair in zip(ours, theirs) for x in pair]

    def flip(xs, what):
        return [from_core(x, what) for x in xs]

    def after(token, xs):
        return [tie(x, token) for x in xs]

    everywhere = tuple(range(ex))
    here, there = everywhere[:CORES], everywhere[CORES:]

    def step(name, keep, got, token):
        if keep.shape[0] == 1:
            return keep, got
        send, keep = fold(name, keep, got, token)
        return keep, from_layer(send, layers // keep.shape[0] // 2, name)

    source = queries[:, 0, :]
    width = total // groups // CHUNKS
    rows = pltpu.with_memory_space_constraint(store[:, 0, :], pltpu.VMEM)
    mine = [take("take0", 0, source, source[:8], width)]
    mine_there, mine_core = [gather_chip(mine[0], "queries0")], [from_core(mine[0], "queries0")]
    mine.append(take("take1", 1, source, mine_core[0], width))
    mine_there.append(gather_chip(mine[1], "queries1"))
    mine_core.append(from_core(mine[1], "queries1"))
    hess = load("load_hessian", hessian[0], mine[1])
    part = condition("condition_here", sizes, hess, here, [mine, mine_core], hess)
    pieces = []
    for xs in zip(*[after(part, xs) for xs in mine_there]):
        pieces += [xs, flip(xs, "queries_there")]
    share = condition("condition_there", sizes, hess, there, pieces, part, part)
    by_chip, by_group = gather_chip(share, "share"), gather_group(share, "share")
    share_core = from_core(share, "share")
    part = score("own_here", sizes, rows, here, [[share], [share_core]], share)[0]
    by_chip, by_group = after(part, by_chip), after(part, by_group)
    by_chip_cores, by_group_cores = flip(by_chip, "by_chip"), flip(by_group, "by_group")
    upper = [cut("cut0", 0, x) for x in by_chip]
    lower = [cut("cut1", 1, x) for x in by_group]
    upper = [[from_group(x, j, "upper") for x in upper] for j in range(1, groups)]
    lower = [gather_chip(x, "lower") for x in lower]
    pieces = [[x] for x in with_cores(by_chip, by_chip_cores)]
    send, keep = score("own_there", sizes, rows, there, pieces, part, part, 1)
    parts = [((0, 0), (keep, from_layer(send, 1, "own")))]
    token = keep
    for j in range(groups - 1):
        pieces = [[by_group[j]], [by_group_cores[j]]]
        part = score("other_here", sizes, rows, here, pieces, token)[0]
        halves = [after(part, pair) for pair in zip(upper[j], lower[j])]
        flips = [flip(pair, "diagonal") for pair in halves]
        pieces = [x for pair in zip(halves, flips) for x in pair]
        made = score("other_there", sizes, rows, there, pieces, part, part, 2)
        columns = made[0].shape[2]
        for c in range(2):
            send, token = made[2 * c : 2 * c + 2]
            parts.append(((j + 1, c * columns), (token, from_layer(send, 1, f"other{c}"))))
    while any(part[0].shape[0] > 1 for _, part in parts):
        parts = [(at, step(f"sum{i}", *part, token)) for i, (at, part) in enumerate(parts)]
    return finish(sizes, parts, total)


def solution(mesh):
    groups, ex, layers = (mesh.shape[a] for a in ("groups", "ex", "layer"))
    in_specs = (P(None, "layer", "ex"), P("layer", "ex", None), P(("groups", "ex"), "layer", None))
    out_specs = P(("groups", "ex", "layer"), None)
    return jax.shard_map(
        functools.partial(shards, groups, ex, layers),
        mesh=mesh,
        in_specs=in_specs,
        out_specs=out_specs,
        check_vma=False,
    )
```

```python
import functools

import jax
import jax.numpy as jnp
from jax import lax
from jax.experimental import pallas as pl
from jax.experimental.pallas import tpu as pltpu
from jax.sharding import PartitionSpec as P

F32, BF16 = jnp.float32, jnp.bfloat16
CORES = 2
CHUNKS = 2
MIB = 1 << 20
VMEM = pl.BlockSpec(memory_space=pltpu.VMEM)
SMEM = pl.BlockSpec(memory_space=pltpu.SMEM)
ANY = pl.BlockSpec(memory_space=pl.ANY)


HBM = pl.BlockSpec(memory_space=pltpu.HBM)


def positions(groups, ex, layers, place):
    at_group, at_ex, at_layer = (ref[0] for ref in place)
    chips = ex // CORES
    chip, core = at_ex // CORES, lax.rem(at_ex, CORES)
    ids = [lax.rem(chip + k, chips) * CORES + (core ^ s) for k in range(chips) for s in range(CORES)]
    blocks = [at_layer ^ r for r in range(layers)]
    return ids, blocks, [lax.rem(at_group + j, groups) for j in range(groups)]


def load_kernel(source, after, out, sem):
    copy = pltpu.make_async_copy(source, out, sem)
    copy.start()
    copy.wait()


def load(source, after):
    return pl.pallas_call(
        load_kernel,
        out_shape=pltpu.VMEM(source.shape, BF16),
        in_specs=[HBM, ANY],
        out_specs=VMEM,
        scratch_shapes=[pltpu.SemaphoreType.DMA],
        compiler_params=pltpu.CompilerParams(vmem_limit_bytes=2 * MIB),
        name="load",
    )(pltpu.with_memory_space_constraint(source, pltpu.HBM), after)


def take_kernel(chunk, at_group, source, after, out, sem):
    rows = out.shape[0]
    at = pl.multiple_of((at_group[0] * CHUNKS + chunk) * rows, rows)
    copy = pltpu.make_async_copy(source.at[pl.ds(at, rows), :], out, sem)
    copy.start()
    copy.wait()


def take(chunk, place, source, after, rows):
    return pl.pallas_call(
        functools.partial(take_kernel, chunk),
        out_shape=pltpu.VMEM((rows, source.shape[1]), BF16),
        in_specs=[SMEM, HBM, ANY],
        out_specs=VMEM,
        scratch_shapes=[pltpu.SemaphoreType.DMA],
        compiler_params=pltpu.CompilerParams(vmem_limit_bytes=2 * MIB),
        name="take",
    )(place[0], pltpu.with_memory_space_constraint(source, pltpu.HBM), after)


def condition_kernel(sizes, *refs):
    place, (hess, *rest) = refs[:3], refs[3:]
    ids, _, _ = positions(*sizes, place)
    pieces, (_, out, right) = rest[: len(ids)], rest[len(ids) :]
    width = pieces[0].shape[1]
    for t, piece in zip(ids, pieces):
        right[:, pl.ds(pl.multiple_of(t * width, width), width)] = piece[...]
    out[...] = lax.dot_general(
        hess[...], right[...], (((1,), (1,)), ((), ())), preferred_element_type=F32
    ).astype(BF16)


def condition(sizes, place, hess, pieces, after):
    rows, queries = hess.shape[0], pieces[0].shape[0]
    return pl.pallas_call(
        functools.partial(condition_kernel, sizes),
        out_shape=pltpu.VMEM((rows, queries), BF16),
        in_specs=[SMEM] * 3 + [VMEM] * (1 + len(pieces)) + [ANY],
        out_specs=VMEM,
        scratch_shapes=[pltpu.VMEM((queries, hess.shape[1]), BF16)],
        compiler_params=pltpu.CompilerParams(vmem_limit_bytes=12 * MIB),
        name="condition",
    )(*place, hess, *pieces, after)


def score_kernel(sizes, direct, *refs):
    place, (store, *rest) = refs[:3], refs[3:]
    ids, blocks, _ = positions(*sizes, place)
    layers = len(blocks)
    pieces, (_, *outs, right) = rest[: len(ids)], rest[len(ids) :]
    rows = store.shape[0] // layers
    depth = pieces[0].shape[0]
    for t, piece in zip(ids, pieces):
        right[pl.ds(pl.multiple_of(t * depth, depth), depth), :] = piece[...]
    for r in [*range(1, layers, 2), *range(0, layers, 2)]:
        at = pl.ds(pl.multiple_of(blocks[r] * rows, rows), rows)
        part = jnp.dot(store[at, :], right[...], preferred_element_type=F32)
        if direct:
            outs[r][0] = part.astype(outs[r].dtype)
        else:
            outs[1 - r % 2][r // 2] = part.astype(outs[1 - r % 2].dtype)


def score(name, sizes, place, store, pieces, after, direct=False):
    depth, width = pieces[0].shape
    layers = sizes[2]
    rows = store.shape[0] // layers
    shapes = [((layers // 2, rows, width), t) for t in (BF16, F32)]
    if direct:
        shapes = [((1, rows, width), BF16 if r else F32) for r in range(layers)]
    return pl.pallas_call(
        functools.partial(score_kernel, sizes, direct),
        out_shape=[pltpu.VMEM(*shape) for shape in shapes],
        in_specs=[SMEM] * 3 + [VMEM] * (1 + len(pieces)) + [ANY],
        out_specs=[VMEM] * len(shapes),
        scratch_shapes=[pltpu.VMEM((len(pieces) * depth, width), BF16)],
        compiler_params=pltpu.CompilerParams(vmem_limit_bytes=12 * MIB),
        name=name,
    )(*place, store, *pieces, after)


def fold_kernel(keep, got, _, send, left):
    for r in range(keep.shape[0]):
        total = keep[r] + got[r].astype(F32)
        if r % 2:
            send[r // 2] = total.astype(BF16)
        else:
            left[r // 2] = total


def fold(keep, got, after):
    shape = (keep.shape[0] // 2,) + keep.shape[1:]
    return pl.pallas_call(
        fold_kernel,
        out_shape=(pltpu.VMEM(shape, BF16), pltpu.VMEM(shape, F32)),
        in_specs=[VMEM, VMEM, ANY],
        out_specs=(VMEM, VMEM),
        compiler_params=pltpu.CompilerParams(vmem_limit_bytes=4 * MIB),
        name="fold",
    )(keep, got, after)


def finish_kernel(sizes, counts, *refs):
    place, (*refs, out) = refs[:3], refs[3:]
    _, _, order = positions(*sizes, place)
    groups = len(order)
    width = refs[0].shape[2]
    for i, count in enumerate(counts):
        (keep, *rest), refs = refs[:count], refs[count:]
        total = keep[0]
        for got in rest:
            total = total + got[0].astype(F32)
        at = order[i % groups] * (out.shape[1] // groups) + i // groups * width
        out[:, pl.ds(pl.multiple_of(at, width), width)] = total


def finish(sizes, place, parts, queries):
    rows = parts[0][0].shape[1]
    return pl.pallas_call(
        functools.partial(finish_kernel, sizes, tuple(map(len, parts))),
        out_shape=jax.ShapeDtypeStruct((rows, queries), F32),
        in_specs=[SMEM] * 3 + [VMEM] * sum(map(len, parts)),
        out_specs=VMEM,
        compiler_params=pltpu.CompilerParams(vmem_limit_bytes=12 * MIB),
        name="finish",
    )(*place, *[a for part in parts for a in part])


def shards(groups, ex, layers, queries, hessian, store):
    chips = ex // CORES
    sizes = groups, ex, layers
    total = queries.shape[0]
    place = [lax.axis_index(a).astype(jnp.int32)[None] for a in ("groups", "ex", "layer")]

    def permute(x, axis, perm, what):
        with jax.named_scope(what):
            return lax.ppermute(x, axis, perm)

    def from_chip(x, k, what):
        perm = [(e, (e - k * CORES) % ex) for e in range(ex)]
        return permute(x, "ex", perm, what + "_from_chip")

    def from_core(x, what):
        return permute(x, "ex", [(e, e ^ 1) for e in range(ex)], what + "_from_core")

    def from_group(x, j, what):
        perm = [(g, (g - j) % groups) for g in range(groups)]
        return permute(x, "groups", perm, what + "_from_group")

    def from_layer(x, r, what):
        return permute(x, "layer", [(z, z ^ r) for z in range(layers)], f"{what}_from_layer_{r}")

    def tie(x, *others):
        return lax.optimization_barrier((x, *others))[0]

    def gather_chip(x, what):
        return [from_chip(x, k, what) for k in range(1, chips)]

    def gather_group(x, what):
        return [from_group(x, j, what) for j in range(1, groups)]

    def with_cores(ours, theirs):
        return [x for pair in zip(ours, theirs) for x in pair]

    def flip(xs, what):
        return [from_core(x, what) for x in xs]

    def after(token, xs):
        return [tie(x, token) for x in xs]

    parts = []

    def advance(token, chain=False):
        for i, part in enumerate(parts):
            if part[0].shape[0] > 1:
                if chain and i and parts[i - 1][0].shape[0] == 1:
                    token = tie(token, parts[i - 1][1])
                send, keep = fold(part[0], part[1], token)
                step = layers // keep.shape[0] // 2
                part[:] = keep, from_layer(send, step, f"sum{i}")

    def send_parts(made):
        send, keep = made
        advance(keep, chain=True)
        parts.append([keep, from_layer(send, 1, f"sum{len(parts)}")])
        return parts[-2][0] if parts[1:] else keep

    rows = pltpu.with_memory_space_constraint(store[:, 0, :], pltpu.VMEM)
    width = total // groups // CHUNKS
    q0 = take(0, place, queries[:, 0, :], place[0], width)
    q0_there, q0_core = gather_chip(q0, "q0"), from_core(q0, "q0")
    hess = load(hessian[0], q0)
    q1 = take(1, place, queries[:, 0, :], hess, width)
    q0_there = after(q1, q0_there)
    q0_cores = [q0_core] + flip(q0_there, "q0_there")
    q1_there, q1_core = gather_chip(q1, "q1"), from_core(q1, "q1")
    s0 = condition(sizes, place, hess, with_cores([q0] + q0_there, q0_cores), q1)
    s0_there, s0_across, s0_core = gather_chip(s0, "s0"), gather_group(s0, "s0"), from_core(s0, "s0")
    q1_there = after(s0, q1_there)
    q1_cores = [q1_core] + flip(q1_there, "q1_there")
    s0_diagonal = [gather_group(x, "s0_there") for x in s0_there]
    s0_cores = [s0_core] + flip(s0_there, "s0_there")
    s1 = condition(sizes, place, hess, with_cores([q1] + q1_there, q1_cores), s0_there[-1])
    s1_there, s1_core = gather_chip(s1, "s1"), from_core(s1, "s1")
    s0_across = after(s1, s0_across)
    s0_across_cores = flip(s0_across, "s0_across")
    last = send_parts(score("score0", sizes, place, rows, with_cores([s0] + s0_there, s0_cores), s1))
    s0_diagonal = [after(last, xs) for xs in s0_diagonal]
    s0_diagonal_cores = [flip(xs, "s0_diagonal") for xs in s0_diagonal]
    s1_across = gather_group(tie(s1, s0_diagonal[-1][-1]), "s1")
    s1_there = after(last, s1_there)
    s1_diagonal = [gather_group(x, "s1_there") for x in s1_there]
    s1_cores = [s1_core] + flip(s1_there, "s1_there")
    for j in range(groups - 1):
        ours = [s0_across[j]] + [xs[j] for xs in s0_diagonal]
        theirs = [s0_across_cores[j]] + [xs[j] for xs in s0_diagonal_cores]
        last = send_parts(score("score1", sizes, place, rows, with_cores(ours, theirs), last))
    last = send_parts(score("score2", sizes, place, rows, with_cores([s1] + s1_there, s1_cores), last))
    s1_across = after(last, s1_across)
    s1_across_cores = flip(s1_across, "s1_across")
    s1_diagonal = [after(last, xs) for xs in s1_diagonal]
    s1_diagonal_cores = [flip(xs, "s1_diagonal") for xs in s1_diagonal]
    for j in range(groups - 1):
        ours = [s1_across[j]] + [xs[j] for xs in s1_diagonal]
        theirs = [s1_across_cores[j]] + [xs[j] for xs in s1_diagonal_cores]
        made = score("score3", sizes, place, rows, with_cores(ours, theirs), last, direct=True)
        advance(made[0])
        parts.append([made[0]] + [from_layer(made[r], r, f"last{j}") for r in range(1, layers)])
    while any(part[0].shape[0] > 1 for part in parts):
        advance(last)
    return finish(sizes, place, parts, total)


def solution(mesh):
    groups, ex, layers = (mesh.shape[a] for a in ("groups", "ex", "layer"))
    in_specs = (P(None, "layer", "ex"), P("layer", "ex", None), P(("groups", "ex"), "layer", None))
    out_specs = P(("groups", "ex", "layer"), None)
    return jax.shard_map(
        functools.partial(shards, groups, ex, layers),
        mesh=mesh,
        in_specs=in_specs,
        out_specs=out_specs,
        check_vma=False,
    )
```

```python
import functools

import jax
import jax.numpy as jnp
from jax import lax
from jax.experimental import pallas as pl
from jax.experimental.pallas import tpu as pltpu
from jax.sharding import PartitionSpec as P

F32, BF16 = jnp.float32, jnp.bfloat16
CORES = 2
CHUNKS = 2
MIB = 1 << 20
VMEM = pl.BlockSpec(memory_space=pltpu.VMEM)
SMEM = pl.BlockSpec(memory_space=pltpu.SMEM)
ANY = pl.BlockSpec(memory_space=pl.ANY)


HBM = pl.BlockSpec(memory_space=pltpu.HBM)


def positions(groups, ex, layers, place):
    at_group, at_ex, at_layer = (ref[0] for ref in place)
    chips = ex // CORES
    chip, core = at_ex // CORES, lax.rem(at_ex, CORES)
    ids = [lax.rem(chip + k, chips) * CORES + (core ^ s) for k in range(chips) for s in range(CORES)]
    blocks = [at_layer ^ r for r in range(layers)]
    return ids, blocks, [lax.rem(at_group + j, groups) for j in range(groups)]


def load_kernel(source, after, out, sem):
    copy = pltpu.make_async_copy(source, out, sem)
    copy.start()
    copy.wait()


def load(source, after):
    return pl.pallas_call(
        load_kernel,
        out_shape=pltpu.VMEM(source.shape, BF16),
        in_specs=[HBM, ANY],
        out_specs=VMEM,
        scratch_shapes=[pltpu.SemaphoreType.DMA],
        compiler_params=pltpu.CompilerParams(vmem_limit_bytes=2 * MIB),
        name="load",
    )(pltpu.with_memory_space_constraint(source, pltpu.HBM), after)


def take_kernel(chunk, at_group, at_ex, at_layer, source, after, out, sem):
    rows = out.shape[0]
    at = pl.multiple_of((at_group[0] * CHUNKS + chunk) * rows, rows)
    copy = pltpu.make_async_copy(source.at[pl.ds(at, rows), :], out, sem)
    copy.start()
    copy.wait()


def take(chunk, place, source, after, rows):
    return pl.pallas_call(
        functools.partial(take_kernel, chunk),
        out_shape=pltpu.VMEM((rows, source.shape[1]), BF16),
        in_specs=[SMEM] * 3 + [HBM, ANY],
        out_specs=VMEM,
        scratch_shapes=[pltpu.SemaphoreType.DMA],
        compiler_params=pltpu.CompilerParams(vmem_limit_bytes=2 * MIB),
        name="take",
    )(*place, pltpu.with_memory_space_constraint(source, pltpu.HBM), after)


def condition_kernel(sizes, *refs):
    place, (hess, *rest) = refs[:3], refs[3:]
    ids, _, _ = positions(*sizes, place)
    pieces, (_, out, right) = rest[: len(ids)], rest[len(ids) :]
    width = pieces[0].shape[1]
    for t, piece in zip(ids, pieces):
        right[:, pl.ds(pl.multiple_of(t * width, width), width)] = piece[...]
    out[...] = lax.dot_general(
        hess[...], right[...], (((1,), (1,)), ((), ())), preferred_element_type=F32
    ).astype(BF16)


def condition(sizes, place, hess, pieces, after):
    rows, queries = hess.shape[0], pieces[0].shape[0]
    return pl.pallas_call(
        functools.partial(condition_kernel, sizes),
        out_shape=pltpu.VMEM((rows, queries), BF16),
        in_specs=[SMEM] * 3 + [VMEM] * (1 + len(pieces)) + [ANY],
        out_specs=VMEM,
        scratch_shapes=[pltpu.VMEM((queries, hess.shape[1]), BF16)],
        compiler_params=pltpu.CompilerParams(vmem_limit_bytes=12 * MIB),
        name="condition",
    )(*place, hess, *pieces, after)


def score_kernel(sizes, direct, *refs):
    place, (store, *rest) = refs[:3], refs[3:]
    ids, blocks, _ = positions(*sizes, place)
    layers = len(blocks)
    pieces, (_, *outs, right) = rest[: len(ids)], rest[len(ids) :]
    rows = store.shape[0] // layers
    depth = pieces[0].shape[0]
    for t, piece in zip(ids, pieces):
        right[pl.ds(pl.multiple_of(t * depth, depth), depth), :] = piece[...]
    for r in [*range(1, layers, 2), *range(0, layers, 2)]:
        at = pl.ds(pl.multiple_of(blocks[r] * rows, rows), rows)
        part = jnp.dot(store[at, :], right[...], preferred_element_type=F32)
        if direct:
            outs[r][0] = part.astype(outs[r].dtype)
        else:
            outs[1 - r % 2][r // 2] = part.astype(outs[1 - r % 2].dtype)


def score(name, sizes, place, store, pieces, after, direct=False):
    depth, width = pieces[0].shape
    layers = sizes[2]
    rows = store.shape[0] // layers
    shapes = [((layers // 2, rows, width), t) for t in (BF16, F32)]
    if direct:
        shapes = [((1, rows, width), BF16 if r else F32) for r in range(layers)]
    return pl.pallas_call(
        functools.partial(score_kernel, sizes, direct),
        out_shape=[pltpu.VMEM(*shape) for shape in shapes],
        in_specs=[SMEM] * 3 + [VMEM] * (1 + len(pieces)) + [ANY],
        out_specs=[VMEM] * len(shapes),
        scratch_shapes=[pltpu.VMEM((len(pieces) * depth, width), BF16)],
        compiler_params=pltpu.CompilerParams(vmem_limit_bytes=12 * MIB),
        name=name,
    )(*place, store, *pieces, after)


def fold_kernel(keep, got, _, send, left):
    for r in range(keep.shape[0]):
        total = keep[r] + got[r].astype(F32)
        if r % 2:
            send[r // 2] = total.astype(BF16)
        else:
            left[r // 2] = total


def fold(keep, got, after):
    shape = (keep.shape[0] // 2,) + keep.shape[1:]
    return pl.pallas_call(
        fold_kernel,
        out_shape=(pltpu.VMEM(shape, BF16), pltpu.VMEM(shape, F32)),
        in_specs=[VMEM, VMEM, ANY],
        out_specs=(VMEM, VMEM),
        compiler_params=pltpu.CompilerParams(vmem_limit_bytes=4 * MIB),
        name="fold",
    )(keep, got, after)


def finish_kernel(sizes, counts, *refs):
    place, (*refs, out) = refs[:3], refs[3:]
    _, _, order = positions(*sizes, place)
    groups = len(order)
    width = refs[0].shape[2]
    for i, count in enumerate(counts):
        (keep, *rest), refs = refs[:count], refs[count:]
        total = keep[0]
        for got in rest:
            total = total + got[0].astype(F32)
        at = order[i % groups] * (out.shape[1] // groups) + i // groups * width
        out[:, pl.ds(pl.multiple_of(at, width), width)] = total


def finish(sizes, place, parts, queries):
    rows = parts[0][0].shape[1]
    return pl.pallas_call(
        functools.partial(finish_kernel, sizes, tuple(map(len, parts))),
        out_shape=jax.ShapeDtypeStruct((rows, queries), F32),
        in_specs=[SMEM] * 3 + [VMEM] * sum(map(len, parts)),
        out_specs=VMEM,
        compiler_params=pltpu.CompilerParams(vmem_limit_bytes=12 * MIB),
        name="finish",
    )(*place, *[a for part in parts for a in part])


def shards(groups, ex, layers, queries, hessian, store):
    chips = ex // CORES
    sizes = groups, ex, layers
    total = queries.shape[0]
    place = [lax.axis_index(a).astype(jnp.int32)[None] for a in ("groups", "ex", "layer")]

    def permute(x, axis, perm, what):
        with jax.named_scope(what):
            return lax.ppermute(x, axis, perm)

    def from_chip(x, k, what):
        perm = [(e, (e - k * CORES) % ex) for e in range(ex)]
        return permute(x, "ex", perm, what + "_from_chip")

    def from_core(x, what):
        return permute(x, "ex", [(e, e ^ 1) for e in range(ex)], what + "_from_core")

    def from_group(x, j, what):
        perm = [(g, (g - j) % groups) for g in range(groups)]
        return permute(x, "groups", perm, what + "_from_group")

    def from_layer(x, r, what):
        return permute(x, "layer", [(z, z ^ r) for z in range(layers)], f"{what}_from_layer_{r}")

    def tie(x, *others):
        return lax.optimization_barrier((x, *others))[0]

    def gather_chip(x, what):
        return [from_chip(x, k, what) for k in range(1, chips)]

    def gather_group(x, what):
        return [from_group(x, j, what) for j in range(1, groups)]

    def with_cores(ours, theirs):
        return [x for pair in zip(ours, theirs) for x in pair]

    def flip(xs, what):
        return [from_core(x, what) for x in xs]

    def after(token, xs):
        return [tie(x, token) for x in xs]

    parts = []

    def advance(token, chain=False):
        for i, part in enumerate(parts):
            if part[0].shape[0] > 1:
                if chain and i and parts[i - 1][0].shape[0] == 1:
                    token = tie(token, parts[i - 1][1])
                send, keep = fold(part[0], part[1], token)
                step = layers // keep.shape[0] // 2
                part[:] = keep, from_layer(send, step, f"sum{i}")

    def send_parts(made):
        send, keep = made
        advance(keep, chain=True)
        parts.append([keep, from_layer(send, 1, f"sum{len(parts)}")])
        return parts[-2][0] if parts[1:] else keep

    rows = pltpu.with_memory_space_constraint(store[:, 0, :], pltpu.VMEM)
    width = total // groups // CHUNKS
    q0 = take(0, place, queries[:, 0, :], place[0], width)
    q0_there, q0_core = gather_chip(q0, "q0"), from_core(q0, "q0")
    hess = load(hessian[0], q0)
    q1 = take(1, place, queries[:, 0, :], hess, width)
    q0_there = after(q1, q0_there)
    q0_cores = [q0_core] + flip(q0_there, "q0_there")
    q1_there, q1_core = gather_chip(q1, "q1"), from_core(q1, "q1")
    s0 = condition(sizes, place, hess, with_cores([q0] + q0_there, q0_cores), q1)
    s0_there, s0_across, s0_core = gather_chip(s0, "s0"), gather_group(s0, "s0"), from_core(s0, "s0")
    q1_there = after(s0, q1_there)
    q1_cores = [q1_core] + flip(q1_there, "q1_there")
    s0_diagonal = [gather_group(x, "s0_there") for x in s0_there]
    s0_cores = [s0_core] + flip(s0_there, "s0_there")
    s1 = condition(sizes, place, hess, with_cores([q1] + q1_there, q1_cores), s0_there[-1])
    s1_there, s1_core = gather_chip(s1, "s1"), from_core(s1, "s1")
    s0_across = after(s1, s0_across)
    s0_across_cores = flip(s0_across, "s0_across")
    last = send_parts(score("score0", sizes, place, rows, with_cores([s0] + s0_there, s0_cores), s1))
    s0_diagonal = [after(last, xs) for xs in s0_diagonal]
    s0_diagonal_cores = [flip(xs, "s0_diagonal") for xs in s0_diagonal]
    s1_across = gather_group(tie(s1, s0_diagonal[-1][-1]), "s1")
    s1_there = after(last, s1_there)
    s1_diagonal = [gather_group(x, "s1_there") for x in s1_there]
    s1_cores = [s1_core] + flip(s1_there, "s1_there")
    for j in range(groups - 1):
        ours = [s0_across[j]] + [xs[j] for xs in s0_diagonal]
        theirs = [s0_across_cores[j]] + [xs[j] for xs in s0_diagonal_cores]
        last = send_parts(score("score1", sizes, place, rows, with_cores(ours, theirs), last))
    last = send_parts(score("score2", sizes, place, rows, with_cores([s1] + s1_there, s1_cores), last))
    s1_across = after(last, s1_across)
    s1_across_cores = flip(s1_across, "s1_across")
    s1_diagonal = [after(last, xs) for xs in s1_diagonal]
    s1_diagonal_cores = [flip(xs, "s1_diagonal") for xs in s1_diagonal]
    for j in range(groups - 1):
        ours = [s1_across[j]] + [xs[j] for xs in s1_diagonal]
        theirs = [s1_across_cores[j]] + [xs[j] for xs in s1_diagonal_cores]
        made = score("score3", sizes, place, rows, with_cores(ours, theirs), last, direct=True)
        advance(made[0])
        parts.append([made[0]] + [from_layer(made[r], r, f"last{j}") for r in range(1, layers)])
    while any(part[0].shape[0] > 1 for part in parts):
        advance(last)
    return finish(sizes, place, parts, total)


def solution(mesh):
    groups, ex, layers = (mesh.shape[a] for a in ("groups", "ex", "layer"))
    in_specs = (P(None, "layer", "ex"), P("layer", "ex", None), P(("groups", "ex"), "layer", None))
    out_specs = P(("groups", "ex", "layer"), None)
    return jax.shard_map(
        functools.partial(shards, groups, ex, layers),
        mesh=mesh,
        in_specs=in_specs,
        out_specs=out_specs,
        check_vma=False,
    )
```

```python
import functools

import jax
import jax.numpy as jnp
from jax import lax
from jax.experimental import pallas as pl
from jax.experimental.pallas import tpu as pltpu
from jax.sharding import PartitionSpec as P

F32, BF16 = jnp.float32, jnp.bfloat16
CORES = 2
CHUNKS = 2
MIB = 1 << 20
VMEM = pl.BlockSpec(memory_space=pltpu.VMEM)
SMEM = pl.BlockSpec(memory_space=pltpu.SMEM)
ANY = pl.BlockSpec(memory_space=pl.ANY)


HBM = pl.BlockSpec(memory_space=pltpu.HBM)


def positions(groups, ex, layers, place):
    at_group, at_ex, at_layer = (ref[0] for ref in place)
    chips = ex // CORES
    chip, core = at_ex // CORES, lax.rem(at_ex, CORES)
    ids = [lax.rem(chip + k, chips) * CORES + (core ^ s) for k in range(chips) for s in range(CORES)]
    blocks = [at_layer ^ r for r in range(layers)]
    return ids, blocks, [lax.rem(at_group + j, groups) for j in range(groups)]


def load_kernel(source, after, out, sem):
    copy = pltpu.make_async_copy(source, out, sem)
    copy.start()
    copy.wait()


def load(source, after):
    return pl.pallas_call(
        load_kernel,
        out_shape=pltpu.VMEM(source.shape, BF16),
        in_specs=[HBM, ANY],
        out_specs=VMEM,
        scratch_shapes=[pltpu.SemaphoreType.DMA],
        compiler_params=pltpu.CompilerParams(vmem_limit_bytes=2 * MIB),
        name="load",
    )(pltpu.with_memory_space_constraint(source, pltpu.HBM), after)


def take_kernel(chunk, at_group, at_ex, at_layer, source, after, out, sem):
    rows = out.shape[0]
    at = pl.multiple_of((at_group[0] * CHUNKS + chunk) * rows, rows)
    copy = pltpu.make_async_copy(source.at[pl.ds(at, rows), :], out, sem)
    copy.start()
    copy.wait()


def take(chunk, place, source, after, rows):
    return pl.pallas_call(
        functools.partial(take_kernel, chunk),
        out_shape=pltpu.VMEM((rows, source.shape[1]), BF16),
        in_specs=[SMEM] * 3 + [HBM, ANY],
        out_specs=VMEM,
        scratch_shapes=[pltpu.SemaphoreType.DMA],
        compiler_params=pltpu.CompilerParams(vmem_limit_bytes=2 * MIB),
        name="take",
    )(*place, pltpu.with_memory_space_constraint(source, pltpu.HBM), after)


def condition_kernel(sizes, *refs):
    place, (hess, *rest) = refs[:3], refs[3:]
    ids, _, _ = positions(*sizes, place)
    pieces, (_, out, right) = rest[: len(ids)], rest[len(ids) :]
    width = pieces[0].shape[1]
    for t, piece in zip(ids, pieces):
        right[:, pl.ds(pl.multiple_of(t * width, width), width)] = piece[...]
    out[...] = lax.dot_general(
        hess[...], right[...], (((1,), (1,)), ((), ())), preferred_element_type=F32
    ).astype(BF16)


def condition(sizes, place, hess, pieces, after):
    rows, queries = hess.shape[0], pieces[0].shape[0]
    return pl.pallas_call(
        functools.partial(condition_kernel, sizes),
        out_shape=pltpu.VMEM((rows, queries), BF16),
        in_specs=[SMEM] * 3 + [VMEM] * (1 + len(pieces)) + [ANY],
        out_specs=VMEM,
        scratch_shapes=[pltpu.VMEM((queries, hess.shape[1]), BF16)],
        compiler_params=pltpu.CompilerParams(vmem_limit_bytes=12 * MIB),
        name="condition",
    )(*place, hess, *pieces, after)


def score_kernel(sizes, columns, *refs):
    place, (store, *rest) = refs[:3], refs[3:]
    ids, blocks, _ = positions(*sizes, place)
    layers, count = len(blocks), len(ids)
    pieces, (_, *outs, right) = rest[: columns * count], rest[columns * count :]
    rows = store.shape[0] // layers
    depth, width = pieces[0].shape
    for i, piece in enumerate(pieces):
        at = pl.ds(pl.multiple_of(ids[i % count] * depth, depth), depth)
        right[at, i // count * width : (i // count + 1) * width] = piece[...]
    for r in [*range(1, layers, 2), *range(0, layers, 2)]:
        at = pl.ds(pl.multiple_of(blocks[r] * rows, rows), rows)
        part = jnp.dot(store[at, :], right[...], preferred_element_type=F32)
        for c in range(columns):
            out = outs[2 * c + 1 - r % 2]
            out[r // 2] = part[:, c * width : (c + 1) * width].astype(out.dtype)


def score(name, sizes, place, store, pieces, after):
    depth, width = pieces[0][0].shape
    layers, columns = sizes[2], len(pieces)
    rows = store.shape[0] // layers
    shapes = [((layers // 2, rows, width), t) for t in (BF16, F32)] * columns
    flat = [x for xs in pieces for x in xs]
    made = pl.pallas_call(
        functools.partial(score_kernel, sizes, columns),
        out_shape=[pltpu.VMEM(*shape) for shape in shapes],
        in_specs=[SMEM] * 3 + [VMEM] * (1 + len(flat)) + [ANY],
        out_specs=[VMEM] * len(shapes),
        scratch_shapes=[pltpu.VMEM((store.shape[1], columns * width), BF16)],
        compiler_params=pltpu.CompilerParams(vmem_limit_bytes=12 * MIB),
        name=name,
    )(*place, store, *flat, after)
    return [made[2 * c : 2 * c + 2] for c in range(columns)]


def fold_kernel(keep, got, _, send, left):
    for r in range(keep.shape[0]):
        total = keep[r] + got[r].astype(F32)
        if r % 2:
            send[r // 2] = total.astype(BF16)
        else:
            left[r // 2] = total


def fold(keep, got, after):
    shape = (keep.shape[0] // 2,) + keep.shape[1:]
    return pl.pallas_call(
        fold_kernel,
        out_shape=(pltpu.VMEM(shape, BF16), pltpu.VMEM(shape, F32)),
        in_specs=[VMEM, VMEM, ANY],
        out_specs=(VMEM, VMEM),
        compiler_params=pltpu.CompilerParams(vmem_limit_bytes=4 * MIB),
        name="fold",
    )(keep, got, after)


def finish_kernel(sizes, counts, *refs):
    place, (*refs, out) = refs[:3], refs[3:]
    _, _, order = positions(*sizes, place)
    groups = len(order)
    width = refs[0].shape[2]
    for i, count in enumerate(counts):
        (keep, *rest), refs = refs[:count], refs[count:]
        total = keep[0]
        for got in rest:
            total = total + got[0].astype(F32)
        at = order[i % groups] * (out.shape[1] // groups) + i // groups * width
        out[:, pl.ds(pl.multiple_of(at, width), width)] = total


def finish(sizes, place, parts, queries):
    rows = parts[0][0].shape[1]
    return pl.pallas_call(
        functools.partial(finish_kernel, sizes, tuple(map(len, parts))),
        out_shape=jax.ShapeDtypeStruct((rows, queries), F32),
        in_specs=[SMEM] * 3 + [VMEM] * sum(map(len, parts)),
        out_specs=VMEM,
        compiler_params=pltpu.CompilerParams(vmem_limit_bytes=12 * MIB),
        name="finish",
    )(*place, *[a for part in parts for a in part])


def shards(groups, ex, layers, queries, hessian, store):
    chips = ex // CORES
    sizes = groups, ex, layers
    total = queries.shape[0]
    place = [lax.axis_index(a).astype(jnp.int32)[None] for a in ("groups", "ex", "layer")]

    def permute(x, axis, perm, what):
        with jax.named_scope(what):
            return lax.ppermute(x, axis, perm)

    def from_chip(x, k, what):
        perm = [(e, (e - k * CORES) % ex) for e in range(ex)]
        return permute(x, "ex", perm, what + "_from_chip")

    def from_core(x, what):
        return permute(x, "ex", [(e, e ^ 1) for e in range(ex)], what + "_from_core")

    def from_group(x, j, what):
        perm = [(g, (g - j) % groups) for g in range(groups)]
        return permute(x, "groups", perm, what + "_from_group")

    def from_layer(x, r, what):
        return permute(x, "layer", [(z, z ^ r) for z in range(layers)], f"{what}_from_layer_{r}")

    def tie(x, *others):
        return lax.optimization_barrier((x, *others))[0]

    def gather_chip(x, what):
        return [from_chip(x, k, what) for k in range(1, chips)]

    def gather_group(x, what):
        return [from_group(x, j, what) for j in range(1, groups)]

    def with_cores(ours, theirs):
        return [x for pair in zip(ours, theirs) for x in pair]

    def flip(xs, what):
        return [from_core(x, what) for x in xs]

    def after(token, xs):
        return [tie(x, token) for x in xs]

    parts = []

    def advance(token, chain=False):
        for i, part in enumerate(parts):
            if part[0].shape[0] > 1:
                if chain and i and parts[i - 1][0].shape[0] == 1:
                    token = tie(token, parts[i - 1][1])
                send, keep = fold(part[0], part[1], token)
                step = layers // keep.shape[0] // 2
                part[:] = keep, from_layer(send, step, f"sum{i}")

    def send_parts(made):
        first = len(parts)
        advance(made[-1][1])
        for send, keep in made:
            parts.append([keep, from_layer(send, 1, f"sum{len(parts)}")])
        return parts[first - 1][0] if first else made[-1][1]

    rows = pltpu.with_memory_space_constraint(store[:, 0, :], pltpu.VMEM)
    width = total // groups // CHUNKS
    q0 = take(0, place, queries[:, 0, :], place[0], width)
    q0_there, q0_core = gather_chip(q0, "q0"), from_core(q0, "q0")
    hess = load(hessian[0], q0)
    q1 = take(1, place, queries[:, 0, :], hess, width)
    q0_there = after(q1, q0_there)
    q0_cores = [q0_core] + flip(q0_there, "q0_there")
    q1_there, q1_core = gather_chip(q1, "q1"), from_core(q1, "q1")
    s0 = condition(sizes, place, hess, with_cores([q0] + q0_there, q0_cores), q1)
    s0_there, s0_across, s0_core = gather_chip(s0, "s0"), gather_group(s0, "s0"), from_core(s0, "s0")
    q1_there = after(s0, q1_there)
    q1_cores = [q1_core] + flip(q1_there, "q1_there")
    s0_diagonal = [gather_group(x, "s0_there") for x in s0_there]
    s0_cores = [s0_core] + flip(s0_there, "s0_there")
    s1 = condition(sizes, place, hess, with_cores([q1] + q1_there, q1_cores), s0_there[-1])
    s1_there, s1_core = gather_chip(s1, "s1"), from_core(s1, "s1")
    s0_across = after(s1, s0_across)
    s0_across_cores = flip(s0_across, "s0_across")
    last = send_parts(score("score0", sizes, place, rows, [with_cores([s0] + s0_there, s0_cores)], s1))
    s0_diagonal = [after(last, xs) for xs in s0_diagonal]
    s0_diagonal_cores = [flip(xs, "s0_diagonal") for xs in s0_diagonal]
    s1_across = gather_group(s1, "s1")
    s1_there = after(last, s1_there)
    s1_across = after(last, s1_across)
    s1_across_cores = flip(s1_across, "s1_across")
    s1_diagonal = [gather_group(x, "s1_there") for x in s1_there]
    s1_cores = [s1_core] + flip(s1_there, "s1_there")
    for j in range(groups - 1):
        ours = [s0_across[j]] + [xs[j] for xs in s0_diagonal]
        theirs = [s0_across_cores[j]] + [xs[j] for xs in s0_diagonal_cores]
        last = send_parts(score("score1", sizes, place, rows, [with_cores(ours, theirs)], tie(last, *s1_across)))
    s1_diagonal = [after(last, xs) for xs in s1_diagonal]
    s1_diagonal_cores = [flip(xs, "s1_diagonal") for xs in s1_diagonal]
    pieces = [with_cores([s1] + s1_there, s1_cores)]
    for j in range(groups - 1):
        ours = [s1_across[j]] + [xs[j] for xs in s1_diagonal]
        theirs = [s1_across_cores[j]] + [xs[j] for xs in s1_diagonal_cores]
        pieces.append(with_cores(ours, theirs))
    last = send_parts(score("score2", sizes, place, rows, pieces, last))
    while any(part[0].shape[0] > 1 for part in parts):
        advance(last)
    return finish(sizes, place, parts, total)


def solution(mesh):
    groups, ex, layers = (mesh.shape[a] for a in ("groups", "ex", "layer"))
    in_specs = (P(None, "layer", "ex"), P("layer", "ex", None), P(("groups", "ex"), "layer", None))
    out_specs = P(("groups", "ex", "layer"), None)
    return jax.shard_map(
        functools.partial(shards, groups, ex, layers),
        mesh=mesh,
        in_specs=in_specs,
        out_specs=out_specs,
        check_vma=False,
    )
```

```python
import functools

import jax
import jax.numpy as jnp
from jax import lax
from jax.experimental import pallas as pl
from jax.experimental.pallas import tpu as pltpu
from jax.sharding import PartitionSpec as P

F32, BF16 = jnp.float32, jnp.bfloat16
CORES = 2
CHUNKS = 2
MIB = 1 << 20
VMEM = pl.BlockSpec(memory_space=pltpu.VMEM)
SMEM = pl.BlockSpec(memory_space=pltpu.SMEM)
ANY = pl.BlockSpec(memory_space=pl.ANY)


HBM = pl.BlockSpec(memory_space=pltpu.HBM)


def positions(groups, ex, layers, place):
    at_group, at_ex, at_layer = (ref[0] for ref in place)
    chips = ex // CORES
    chip, core = at_ex // CORES, lax.rem(at_ex, CORES)
    ids = [lax.rem(chip + k, chips) * CORES + (core ^ s) for k in range(chips) for s in range(CORES)]
    blocks = [at_layer ^ r for r in range(layers)]
    return ids, blocks, [lax.rem(at_group + j, groups) for j in range(groups)]


def load_kernel(source, after, out, sem):
    copy = pltpu.make_async_copy(source, out, sem)
    copy.start()
    copy.wait()


def load(source, after):
    return pl.pallas_call(
        load_kernel,
        out_shape=pltpu.VMEM(source.shape, BF16),
        in_specs=[HBM, ANY],
        out_specs=VMEM,
        scratch_shapes=[pltpu.SemaphoreType.DMA],
        compiler_params=pltpu.CompilerParams(vmem_limit_bytes=2 * MIB),
        name="load",
    )(pltpu.with_memory_space_constraint(source, pltpu.HBM), after)


def take_kernel(chunk, at_group, at_ex, at_layer, source, after, out, sem):
    rows = out.shape[0]
    at = pl.multiple_of((at_group[0] * CHUNKS + chunk) * rows, rows)
    copy = pltpu.make_async_copy(source.at[pl.ds(at, rows), :], out, sem)
    copy.start()
    copy.wait()


def take(chunk, place, source, after, rows):
    return pl.pallas_call(
        functools.partial(take_kernel, chunk),
        out_shape=pltpu.VMEM((rows, source.shape[1]), BF16),
        in_specs=[SMEM] * 3 + [HBM, ANY],
        out_specs=VMEM,
        scratch_shapes=[pltpu.SemaphoreType.DMA],
        compiler_params=pltpu.CompilerParams(vmem_limit_bytes=2 * MIB),
        name="take",
    )(*place, pltpu.with_memory_space_constraint(source, pltpu.HBM), after)


def condition_kernel(sizes, *refs):
    place, (hess, *rest) = refs[:3], refs[3:]
    ids, _, _ = positions(*sizes, place)
    pieces, (_, *outs, right) = rest[: len(ids)], rest[len(ids) :]
    width = pieces[0].shape[1]
    for t, piece in zip(ids, pieces):
        right[:, pl.ds(pl.multiple_of(t * width, width), width)] = piece[...]
    height = hess.shape[0]
    outs[0][...] = lax.dot_general(
        hess[...], right[...], (((1,), (1,)), ((), ())), preferred_element_type=F32
    ).astype(BF16)
    for out in outs[1:]:
        out[:height, :] = outs[0][...]
        out[height:, :] = jnp.zeros((out.shape[0] - height, out.shape[1]), BF16)


def condition(sizes, place, hess, pieces, after, more):
    rows, queries = hess.shape[0], pieces[0].shape[0]
    shapes = [(rows + count, queries) for count in (0, *more)]
    return pl.pallas_call(
        functools.partial(condition_kernel, sizes),
        out_shape=[pltpu.VMEM(shape, BF16) for shape in shapes],
        in_specs=[SMEM] * 3 + [VMEM] * (1 + len(pieces)) + [ANY],
        out_specs=[VMEM] * len(shapes),
        scratch_shapes=[pltpu.VMEM((queries, hess.shape[1]), BF16)],
        compiler_params=pltpu.CompilerParams(vmem_limit_bytes=12 * MIB),
        name="condition",
    )(*place, hess, *pieces, after)


def score_kernel(sizes, columns, direct, *refs):
    place, (store, *rest) = refs[:3], refs[3:]
    ids, blocks, _ = positions(*sizes, place)
    layers, count = len(blocks), len(ids)
    pieces, (_, *outs, right) = rest[: columns * count], rest[columns * count :]
    rows = store.shape[0] // layers
    depth, width = store.shape[1] // count, pieces[0].shape[1]
    for i, piece in enumerate(pieces):
        at = pl.ds(pl.multiple_of(ids[i % count] * depth, depth), depth)
        right[at, i // count * width : (i // count + 1) * width] = piece[:depth, :]
    for r in reversed(range(layers)) if direct else [*range(1, layers, 2), *range(0, layers, 2)]:
        at = pl.ds(pl.multiple_of(blocks[r] * rows, rows), rows)
        part = jnp.dot(store[at, :], right[...], preferred_element_type=F32)
        if direct:
            outs[r][0] = part.astype(outs[r].dtype)
            continue
        for c in range(columns):
            out = outs[2 * c + 1 - r % 2]
            out[r // 2] = part[:, c * width : (c + 1) * width].astype(out.dtype)


def score(name, sizes, place, store, pieces, after, direct=False):
    width = pieces[0][0].shape[1]
    layers, columns = sizes[2], len(pieces)
    rows = store.shape[0] // layers
    shapes = [((layers // 2, rows, width), t) for t in (BF16, F32)] * columns
    if direct:
        shapes = [((1, rows, columns * width), BF16 if r else F32) for r in range(layers)]
    flat = [x for xs in pieces for x in xs]
    made = pl.pallas_call(
        functools.partial(score_kernel, sizes, columns, direct),
        out_shape=[pltpu.VMEM(*shape) for shape in shapes],
        in_specs=[SMEM] * 3 + [VMEM] * (1 + len(flat)) + [ANY],
        out_specs=[VMEM] * len(shapes),
        scratch_shapes=[pltpu.VMEM((store.shape[1], columns * width), BF16)],
        compiler_params=pltpu.CompilerParams(vmem_limit_bytes=12 * MIB),
        name=name,
    )(*place, store, *flat, after)
    return made if direct else [made[2 * c : 2 * c + 2] for c in range(columns)]


def fold_kernel(keep, got, _, send, left):
    for r in range(keep.shape[0]):
        total = keep[r] + got[r].astype(F32)
        if r % 2:
            send[r // 2] = total.astype(BF16)
        else:
            left[r // 2] = total


def fold(keep, got, after):
    shape = (keep.shape[0] // 2,) + keep.shape[1:]
    return pl.pallas_call(
        fold_kernel,
        out_shape=(pltpu.VMEM(shape, BF16), pltpu.VMEM(shape, F32)),
        in_specs=[VMEM, VMEM, ANY],
        out_specs=(VMEM, VMEM),
        compiler_params=pltpu.CompilerParams(vmem_limit_bytes=4 * MIB),
        name="fold",
    )(keep, got, after)


def finish_kernel(sizes, counts, *refs):
    place, (*refs, out) = refs[:3], refs[3:]
    _, _, order = positions(*sizes, place)
    groups = len(order)
    span = out.shape[1] // groups
    width = span // CHUNKS
    i = 0
    for count in counts:
        (keep, *rest), refs = refs[:count], refs[count:]
        total = keep[0]
        for got in rest:
            total = total + got[0].astype(F32)
        for low in range(0, total.shape[1], width):
            at = order[i % groups] * span + i // groups * width
            out[:, pl.ds(pl.multiple_of(at, width), width)] = total[:, low : low + width]
            i += 1


def finish(sizes, place, parts, queries):
    rows = parts[0][0].shape[1]
    return pl.pallas_call(
        functools.partial(finish_kernel, sizes, tuple(map(len, parts))),
        out_shape=jax.ShapeDtypeStruct((rows, queries), F32),
        in_specs=[SMEM] * 3 + [VMEM] * sum(map(len, parts)),
        out_specs=VMEM,
        compiler_params=pltpu.CompilerParams(vmem_limit_bytes=12 * MIB),
        name="finish",
    )(*place, *[a for part in parts for a in part])


def shards(groups, ex, layers, queries, hessian, store):
    chips = ex // CORES
    sizes = groups, ex, layers
    total = queries.shape[0]
    place = [lax.axis_index(a).astype(jnp.int32)[None] for a in ("groups", "ex", "layer")]

    def permute(x, axis, perm, what):
        with jax.named_scope(what):
            return lax.ppermute(x, axis, perm)

    def from_chip(x, k, what):
        perm = [(e, (e - k * CORES) % ex) for e in range(ex)]
        return permute(x, "ex", perm, what + "_from_chip")

    def from_core(x, what):
        return permute(x, "ex", [(e, e ^ 1) for e in range(ex)], what + "_from_core")

    def from_group(x, j, what):
        perm = [(g, (g - j) % groups) for g in range(groups)]
        return permute(x, "groups", perm, what + "_from_group")

    def from_layer(x, r, what):
        return permute(x, "layer", [(z, z ^ r) for z in range(layers)], f"{what}_from_layer_{r}")

    def tie(x, *others):
        return lax.optimization_barrier((x, *others))[0]

    def gather_chip(x, what):
        return [from_chip(x, k, what) for k in range(1, chips)]

    def gather_group(x, what):
        return [from_group(x, j, what) for j in range(1, groups)]

    def with_cores(ours, theirs):
        return [x for pair in zip(ours, theirs) for x in pair]

    def flip(xs, what):
        return [from_core(x, what) for x in xs]

    def after(token, xs):
        return [tie(x, token) for x in xs]

    parts = []

    def advance(token, chain=False):
        for i, part in enumerate(parts):
            if part[0].shape[0] > 1:
                if chain and i and parts[i - 1][0].shape[0] == 1:
                    token = tie(token, parts[i - 1][1])
                send, keep = fold(part[0], part[1], token)
                step = layers // keep.shape[0] // 2
                part[:] = keep, from_layer(send, step, f"sum{i}")

    def send_parts(made):
        first = len(parts)
        advance(made[-1][1])
        for send, keep in made:
            parts.append([keep, from_layer(send, 1, f"sum{len(parts)}")])
        return parts[first - 1][0] if first else made[-1][1]

    rows = pltpu.with_memory_space_constraint(store[:, 0, :], pltpu.VMEM)
    width = total // groups // CHUNKS
    q0 = take(0, place, queries[:, 0, :], place[0], width)
    q0_there, q0_core = gather_chip(q0, "q0"), from_core(q0, "q0")
    hess = load(hessian[0], q0)
    q1 = take(1, place, queries[:, 0, :], hess, width)
    q0_there = after(q1, q0_there)
    q0_cores = [q0_core] + flip(q0_there, "q0_there")
    q1_there, q1_core = gather_chip(q1, "q1"), from_core(q1, "q1")
    s0, s0_long, s0_longer = condition(sizes, place, hess, with_cores([q0] + q0_there, q0_cores), q1, (16, 16))
    s0_there, s0_across, s0_core = gather_chip(s0_long, "s0"), gather_group(s0_longer, "s0"), from_core(s0, "s0")
    q1_there = after(s0, q1_there)
    q1_cores = [q1_core] + flip(q1_there, "q1_there")
    s1, s1_long = condition(sizes, place, hess, with_cores([q1] + q1_there, q1_cores), s0, (16,))
    s1_there, s1_core = gather_chip(s1, "s1"), from_core(s1, "s1")
    s0_there, s0_across = after(s1, s0_there), after(s1, s0_across)
    s0_diagonal = [gather_group(x, "s0_there") for x in s0_there]
    s0_cores = [s0_core] + flip(s0_there, "s0_there")
    s0_across_cores = flip(s0_across, "s0_across")
    last = send_parts(score("score0", sizes, place, rows, [with_cores([s0] + s0_there, s0_cores)], s1))
    s0_diagonal = [after(last, xs) for xs in s0_diagonal]
    s0_diagonal_cores = [flip(xs, "s0_diagonal") for xs in s0_diagonal]
    s1_across = gather_group(s1_long, "s1")
    s1_there = after(last, s1_there)
    s1_across = after(last, s1_across)
    s1_across_cores = flip(s1_across, "s1_across")
    s1_diagonal = [gather_group(x, "s1_there") for x in s1_there]
    s1_cores = [s1_core] + flip(s1_there, "s1_there")
    for j in range(groups - 1):
        ours = [s0_across[j]] + [xs[j] for xs in s0_diagonal]
        theirs = [s0_across_cores[j]] + [xs[j] for xs in s0_diagonal_cores]
        last = send_parts(score("score1", sizes, place, rows, [with_cores(ours, theirs)], tie(last, *s1_across)))
    s1_diagonal = [after(last, xs) for xs in s1_diagonal]
    s1_diagonal_cores = [flip(xs, "s1_diagonal") for xs in s1_diagonal]
    pieces = [with_cores([s1] + s1_there, s1_cores)]
    for j in range(groups - 1):
        ours = [s1_across[j]] + [xs[j] for xs in s1_diagonal]
        theirs = [s1_across_cores[j]] + [xs[j] for xs in s1_diagonal_cores]
        pieces.append(with_cores(ours, theirs))
    last = send_parts(score("score2", sizes, place, rows, pieces, last))
    while any(part[0].shape[0] > 1 for part in parts):
        advance(last)
    return finish(sizes, place, parts, total)


def solution(mesh):
    groups, ex, layers = (mesh.shape[a] for a in ("groups", "ex", "layer"))
    in_specs = (P(None, "layer", "ex"), P("layer", "ex", None), P(("groups", "ex"), "layer", None))
    out_specs = P(("groups", "ex", "layer"), None)
    return jax.shard_map(
        functools.partial(shards, groups, ex, layers),
        mesh=mesh,
        in_specs=in_specs,
        out_specs=out_specs,
        check_vma=False,
    )
```

```python
import functools

import jax
import jax.numpy as jnp
from jax import lax
from jax.experimental import pallas as pl
from jax.experimental.pallas import tpu as pltpu
from jax.sharding import PartitionSpec as P

F32, BF16 = jnp.float32, jnp.bfloat16
CORES = 2
CHUNKS = 2
MIB = 1 << 20
VMEM = pl.BlockSpec(memory_space=pltpu.VMEM)
SMEM = pl.BlockSpec(memory_space=pltpu.SMEM)
ANY = pl.BlockSpec(memory_space=pl.ANY)


HBM = pl.BlockSpec(memory_space=pltpu.HBM)


def positions(groups, ex, layers, place):
    at_group, at_ex, at_layer = (ref[0] for ref in place)
    chips = ex // CORES
    chip, core = at_ex // CORES, lax.rem(at_ex, CORES)
    ids = [lax.rem(chip + k, chips) * CORES + (core ^ s) for k in range(chips) for s in range(CORES)]
    blocks = [at_layer ^ r for r in range(layers)]
    return ids, blocks, [lax.rem(at_group + j, groups) for j in range(groups)]


def load_kernel(source, after, out, sem):
    copy = pltpu.make_async_copy(source, out, sem)
    copy.start()
    copy.wait()


def load(source, after):
    return pl.pallas_call(
        load_kernel,
        out_shape=pltpu.VMEM(source.shape, BF16),
        in_specs=[HBM, ANY],
        out_specs=VMEM,
        scratch_shapes=[pltpu.SemaphoreType.DMA],
        compiler_params=pltpu.CompilerParams(vmem_limit_bytes=2 * MIB),
        name="load",
    )(pltpu.with_memory_space_constraint(source, pltpu.HBM), after)


def take_kernel(chunk, at_group, at_ex, at_layer, source, after, out, sem):
    rows = out.shape[0]
    at = pl.multiple_of((at_group[0] * CHUNKS + chunk) * rows, rows)
    copy = pltpu.make_async_copy(source.at[pl.ds(at, rows), :], out, sem)
    copy.start()
    copy.wait()


def take(chunk, place, source, after, rows):
    return pl.pallas_call(
        functools.partial(take_kernel, chunk),
        out_shape=pltpu.VMEM((rows, source.shape[1]), BF16),
        in_specs=[SMEM] * 3 + [HBM, ANY],
        out_specs=VMEM,
        scratch_shapes=[pltpu.SemaphoreType.DMA],
        compiler_params=pltpu.CompilerParams(vmem_limit_bytes=2 * MIB),
        name="take",
    )(*place, pltpu.with_memory_space_constraint(source, pltpu.HBM), after)


def condition_kernel(sizes, *refs):
    place, (hess, *rest) = refs[:3], refs[3:]
    ids, _, _ = positions(*sizes, place)
    pieces, (_, *outs, right) = rest[: len(ids)], rest[len(ids) :]
    width = pieces[0].shape[1]
    for t, piece in zip(ids, pieces):
        right[:, pl.ds(pl.multiple_of(t * width, width), width)] = piece[...]
    height = hess.shape[0]
    outs[0][...] = lax.dot_general(
        hess[...], right[...], (((1,), (1,)), ((), ())), preferred_element_type=F32
    ).astype(BF16)
    for out in outs[1:]:
        out[:height, :] = outs[0][...]
        out[height:, :] = jnp.zeros((out.shape[0] - height, out.shape[1]), BF16)


def condition(sizes, place, hess, pieces, after, more):
    rows, queries = hess.shape[0], pieces[0].shape[0]
    shapes = [(rows + count, queries) for count in (0, *more)]
    return pl.pallas_call(
        functools.partial(condition_kernel, sizes),
        out_shape=[pltpu.VMEM(shape, BF16) for shape in shapes],
        in_specs=[SMEM] * 3 + [VMEM] * (1 + len(pieces)) + [ANY],
        out_specs=[VMEM] * len(shapes),
        scratch_shapes=[pltpu.VMEM((queries, hess.shape[1]), BF16)],
        compiler_params=pltpu.CompilerParams(vmem_limit_bytes=12 * MIB),
        name="condition",
    )(*place, hess, *pieces, after)


def score_kernel(sizes, columns, direct, *refs):
    place, (store, *rest) = refs[:3], refs[3:]
    ids, blocks, _ = positions(*sizes, place)
    layers, count = len(blocks), len(ids)
    pieces, (_, *outs, right) = rest[: columns * count], rest[columns * count :]
    rows = store.shape[0] // layers
    depth, width = store.shape[1] // count, pieces[0].shape[1]
    for i, piece in enumerate(pieces):
        at = pl.ds(pl.multiple_of(ids[i % count] * depth, depth), depth)
        right[at, i // count * width : (i // count + 1) * width] = piece[:depth, :]
    for r in reversed(range(layers)) if direct else [*range(1, layers, 2), *range(0, layers, 2)]:
        at = pl.ds(pl.multiple_of(blocks[r] * rows, rows), rows)
        part = jnp.dot(store[at, :], right[...], preferred_element_type=F32)
        if direct:
            outs[r][0] = part.astype(outs[r].dtype)
            continue
        for c in range(columns):
            out = outs[2 * c + 1 - r % 2]
            out[r // 2] = part[:, c * width : (c + 1) * width].astype(out.dtype)


def score(name, sizes, place, store, pieces, after, direct=False):
    width = pieces[0][0].shape[1]
    layers, columns = sizes[2], len(pieces)
    rows = store.shape[0] // layers
    shapes = [((layers // 2, rows, width), t) for t in (BF16, F32)] * columns
    if direct:
        shapes = [((1, rows, columns * width), BF16 if r else F32) for r in range(layers)]
    flat = [x for xs in pieces for x in xs]
    made = pl.pallas_call(
        functools.partial(score_kernel, sizes, columns, direct),
        out_shape=[pltpu.VMEM(*shape) for shape in shapes],
        in_specs=[SMEM] * 3 + [VMEM] * (1 + len(flat)) + [ANY],
        out_specs=[VMEM] * len(shapes),
        scratch_shapes=[pltpu.VMEM((store.shape[1], columns * width), BF16)],
        compiler_params=pltpu.CompilerParams(vmem_limit_bytes=12 * MIB),
        name=name,
    )(*place, store, *flat, after)
    return made if direct else [made[2 * c : 2 * c + 2] for c in range(columns)]


def fold_kernel(keep, got, _, send, left):
    for r in range(keep.shape[0]):
        total = keep[r] + got[r].astype(F32)
        if r % 2:
            send[r // 2] = total.astype(BF16)
        else:
            left[r // 2] = total


def fold(keep, got, after):
    shape = (keep.shape[0] // 2,) + keep.shape[1:]
    return pl.pallas_call(
        fold_kernel,
        out_shape=(pltpu.VMEM(shape, BF16), pltpu.VMEM(shape, F32)),
        in_specs=[VMEM, VMEM, ANY],
        out_specs=(VMEM, VMEM),
        compiler_params=pltpu.CompilerParams(vmem_limit_bytes=4 * MIB),
        name="fold",
    )(keep, got, after)


def finish_kernel(sizes, counts, *refs):
    place, (*refs, out) = refs[:3], refs[3:]
    _, _, order = positions(*sizes, place)
    groups = len(order)
    span = out.shape[1] // groups
    width = span // CHUNKS
    i = 0
    for count in counts:
        (keep, *rest), refs = refs[:count], refs[count:]
        total = keep[0]
        for got in rest:
            total = total + got[0].astype(F32)
        for low in range(0, total.shape[1], width):
            at = order[i % groups] * span + i // groups * width
            out[:, pl.ds(pl.multiple_of(at, width), width)] = total[:, low : low + width]
            i += 1


def finish(sizes, place, parts, queries):
    rows = parts[0][0].shape[1]
    return pl.pallas_call(
        functools.partial(finish_kernel, sizes, tuple(map(len, parts))),
        out_shape=jax.ShapeDtypeStruct((rows, queries), F32),
        in_specs=[SMEM] * 3 + [VMEM] * sum(map(len, parts)),
        out_specs=VMEM,
        compiler_params=pltpu.CompilerParams(vmem_limit_bytes=12 * MIB),
        name="finish",
    )(*place, *[a for part in parts for a in part])


def shards(groups, ex, layers, queries, hessian, store):
    chips = ex // CORES
    sizes = groups, ex, layers
    total = queries.shape[0]
    place = [lax.axis_index(a).astype(jnp.int32)[None] for a in ("groups", "ex", "layer")]

    def permute(x, axis, perm, what):
        with jax.named_scope(what):
            return lax.ppermute(x, axis, perm)

    def from_chip(x, k, what):
        perm = [(e, (e - k * CORES) % ex) for e in range(ex)]
        return permute(x, "ex", perm, what + "_from_chip")

    def from_core(x, what):
        return permute(x, "ex", [(e, e ^ 1) for e in range(ex)], what + "_from_core")

    def from_group(x, j, what):
        perm = [(g, (g - j) % groups) for g in range(groups)]
        return permute(x, "groups", perm, what + "_from_group")

    def from_layer(x, r, what):
        return permute(x, "layer", [(z, z ^ r) for z in range(layers)], f"{what}_from_layer_{r}")

    def tie(x, *others):
        return lax.optimization_barrier((x, *others))[0]

    def gather_chip(x, what):
        return [from_chip(x, k, what) for k in range(1, chips)]

    def gather_group(x, what):
        return [from_group(x, j, what) for j in range(1, groups)]

    def with_cores(ours, theirs):
        return [x for pair in zip(ours, theirs) for x in pair]

    def flip(xs, what):
        return [from_core(x, what) for x in xs]

    def after(token, xs):
        return [tie(x, token) for x in xs]

    parts = []

    def advance(token, chain=False):
        for i, part in enumerate(parts):
            if part[0].shape[0] > 1:
                if chain and i and parts[i - 1][0].shape[0] == 1:
                    token = tie(token, parts[i - 1][1])
                send, keep = fold(part[0], part[1], token)
                step = layers // keep.shape[0] // 2
                part[:] = keep, from_layer(send, step, f"sum{i}")

    def send_parts(made):
        first = len(parts)
        advance(made[-1][1])
        for send, keep in made:
            parts.append([keep, from_layer(send, 1, f"sum{len(parts)}")])
        return parts[first - 1][0] if first else made[-1][1]

    rows = pltpu.with_memory_space_constraint(store[:, 0, :], pltpu.VMEM)
    width = total // groups // CHUNKS
    q0 = take(0, place, queries[:, 0, :], place[0], width)
    q0_there, q0_core = gather_chip(q0, "q0"), from_core(q0, "q0")
    hess = load(hessian[0], q0)
    q1 = take(1, place, queries[:, 0, :], hess, width)
    q0_there = after(q1, q0_there)
    q0_cores = [q0_core] + flip(q0_there, "q0_there")
    q1_there, q1_core = gather_chip(q1, "q1"), from_core(q1, "q1")
    s0, s0_long, s0_longer = condition(sizes, place, hess, with_cores([q0] + q0_there, q0_cores), q1, (16, 16))
    s0_there, s0_across, s0_core = gather_chip(s0_long, "s0"), gather_group(s0_longer, "s0"), from_core(s0, "s0")
    q1_there = after(s0, q1_there)
    q1_cores = [q1_core] + flip(q1_there, "q1_there")
    s1, s1_long = condition(sizes, place, hess, with_cores([q1] + q1_there, q1_cores), s0, (16,))
    s1_there, s1_core = gather_chip(s1, "s1"), from_core(s1, "s1")
    s0_there, s0_across = after(s1, s0_there), after(s1, s0_across)
    s0_diagonal = [gather_group(x, "s0_there") for x in s0_there]
    s0_cores = [s0_core] + flip(s0_there, "s0_there")
    s0_across_cores = flip(s0_across, "s0_across")
    last = send_parts(score("score0", sizes, place, rows, [with_cores([s0] + s0_there, s0_cores)], s1))
    s0_diagonal = [after(last, xs) for xs in s0_diagonal]
    s0_diagonal_cores = [flip(xs, "s0_diagonal") for xs in s0_diagonal]
    s1_across = gather_group(s1_long, "s1")
    s1_there = after(last, s1_there)
    s1_across = after(last, s1_across)
    s1_across_cores = flip(s1_across, "s1_across")
    s1_diagonal = [gather_group(x, "s1_there") for x in s1_there]
    s1_cores = [s1_core] + flip(s1_there, "s1_there")
    pieces = []
    for j in range(groups - 1):
        ours = [s0_across[j]] + [xs[j] for xs in s0_diagonal]
        theirs = [s0_across_cores[j]] + [xs[j] for xs in s0_diagonal_cores]
        pieces.append(with_cores(ours, theirs))
    pieces.append(with_cores([s1] + s1_there, s1_cores))
    last = send_parts(score("score1", sizes, place, rows, pieces, last))
    s1_across = after(last, s1_across)
    s1_across_cores = flip(s1_across, "s1_across")
    s1_diagonal = [after(last, xs) for xs in s1_diagonal]
    s1_diagonal_cores = [flip(xs, "s1_diagonal") for xs in s1_diagonal]
    pieces = []
    for j in range(groups - 1):
        ours = [s1_across[j]] + [xs[j] for xs in s1_diagonal]
        theirs = [s1_across_cores[j]] + [xs[j] for xs in s1_diagonal_cores]
        pieces.append(with_cores(ours, theirs))
    last = send_parts(score("score2", sizes, place, rows, pieces, last))
    while any(part[0].shape[0] > 1 for part in parts):
        advance(last)
    return finish(sizes, place, parts, total)


def solution(mesh):
    groups, ex, layers = (mesh.shape[a] for a in ("groups", "ex", "layer"))
    in_specs = (P(None, "layer", "ex"), P("layer", "ex", None), P(("groups", "ex"), "layer", None))
    out_specs = P(("groups", "ex", "layer"), None)
    return jax.shard_map(
        functools.partial(shards, groups, ex, layers),
        mesh=mesh,
        in_specs=in_specs,
        out_specs=out_specs,
        check_vma=False,
    )
```

```python
import functools

import jax
import jax.numpy as jnp
from jax import lax
from jax.experimental import pallas as pl
from jax.experimental.pallas import tpu as pltpu
from jax.sharding import PartitionSpec as P

F32, BF16 = jnp.float32, jnp.bfloat16
CORES = 2
CHUNKS = 2
MIB = 1 << 20
VMEM = pl.BlockSpec(memory_space=pltpu.VMEM)
SMEM = pl.BlockSpec(memory_space=pltpu.SMEM)
ANY = pl.BlockSpec(memory_space=pl.ANY)


HBM = pl.BlockSpec(memory_space=pltpu.HBM)


def positions(groups, ex, layers, place):
    at_group, at_ex, at_layer = (ref[0] for ref in place)
    chips = ex // CORES
    chip, core = at_ex // CORES, lax.rem(at_ex, CORES)
    ids = [lax.rem(chip + k, chips) * CORES + (core ^ s) for k in range(chips) for s in range(CORES)]
    blocks = [at_layer ^ r for r in range(layers)]
    return ids, blocks, [lax.rem(at_group + j, groups) for j in range(groups)]


def load_kernel(source, after, out, sem):
    copy = pltpu.make_async_copy(source, out, sem)
    copy.start()
    copy.wait()


def load(source, after):
    return pl.pallas_call(
        load_kernel,
        out_shape=pltpu.VMEM(source.shape, BF16),
        in_specs=[HBM, ANY],
        out_specs=VMEM,
        scratch_shapes=[pltpu.SemaphoreType.DMA],
        compiler_params=pltpu.CompilerParams(vmem_limit_bytes=2 * MIB),
        name="load",
    )(pltpu.with_memory_space_constraint(source, pltpu.HBM), after)


def take_kernel(chunk, at_group, at_ex, at_layer, source, after, out, sem):
    rows = out.shape[0]
    at = pl.multiple_of((at_group[0] * CHUNKS + chunk) * rows, rows)
    copy = pltpu.make_async_copy(source.at[pl.ds(at, rows), :], out, sem)
    copy.start()
    copy.wait()


def take(chunk, place, source, after, rows):
    return pl.pallas_call(
        functools.partial(take_kernel, chunk),
        out_shape=pltpu.VMEM((rows, source.shape[1]), BF16),
        in_specs=[SMEM] * 3 + [HBM, ANY],
        out_specs=VMEM,
        scratch_shapes=[pltpu.SemaphoreType.DMA],
        compiler_params=pltpu.CompilerParams(vmem_limit_bytes=2 * MIB),
        name="take",
    )(*place, pltpu.with_memory_space_constraint(source, pltpu.HBM), after)


def condition_kernel(sizes, *refs):
    place, (hess, *rest) = refs[:3], refs[3:]
    ids, _, _ = positions(*sizes, place)
    pieces, (_, *outs, right) = rest[: len(ids)], rest[len(ids) :]
    width = pieces[0].shape[1]
    for t, piece in zip(ids, pieces):
        right[:, pl.ds(pl.multiple_of(t * width, width), width)] = piece[...]
    height = hess.shape[0]
    outs[0][...] = lax.dot_general(
        hess[...], right[...], (((1,), (1,)), ((), ())), preferred_element_type=F32
    ).astype(BF16)
    for out in outs[1:]:
        out[:height, :] = outs[0][...]
        out[height:, :] = jnp.zeros((out.shape[0] - height, out.shape[1]), BF16)


def condition(sizes, place, hess, pieces, after, more):
    rows, queries = hess.shape[0], pieces[0].shape[0]
    shapes = [(rows + count, queries) for count in (0, *more)]
    return pl.pallas_call(
        functools.partial(condition_kernel, sizes),
        out_shape=[pltpu.VMEM(shape, BF16) for shape in shapes],
        in_specs=[SMEM] * 3 + [VMEM] * (1 + len(pieces)) + [ANY],
        out_specs=[VMEM] * len(shapes),
        scratch_shapes=[pltpu.VMEM((queries, hess.shape[1]), BF16)],
        compiler_params=pltpu.CompilerParams(vmem_limit_bytes=12 * MIB),
        name="condition",
    )(*place, hess, *pieces, after)


def score_kernel(sizes, columns, direct, *refs):
    place, (store, *rest) = refs[:3], refs[3:]
    ids, blocks, _ = positions(*sizes, place)
    layers, count = len(blocks), len(ids)
    pieces, (_, *outs, right, total) = rest[: columns * count], rest[columns * count :]
    rows = store.shape[0] // layers
    depth, width = store.shape[1] // count, pieces[0].shape[1]
    for i, piece in enumerate(pieces):
        at = pl.ds(pl.multiple_of(ids[i % count] * depth, depth), depth)
        right[at, i // count * width : (i // count + 1) * width] = piece[:depth, :]
    total[...] = jnp.dot(store[...], right[...], preferred_element_type=F32)
    for r in range(layers):
        part = total[pl.ds(pl.multiple_of(blocks[r] * rows, rows), rows), :]
        if direct:
            outs[r][0] = part.astype(outs[r].dtype)
            continue
        for c in range(columns):
            out = outs[2 * c + 1 - r % 2]
            out[r // 2] = part[:, c * width : (c + 1) * width].astype(out.dtype)


def score(name, sizes, place, store, pieces, after, direct=False):
    width = pieces[0][0].shape[1]
    layers, columns = sizes[2], len(pieces)
    rows = store.shape[0] // layers
    shapes = [((layers // 2, rows, width), t) for t in (BF16, F32)] * columns
    if direct:
        shapes = [((1, rows, columns * width), BF16 if r else F32) for r in range(layers)]
    flat = [x for xs in pieces for x in xs]
    made = pl.pallas_call(
        functools.partial(score_kernel, sizes, columns, direct),
        out_shape=[pltpu.VMEM(*shape) for shape in shapes],
        in_specs=[SMEM] * 3 + [VMEM] * (1 + len(flat)) + [ANY],
        out_specs=[VMEM] * len(shapes),
        scratch_shapes=[
            pltpu.VMEM((store.shape[1], columns * width), BF16),
            pltpu.VMEM((store.shape[0], columns * width), F32),
        ],
        compiler_params=pltpu.CompilerParams(vmem_limit_bytes=12 * MIB),
        name=name,
    )(*place, store, *flat, after)
    return made if direct else [made[2 * c : 2 * c + 2] for c in range(columns)]


def fold_kernel(keep, got, _, send, left):
    for r in range(keep.shape[0]):
        total = keep[r] + got[r].astype(F32)
        if r % 2:
            send[r // 2] = total.astype(BF16)
        else:
            left[r // 2] = total


def fold(keep, got, after):
    shape = (keep.shape[0] // 2,) + keep.shape[1:]
    return pl.pallas_call(
        fold_kernel,
        out_shape=(pltpu.VMEM(shape, BF16), pltpu.VMEM(shape, F32)),
        in_specs=[VMEM, VMEM, ANY],
        out_specs=(VMEM, VMEM),
        compiler_params=pltpu.CompilerParams(vmem_limit_bytes=4 * MIB),
        name="fold",
    )(keep, got, after)


def finish_kernel(sizes, counts, *refs):
    place, (*refs, out) = refs[:3], refs[3:]
    _, _, order = positions(*sizes, place)
    groups = len(order)
    span = out.shape[1] // groups
    width = span // CHUNKS
    i = 0
    for count in counts:
        (keep, *rest), refs = refs[:count], refs[count:]
        total = keep[0]
        for got in rest:
            total = total + got[0].astype(F32)
        for low in range(0, total.shape[1], width):
            at = order[i % groups] * span + i // groups * width
            out[:, pl.ds(pl.multiple_of(at, width), width)] = total[:, low : low + width]
            i += 1


def finish(sizes, place, parts, queries):
    rows = parts[0][0].shape[1]
    return pl.pallas_call(
        functools.partial(finish_kernel, sizes, tuple(map(len, parts))),
        out_shape=jax.ShapeDtypeStruct((rows, queries), F32),
        in_specs=[SMEM] * 3 + [VMEM] * sum(map(len, parts)),
        out_specs=VMEM,
        compiler_params=pltpu.CompilerParams(vmem_limit_bytes=12 * MIB),
        name="finish",
    )(*place, *[a for part in parts for a in part])


def shards(groups, ex, layers, queries, hessian, store):
    chips = ex // CORES
    sizes = groups, ex, layers
    total = queries.shape[0]
    place = [lax.axis_index(a).astype(jnp.int32)[None] for a in ("groups", "ex", "layer")]

    def permute(x, axis, perm, what):
        with jax.named_scope(what):
            return lax.ppermute(x, axis, perm)

    def from_chip(x, k, what):
        perm = [(e, (e - k * CORES) % ex) for e in range(ex)]
        return permute(x, "ex", perm, what + "_from_chip")

    def from_core(x, what):
        return permute(x, "ex", [(e, e ^ 1) for e in range(ex)], what + "_from_core")

    def from_group(x, j, what):
        perm = [(g, (g - j) % groups) for g in range(groups)]
        return permute(x, "groups", perm, what + "_from_group")

    def from_layer(x, r, what):
        return permute(x, "layer", [(z, z ^ r) for z in range(layers)], f"{what}_from_layer_{r}")

    def tie(x, *others):
        return lax.optimization_barrier((x, *others))[0]

    def gather_chip(x, what):
        return [from_chip(x, k, what) for k in range(1, chips)]

    def gather_group(x, what):
        return [from_group(x, j, what) for j in range(1, groups)]

    def with_cores(ours, theirs):
        return [x for pair in zip(ours, theirs) for x in pair]

    def flip(xs, what):
        return [from_core(x, what) for x in xs]

    def after(token, xs):
        return [tie(x, token) for x in xs]

    parts = []

    def advance(token, chain=False):
        for i, part in enumerate(parts):
            if part[0].shape[0] > 1:
                if chain and i and parts[i - 1][0].shape[0] == 1:
                    token = tie(token, parts[i - 1][1])
                send, keep = fold(part[0], part[1], token)
                step = layers // keep.shape[0] // 2
                part[:] = keep, from_layer(send, step, f"sum{i}")

    def send_parts(made):
        first = len(parts)
        advance(made[-1][1])
        for send, keep in made:
            parts.append([keep, from_layer(send, 1, f"sum{len(parts)}")])
        return parts[first - 1][0] if first else made[-1][1]

    rows = pltpu.with_memory_space_constraint(store[:, 0, :], pltpu.VMEM)
    width = total // groups // CHUNKS
    q0 = take(0, place, queries[:, 0, :], place[0], width)
    q0_there, q0_core = gather_chip(q0, "q0"), from_core(q0, "q0")
    hess = load(hessian[0], q0)
    q1 = take(1, place, queries[:, 0, :], hess, width)
    q0_there = after(q1, q0_there)
    q0_cores = [q0_core] + flip(q0_there, "q0_there")
    q1_there, q1_core = gather_chip(q1, "q1"), from_core(q1, "q1")
    s0, s0_long, s0_longer = condition(sizes, place, hess, with_cores([q0] + q0_there, q0_cores), q1, (16, 16))
    s0_there, s0_across, s0_core = gather_chip(s0_long, "s0"), gather_group(s0_longer, "s0"), from_core(s0, "s0")
    q1_there = after(s0, q1_there)
    q1_cores = [q1_core] + flip(q1_there, "q1_there")
    s1, s1_long = condition(sizes, place, hess, with_cores([q1] + q1_there, q1_cores), s0, (16,))
    s1_there, s1_core = gather_chip(s1, "s1"), from_core(s1, "s1")
    s0_there, s0_across = after(s1, s0_there), after(s1, s0_across)
    s0_diagonal = [gather_group(x, "s0_there") for x in s0_there]
    s0_cores = [s0_core] + flip(s0_there, "s0_there")
    s0_across_cores = flip(s0_across, "s0_across")
    last = send_parts(score("score0", sizes, place, rows, [with_cores([s0] + s0_there, s0_cores)], s1))
    s0_diagonal = [after(last, xs) for xs in s0_diagonal]
    s0_diagonal_cores = [flip(xs, "s0_diagonal") for xs in s0_diagonal]
    s1_across = gather_group(s1_long, "s1")
    s1_there = after(last, s1_there)
    s1_across = after(last, s1_across)
    s1_across_cores = flip(s1_across, "s1_across")
    s1_diagonal = [gather_group(x, "s1_there") for x in s1_there]
    s1_cores = [s1_core] + flip(s1_there, "s1_there")
    pieces = []
    for j in range(groups - 1):
        ours = [s0_across[j]] + [xs[j] for xs in s0_diagonal]
        theirs = [s0_across_cores[j]] + [xs[j] for xs in s0_diagonal_cores]
        pieces.append(with_cores(ours, theirs))
    pieces.append(with_cores([s1] + s1_there, s1_cores))
    last = send_parts(score("score1", sizes, place, rows, pieces, last))
    s1_across = after(last, s1_across)
    s1_across_cores = flip(s1_across, "s1_across")
    s1_diagonal = [after(last, xs) for xs in s1_diagonal]
    s1_diagonal_cores = [flip(xs, "s1_diagonal") for xs in s1_diagonal]
    pieces = []
    for j in range(groups - 1):
        ours = [s1_across[j]] + [xs[j] for xs in s1_diagonal]
        theirs = [s1_across_cores[j]] + [xs[j] for xs in s1_diagonal_cores]
        pieces.append(with_cores(ours, theirs))
    last = send_parts(score("score2", sizes, place, rows, pieces, last))
    while any(part[0].shape[0] > 1 for part in parts):
        advance(last)
    return finish(sizes, place, parts, total)


def solution(mesh):
    groups, ex, layers = (mesh.shape[a] for a in ("groups", "ex", "layer"))
    in_specs = (P(None, "layer", "ex"), P("layer", "ex", None), P(("groups", "ex"), "layer", None))
    out_specs = P(("groups", "ex", "layer"), None)
    return jax.shard_map(
        functools.partial(shards, groups, ex, layers),
        mesh=mesh,
        in_specs=in_specs,
        out_specs=out_specs,
        check_vma=False,
    )
```

```python
import functools

import jax
import jax.numpy as jnp
from jax import lax
from jax.experimental import pallas as pl
from jax.experimental.pallas import tpu as pltpu
from jax.sharding import PartitionSpec as P

F32, BF16 = jnp.float32, jnp.bfloat16
CORES = 2
CHUNKS = 2
MIB = 1 << 20
VMEM = pl.BlockSpec(memory_space=pltpu.VMEM)
SMEM = pl.BlockSpec(memory_space=pltpu.SMEM)
ANY = pl.BlockSpec(memory_space=pl.ANY)


HBM = pl.BlockSpec(memory_space=pltpu.HBM)


def positions(groups, ex, layers, place):
    at_group, at_ex, at_layer = (ref[0] for ref in place)
    chips = ex // CORES
    chip, core = at_ex // CORES, lax.rem(at_ex, CORES)
    ids = [lax.rem(chip + k, chips) * CORES + (core ^ s) for k in range(chips) for s in range(CORES)]
    blocks = [at_layer ^ r for r in range(layers)]
    return ids, blocks, [lax.rem(at_group + j, groups) for j in range(groups)]


def load_kernel(source, after, out, sem):
    copy = pltpu.make_async_copy(source, out, sem)
    copy.start()
    copy.wait()


def load(source, after):
    return pl.pallas_call(
        load_kernel,
        out_shape=pltpu.VMEM(source.shape, BF16),
        in_specs=[HBM, ANY],
        out_specs=VMEM,
        scratch_shapes=[pltpu.SemaphoreType.DMA],
        compiler_params=pltpu.CompilerParams(vmem_limit_bytes=2 * MIB),
        name="load",
    )(pltpu.with_memory_space_constraint(source, pltpu.HBM), after)


def take_kernel(chunk, at_group, at_ex, at_layer, source, after, out, sem):
    rows = out.shape[0]
    at = pl.multiple_of((at_group[0] * CHUNKS + chunk) * rows, rows)
    copy = pltpu.make_async_copy(source.at[pl.ds(at, rows), :], out, sem)
    copy.start()
    copy.wait()


def take(chunk, place, source, after, rows):
    return pl.pallas_call(
        functools.partial(take_kernel, chunk),
        out_shape=pltpu.VMEM((rows, source.shape[1]), BF16),
        in_specs=[SMEM] * 3 + [HBM, ANY],
        out_specs=VMEM,
        scratch_shapes=[pltpu.SemaphoreType.DMA],
        compiler_params=pltpu.CompilerParams(vmem_limit_bytes=2 * MIB),
        name="take",
    )(*place, pltpu.with_memory_space_constraint(source, pltpu.HBM), after)


def runs_of(ids, at_ids, depth):
    if len(at_ids) == len(ids):
        return [ids[t] * depth for t in at_ids], [(0, 0, len(ids) * depth)]
    span = CORES * depth
    at = [(i // CORES * CORES + lax.rem(ids[t], CORES)) * depth for i, t in enumerate(at_ids)]
    return at, [(i * span, ids[t] // CORES * span, span) for i, t in enumerate(at_ids[::CORES])]


def condition_kernel(sizes, at_ids, first, *refs):
    place, (hess, *rest) = refs[:3], refs[3:]
    ids, _, _ = positions(*sizes, place)
    pieces, rest = rest[: len(at_ids)], rest[len(at_ids) + 1 :]
    before, (*outs, right) = rest[0] if first else None, rest[first:]
    depth, height = pieces[0].shape[1], hess.shape[0]
    places, runs = runs_of(ids, at_ids, depth)
    for at, piece in zip(places, pieces):
        right[:, pl.ds(pl.multiple_of(at, depth), depth)] = piece[...]
    total = before[...] if first else None
    for low, column, span in runs:
        term = lax.dot_general(
            hess[:, pl.ds(pl.multiple_of(column, depth), span)],
            right[:, low : low + span],
            (((1,), (1,)), ((), ())),
            preferred_element_type=F32,
        )
        total = term if total is None else total + term
    outs[0][...] = total.astype(outs[0].dtype)
    for out in outs[1:]:
        out[:height, :] = outs[0][...]
        if out.shape[0] > height:
            out[height:, :] = jnp.zeros((out.shape[0] - height, out.shape[1]), BF16)


def condition(sizes, place, hess, at_ids, pieces, after, more=None, before=None):
    rows, (queries, depth) = hess.shape[0], pieces[0].shape
    shapes = [((rows, queries), F32)]
    if more is not None:
        shapes = [((rows + count, queries), BF16) for count in (0, *more)]
    first = [] if before is None else [before]
    return pl.pallas_call(
        functools.partial(condition_kernel, sizes, tuple(at_ids), len(first)),
        out_shape=[pltpu.VMEM(*shape) for shape in shapes],
        in_specs=[SMEM] * 3 + [VMEM] * (1 + len(pieces)) + [ANY] + [VMEM] * len(first),
        out_specs=[VMEM] * len(shapes),
        scratch_shapes=[pltpu.VMEM((queries, len(at_ids) * depth), BF16)],
        compiler_params=pltpu.CompilerParams(vmem_limit_bytes=12 * MIB),
        name="condition" if more is not None else "condition_part",
    )(*place, hess, *pieces, after, *first)


def score_kernel(sizes, columns, direct, *refs):
    place, (store, *rest) = refs[:3], refs[3:]
    ids, blocks, _ = positions(*sizes, place)
    layers, count = len(blocks), len(ids)
    pieces, (_, *outs, right) = rest[: columns * count], rest[columns * count :]
    rows = store.shape[0] // layers
    depth, width = store.shape[1] // count, pieces[0].shape[1]
    for i, piece in enumerate(pieces):
        at = pl.ds(pl.multiple_of(ids[i % count] * depth, depth), depth)
        right[at, i // count * width : (i // count + 1) * width] = piece[:depth, :]
    for r in reversed(range(layers)) if direct else [*range(1, layers, 2), *range(0, layers, 2)]:
        at = pl.ds(pl.multiple_of(blocks[r] * rows, rows), rows)
        part = jnp.dot(store[at, :], right[...], preferred_element_type=F32)
        if direct:
            outs[r][0] = part.astype(outs[r].dtype)
            continue
        for c in range(columns):
            out = outs[2 * c + 1 - r % 2]
            out[r // 2] = part[:, c * width : (c + 1) * width].astype(out.dtype)


def score(name, sizes, place, store, pieces, after, direct=False):
    width = pieces[0][0].shape[1]
    layers, columns = sizes[2], len(pieces)
    rows = store.shape[0] // layers
    shapes = [((layers // 2, rows, width), t) for t in (BF16, F32)] * columns
    if direct:
        shapes = [((1, rows, columns * width), BF16 if r else F32) for r in range(layers)]
    flat = [x for xs in pieces for x in xs]
    made = pl.pallas_call(
        functools.partial(score_kernel, sizes, columns, direct),
        out_shape=[pltpu.VMEM(*shape) for shape in shapes],
        in_specs=[SMEM] * 3 + [VMEM] * (1 + len(flat)) + [ANY],
        out_specs=[VMEM] * len(shapes),
        scratch_shapes=[pltpu.VMEM((store.shape[1], columns * width), BF16)],
        compiler_params=pltpu.CompilerParams(vmem_limit_bytes=12 * MIB),
        name=name,
    )(*place, store, *flat, after)
    return made if direct else [made[2 * c : 2 * c + 2] for c in range(columns)]


def fold_kernel(keep, got, _, send, left):
    for r in range(keep.shape[0]):
        total = keep[r] + got[r].astype(F32)
        if r % 2:
            send[r // 2] = total.astype(BF16)
        else:
            left[r // 2] = total


def fold(keep, got, after):
    shape = (keep.shape[0] // 2,) + keep.shape[1:]
    return pl.pallas_call(
        fold_kernel,
        out_shape=(pltpu.VMEM(shape, BF16), pltpu.VMEM(shape, F32)),
        in_specs=[VMEM, VMEM, ANY],
        out_specs=(VMEM, VMEM),
        compiler_params=pltpu.CompilerParams(vmem_limit_bytes=4 * MIB),
        name="fold",
    )(keep, got, after)


def finish_kernel(sizes, counts, *refs):
    place, (*refs, out) = refs[:3], refs[3:]
    _, _, order = positions(*sizes, place)
    groups = len(order)
    span = out.shape[1] // groups
    width = span // CHUNKS
    i = 0
    for count in counts:
        (keep, *rest), refs = refs[:count], refs[count:]
        total = keep[0]
        for got in rest:
            total = total + got[0].astype(F32)
        for low in range(0, total.shape[1], width):
            at = order[i % groups] * span + i // groups * width
            out[:, pl.ds(pl.multiple_of(at, width), width)] = total[:, low : low + width]
            i += 1


def finish(sizes, place, parts, queries):
    rows = parts[0][0].shape[1]
    return pl.pallas_call(
        functools.partial(finish_kernel, sizes, tuple(map(len, parts))),
        out_shape=jax.ShapeDtypeStruct((rows, queries), F32),
        in_specs=[SMEM] * 3 + [VMEM] * sum(map(len, parts)),
        out_specs=VMEM,
        compiler_params=pltpu.CompilerParams(vmem_limit_bytes=12 * MIB),
        name="finish",
    )(*place, *[a for part in parts for a in part])


def shards(groups, ex, layers, queries, hessian, store):
    chips = ex // CORES
    sizes = groups, ex, layers
    total = queries.shape[0]
    place = [lax.axis_index(a).astype(jnp.int32)[None] for a in ("groups", "ex", "layer")]

    def permute(x, axis, perm, what):
        with jax.named_scope(what):
            return lax.ppermute(x, axis, perm)

    def from_chip(x, k, what):
        perm = [(e, (e - k * CORES) % ex) for e in range(ex)]
        return permute(x, "ex", perm, what + "_from_chip")

    def from_core(x, what):
        return permute(x, "ex", [(e, e ^ 1) for e in range(ex)], what + "_from_core")

    def from_group(x, j, what):
        perm = [(g, (g - j) % groups) for g in range(groups)]
        return permute(x, "groups", perm, what + "_from_group")

    def from_layer(x, r, what):
        return permute(x, "layer", [(z, z ^ r) for z in range(layers)], f"{what}_from_layer_{r}")

    def tie(x, *others):
        return lax.optimization_barrier((x, *others))[0]

    def gather_chip(x, what):
        return [from_chip(x, k, what) for k in range(1, chips)]

    def gather_group(x, what):
        return [from_group(x, j, what) for j in range(1, groups)]

    def with_cores(ours, theirs):
        return [x for pair in zip(ours, theirs) for x in pair]

    def flip(xs, what):
        return [from_core(x, what) for x in xs]

    def after(token, xs):
        return [tie(x, token) for x in xs]

    parts = []

    def advance(token, chain=False):
        for i, part in enumerate(parts):
            if part[0].shape[0] > 1:
                if chain and i and parts[i - 1][0].shape[0] == 1:
                    token = tie(token, parts[i - 1][1])
                send, keep = fold(part[0], part[1], token)
                step = layers // keep.shape[0] // 2
                part[:] = keep, from_layer(send, step, f"sum{i}")

    def send_parts(made):
        first = len(parts)
        advance(made[-1][1])
        for send, keep in made:
            parts.append([keep, from_layer(send, 1, f"sum{len(parts)}")])
        return parts[first - 1][0] if first else made[-1][1]

    rows = pltpu.with_memory_space_constraint(store[:, 0, :], pltpu.VMEM)
    width = total // groups // CHUNKS
    q0 = take(0, place, queries[:, 0, :], place[0], width)
    q0_there, q0_core = gather_chip(q0, "q0"), from_core(q0, "q0")
    hess = load(hessian[0], q0)
    q1 = take(1, place, queries[:, 0, :], hess, width)
    q0_there = after(q1, q0_there)
    q0_cores = [q0_core] + flip(q0_there, "q0_there")
    q1_there, q1_core = gather_chip(q1, "q1"), from_core(q1, "q1")
    s0, s0_long, s0_longer = condition(sizes, place, hess, range(ex), with_cores([q0] + q0_there, q0_cores), q1, (16, 0))
    s0_there, s0_across, s0_core = gather_chip(s0_long, "s0"), gather_group(s0_longer, "s0"), from_core(s0, "s0")
    part = condition(sizes, place, hess, range(CORES), [q1, q1_core], s0)[0]
    q1_there = after(part, q1_there)
    pieces = with_cores(q1_there, flip(q1_there, "q1_there"))
    s1, s1_long, s1_longer = condition(sizes, place, hess, range(CORES, ex), pieces, part, (0, 32), part)
    s1_there, s1_core = gather_chip(s1_longer, "s1"), from_core(s1, "s1")
    s0_there, s0_across = after(s1, s0_there), after(s1, s0_across)
    s0_diagonal = [gather_group(x, "s0_there") for x in s0_there]
    s0_cores = [s0_core] + flip(s0_there, "s0_there")
    s0_across_cores = flip(s0_across, "s0_across")
    last = send_parts(score("score0", sizes, place, rows, [with_cores([s0] + s0_there, s0_cores)], s1))
    s0_diagonal = [after(last, xs) for xs in s0_diagonal]
    s0_diagonal_cores = [flip(xs, "s0_diagonal") for xs in s0_diagonal]
    s1_across = gather_group(s1_long, "s1")
    s1_there = after(last, s1_there)
    s1_across = after(last, s1_across)
    s1_across_cores = flip(s1_across, "s1_across")
    s1_diagonal = [gather_group(x, "s1_there") for x in s1_there]
    s1_cores = [s1_core] + flip(s1_there, "s1_there")
    pieces = []
    for j in range(groups - 1):
        ours = [s0_across[j]] + [xs[j] for xs in s0_diagonal]
        theirs = [s0_across_cores[j]] + [xs[j] for xs in s0_diagonal_cores]
        pieces.append(with_cores(ours, theirs))
    pieces.append(with_cores([s1] + s1_there, s1_cores))
    last = send_parts(score("score1", sizes, place, rows, pieces, last))
    s1_across = after(last, s1_across)
    s1_across_cores = flip(s1_across, "s1_across")
    s1_diagonal = [after(last, xs) for xs in s1_diagonal]
    s1_diagonal_cores = [flip(xs, "s1_diagonal") for xs in s1_diagonal]
    pieces = []
    for j in range(groups - 1):
        ours = [s1_across[j]] + [xs[j] for xs in s1_diagonal]
        theirs = [s1_across_cores[j]] + [xs[j] for xs in s1_diagonal_cores]
        pieces.append(with_cores(ours, theirs))
    last = send_parts(score("score2", sizes, place, rows, pieces, last))
    while any(part[0].shape[0] > 1 for part in parts):
        advance(last)
    return finish(sizes, place, parts, total)


def solution(mesh):
    groups, ex, layers = (mesh.shape[a] for a in ("groups", "ex", "layer"))
    in_specs = (P(None, "layer", "ex"), P("layer", "ex", None), P(("groups", "ex"), "layer", None))
    out_specs = P(("groups", "ex", "layer"), None)
    return jax.shard_map(
        functools.partial(shards, groups, ex, layers),
        mesh=mesh,
        in_specs=in_specs,
        out_specs=out_specs,
        check_vma=False,
    )
```

```python
import functools

import jax
import jax.numpy as jnp
from jax import lax
from jax.experimental import pallas as pl
from jax.experimental.pallas import tpu as pltpu
from jax.sharding import PartitionSpec as P

F32, BF16 = jnp.float32, jnp.bfloat16
CORES = 2
CHUNKS = 2
MIB = 1 << 20
VMEM = pl.BlockSpec(memory_space=pltpu.VMEM)
SMEM = pl.BlockSpec(memory_space=pltpu.SMEM)
ANY = pl.BlockSpec(memory_space=pl.ANY)


HBM = pl.BlockSpec(memory_space=pltpu.HBM)


def positions(groups, ex, layers, place):
    at_group, at_ex, at_layer = (ref[0] for ref in place)
    chips = ex // CORES
    chip, core = at_ex // CORES, lax.rem(at_ex, CORES)
    ids = [lax.rem(chip + k, chips) * CORES + (core ^ s) for k in range(chips) for s in range(CORES)]
    blocks = [at_layer ^ r for r in range(layers)]
    return ids, blocks, [lax.rem(at_group + j, groups) for j in range(groups)]


def load_kernel(source, after, out, sem):
    copy = pltpu.make_async_copy(source, out, sem)
    copy.start()
    copy.wait()


def load(source, after):
    return pl.pallas_call(
        load_kernel,
        out_shape=pltpu.VMEM(source.shape, BF16),
        in_specs=[HBM, ANY],
        out_specs=VMEM,
        scratch_shapes=[pltpu.SemaphoreType.DMA],
        compiler_params=pltpu.CompilerParams(vmem_limit_bytes=2 * MIB),
        name="load",
    )(pltpu.with_memory_space_constraint(source, pltpu.HBM), after)


def take_kernel(chunk, at_group, at_ex, at_layer, source, after, out, sem):
    rows = out.shape[0]
    at = pl.multiple_of((at_group[0] * CHUNKS + chunk) * rows, rows)
    copy = pltpu.make_async_copy(source.at[pl.ds(at, rows), :], out, sem)
    copy.start()
    copy.wait()


def take(chunk, place, source, after, rows):
    return pl.pallas_call(
        functools.partial(take_kernel, chunk),
        out_shape=pltpu.VMEM((rows, source.shape[1]), BF16),
        in_specs=[SMEM] * 3 + [HBM, ANY],
        out_specs=VMEM,
        scratch_shapes=[pltpu.SemaphoreType.DMA],
        compiler_params=pltpu.CompilerParams(vmem_limit_bytes=2 * MIB),
        name="take",
    )(*place, pltpu.with_memory_space_constraint(source, pltpu.HBM), after)


def condition_kernel(sizes, *refs):
    place, (hess, *rest) = refs[:3], refs[3:]
    ids, _, _ = positions(*sizes, place)
    pieces, (_, *outs, right) = rest[: len(ids)], rest[len(ids) :]
    width = pieces[0].shape[1]
    for t, piece in zip(ids, pieces):
        right[:, pl.ds(pl.multiple_of(t * width, width), width)] = piece[...]
    height = hess.shape[0]
    outs[0][...] = lax.dot_general(
        hess[...], right[...], (((1,), (1,)), ((), ())), preferred_element_type=F32
    ).astype(BF16)
    for out in outs[1:]:
        out[:height, :] = outs[0][...]
        if out.shape[0] > height:
            out[height:, :] = jnp.zeros((out.shape[0] - height, out.shape[1]), BF16)


def condition(sizes, place, hess, pieces, after, more):
    rows, queries = hess.shape[0], pieces[0].shape[0]
    shapes = [(rows + count, queries) for count in (0, *more)]
    return pl.pallas_call(
        functools.partial(condition_kernel, sizes),
        out_shape=[pltpu.VMEM(shape, BF16) for shape in shapes],
        in_specs=[SMEM] * 3 + [VMEM] * (1 + len(pieces)) + [ANY],
        out_specs=[VMEM] * len(shapes),
        scratch_shapes=[pltpu.VMEM((queries, hess.shape[1]), BF16)],
        compiler_params=pltpu.CompilerParams(vmem_limit_bytes=12 * MIB),
        name="condition",
    )(*place, hess, *pieces, after)


def score_kernel(sizes, columns, direct, *refs):
    place, (store, *rest) = refs[:3], refs[3:]
    ids, blocks, _ = positions(*sizes, place)
    layers, count = len(blocks), len(ids)
    pieces, (_, *outs, right) = rest[: columns * count], rest[columns * count :]
    rows = store.shape[0] // layers
    depth, width = store.shape[1] // count, pieces[0].shape[1]
    for i, piece in enumerate(pieces):
        at = pl.ds(pl.multiple_of(ids[i % count] * depth, depth), depth)
        right[at, i // count * width : (i // count + 1) * width] = piece[:depth, :]
    for r in reversed(range(layers)) if direct else [*range(1, layers, 2), *range(0, layers, 2)]:
        at = pl.ds(pl.multiple_of(blocks[r] * rows, rows), rows)
        part = jnp.dot(store[at, :], right[...], preferred_element_type=F32)
        if direct:
            outs[r][0] = part.astype(outs[r].dtype)
            continue
        for c in range(columns):
            out = outs[2 * c + 1 - r % 2]
            out[r // 2] = part[:, c * width : (c + 1) * width].astype(out.dtype)


def score(name, sizes, place, store, pieces, after, direct=False):
    width = pieces[0][0].shape[1]
    layers, columns = sizes[2], len(pieces)
    rows = store.shape[0] // layers
    shapes = [((layers // 2, rows, width), t) for t in (BF16, F32)] * columns
    if direct:
        shapes = [((1, rows, columns * width), BF16 if r else F32) for r in range(layers)]
    flat = [x for xs in pieces for x in xs]
    made = pl.pallas_call(
        functools.partial(score_kernel, sizes, columns, direct),
        out_shape=[pltpu.VMEM(*shape) for shape in shapes],
        in_specs=[SMEM] * 3 + [VMEM] * (1 + len(flat)) + [ANY],
        out_specs=[VMEM] * len(shapes),
        scratch_shapes=[pltpu.VMEM((store.shape[1], columns * width), BF16)],
        compiler_params=pltpu.CompilerParams(vmem_limit_bytes=12 * MIB),
        name=name,
    )(*place, store, *flat, after)
    return made if direct else [made[2 * c : 2 * c + 2] for c in range(columns)]


def fold_kernel(keep, got, _, send, left):
    for r in range(keep.shape[0]):
        total = keep[r] + got[r].astype(F32)
        if r % 2:
            send[r // 2] = total.astype(BF16)
        else:
            left[r // 2] = total


def fold(keep, got, after):
    shape = (keep.shape[0] // 2,) + keep.shape[1:]
    return pl.pallas_call(
        fold_kernel,
        out_shape=(pltpu.VMEM(shape, BF16), pltpu.VMEM(shape, F32)),
        in_specs=[VMEM, VMEM, ANY],
        out_specs=(VMEM, VMEM),
        compiler_params=pltpu.CompilerParams(vmem_limit_bytes=4 * MIB),
        name="fold",
    )(keep, got, after)


def finish_kernel(sizes, counts, *refs):
    place, (*refs, out) = refs[:3], refs[3:]
    _, _, order = positions(*sizes, place)
    groups = len(order)
    span = out.shape[1] // groups
    width = span // CHUNKS
    i = 0
    for count in counts:
        (keep, *rest), refs = refs[:count], refs[count:]
        total = keep[0]
        for got in rest:
            total = total + got[0].astype(F32)
        for low in range(0, total.shape[1], width):
            at = order[i % groups] * span + i // groups * width
            out[:, pl.ds(pl.multiple_of(at, width), width)] = total[:, low : low + width]
            i += 1


def finish(sizes, place, parts, queries):
    rows = parts[0][0].shape[1]
    return pl.pallas_call(
        functools.partial(finish_kernel, sizes, tuple(map(len, parts))),
        out_shape=jax.ShapeDtypeStruct((rows, queries), F32),
        in_specs=[SMEM] * 3 + [VMEM] * sum(map(len, parts)),
        out_specs=VMEM,
        compiler_params=pltpu.CompilerParams(vmem_limit_bytes=12 * MIB),
        name="finish",
    )(*place, *[a for part in parts for a in part])


def shards(groups, ex, layers, queries, hessian, store):
    chips = ex // CORES
    sizes = groups, ex, layers
    total = queries.shape[0]
    place = [lax.axis_index(a).astype(jnp.int32)[None] for a in ("groups", "ex", "layer")]

    def permute(x, axis, perm, what):
        with jax.named_scope(what):
            return lax.ppermute(x, axis, perm)

    def from_chip(x, k, what):
        perm = [(e, (e - k * CORES) % ex) for e in range(ex)]
        return permute(x, "ex", perm, what + "_from_chip")

    def from_core(x, what):
        return permute(x, "ex", [(e, e ^ 1) for e in range(ex)], what + "_from_core")

    def from_group(x, j, what):
        perm = [(g, (g - j) % groups) for g in range(groups)]
        return permute(x, "groups", perm, what + "_from_group")

    def from_layer(x, r, what):
        return permute(x, "layer", [(z, z ^ r) for z in range(layers)], f"{what}_from_layer_{r}")

    def tie(x, *others):
        return lax.optimization_barrier((x, *others))[0]

    def gather_chip(x, what):
        return [from_chip(x, k, what) for k in range(1, chips)]

    def gather_group(x, what):
        return [from_group(x, j, what) for j in range(1, groups)]

    def with_cores(ours, theirs):
        return [x for pair in zip(ours, theirs) for x in pair]

    def flip(xs, what):
        return [from_core(x, what) for x in xs]

    def after(token, xs):
        return [tie(x, token) for x in xs]

    parts = []

    def advance(token, chain=False):
        for i, part in enumerate(parts):
            if part[0].shape[0] > 1:
                if chain and i and parts[i - 1][0].shape[0] == 1:
                    token = tie(token, parts[i - 1][1])
                send, keep = fold(part[0], part[1], token)
                step = layers // keep.shape[0] // 2
                part[:] = keep, from_layer(send, step, f"sum{i}")

    def send_parts(made):
        first = len(parts)
        advance(made[-1][1])
        for send, keep in made:
            parts.append([keep, from_layer(send, 1, f"sum{len(parts)}")])
        return parts[first - 1][0] if first else made[-1][1]

    rows = pltpu.with_memory_space_constraint(store[:, 0, :], pltpu.VMEM)
    width = total // groups // CHUNKS
    q0 = take(0, place, queries[:, 0, :], place[0], width)
    q0_there, q0_core = gather_chip(q0, "q0"), from_core(q0, "q0")
    hess = load(hessian[0], q0)
    q1 = take(1, place, queries[:, 0, :], hess, width)
    q0_there = after(q1, q0_there)
    q0_cores = [q0_core] + flip(q0_there, "q0_there")
    q1_there, q1_core = gather_chip(q1, "q1"), from_core(q1, "q1")
    s0, s0_long, s0_longer = condition(sizes, place, hess, with_cores([q0] + q0_there, q0_cores), q1, (16, 0))
    s0_there, s0_across, s0_core = gather_chip(s0_long, "s0"), gather_group(s0_longer, "s0"), from_core(s0, "s0")
    q1_there = after(s0, q1_there)
    q1_cores = [q1_core] + flip(q1_there, "q1_there")
    s1, s1_long = condition(sizes, place, hess, with_cores([q1] + q1_there, q1_cores), s0, (0,))
    s1_there, s1_core = gather_chip(s1, "s1"), from_core(s1, "s1")
    s0_there, s0_across = after(s1, s0_there), after(s1, s0_across)
    s0_diagonal = [gather_group(x, "s0_there") for x in s0_there]
    s0_cores = [s0_core] + flip(s0_there, "s0_there")
    s0_across_cores = flip(s0_across, "s0_across")
    last = send_parts(score("score0", sizes, place, rows, [with_cores([s0] + s0_there, s0_cores)], s1))
    s0_diagonal = [after(last, xs) for xs in s0_diagonal]
    s0_diagonal_cores = [flip(xs, "s0_diagonal") for xs in s0_diagonal]
    s1_across = gather_group(s1_long, "s1")
    s1_there = after(last, s1_there)
    s1_across = after(last, s1_across)
    s1_across_cores = flip(s1_across, "s1_across")
    s1_diagonal = [gather_group(x, "s1_there") for x in s1_there]
    s1_cores = [s1_core] + flip(s1_there, "s1_there")
    pieces = []
    for j in range(groups - 1):
        ours = [s0_across[j]] + [xs[j] for xs in s0_diagonal]
        theirs = [s0_across_cores[j]] + [xs[j] for xs in s0_diagonal_cores]
        pieces.append(with_cores(ours, theirs))
    pieces.append(with_cores([s1] + s1_there, s1_cores))
    last = send_parts(score("score1", sizes, place, rows, pieces, last))
    s1_across = after(last, s1_across)
    s1_across_cores = flip(s1_across, "s1_across")
    s1_diagonal = [after(last, xs) for xs in s1_diagonal]
    s1_diagonal_cores = [flip(xs, "s1_diagonal") for xs in s1_diagonal]
    pieces = []
    for j in range(groups - 1):
        ours = [s1_across[j]] + [xs[j] for xs in s1_diagonal]
        theirs = [s1_across_cores[j]] + [xs[j] for xs in s1_diagonal_cores]
        pieces.append(with_cores(ours, theirs))
    last = send_parts(score("score2", sizes, place, rows, pieces, last))
    while any(part[0].shape[0] > 1 for part in parts):
        advance(last)
    return finish(sizes, place, parts, total)


def solution(mesh):
    groups, ex, layers = (mesh.shape[a] for a in ("groups", "ex", "layer"))
    in_specs = (P(None, "layer", "ex"), P("layer", "ex", None), P(("groups", "ex"), "layer", None))
    out_specs = P(("groups", "ex", "layer"), None)
    return jax.shard_map(
        functools.partial(shards, groups, ex, layers),
        mesh=mesh,
        in_specs=in_specs,
        out_specs=out_specs,
        check_vma=False,
    )
```

```python
import functools

import jax
import jax.numpy as jnp
from jax import lax
from jax.experimental import pallas as pl
from jax.experimental.pallas import tpu as pltpu
from jax.sharding import PartitionSpec as P

F32, BF16 = jnp.float32, jnp.bfloat16
CORES = 2
CHUNKS = 2
MIB = 1 << 20
VMEM = pl.BlockSpec(memory_space=pltpu.VMEM)
SMEM = pl.BlockSpec(memory_space=pltpu.SMEM)
ANY = pl.BlockSpec(memory_space=pl.ANY)


HBM = pl.BlockSpec(memory_space=pltpu.HBM)


def positions(groups, ex, layers, place):
    at_group, at_ex, at_layer = (ref[0] for ref in place)
    chips = ex // CORES
    chip, core = at_ex // CORES, lax.rem(at_ex, CORES)
    ids = [lax.rem(chip + k, chips) * CORES + (core ^ s) for k in range(chips) for s in range(CORES)]
    blocks = [at_layer ^ r for r in range(layers)]
    return ids, blocks, [lax.rem(at_group + j, groups) for j in range(groups)]


def load_kernel(source, after, out, sem):
    copy = pltpu.make_async_copy(source, out, sem)
    copy.start()
    copy.wait()


def load(source, after):
    return pl.pallas_call(
        load_kernel,
        out_shape=pltpu.VMEM(source.shape, BF16),
        in_specs=[HBM, ANY],
        out_specs=VMEM,
        scratch_shapes=[pltpu.SemaphoreType.DMA],
        compiler_params=pltpu.CompilerParams(vmem_limit_bytes=2 * MIB),
        name="load",
    )(pltpu.with_memory_space_constraint(source, pltpu.HBM), after)


def take_kernel(chunk, at_group, at_ex, at_layer, source, after, out, sem):
    rows = out.shape[0]
    at = pl.multiple_of((at_group[0] * CHUNKS + chunk) * rows, rows)
    copy = pltpu.make_async_copy(source.at[pl.ds(at, rows), :], out, sem)
    copy.start()
    copy.wait()


def take(chunk, place, source, after, rows):
    return pl.pallas_call(
        functools.partial(take_kernel, chunk),
        out_shape=pltpu.VMEM((rows, source.shape[1]), BF16),
        in_specs=[SMEM] * 3 + [HBM, ANY],
        out_specs=VMEM,
        scratch_shapes=[pltpu.SemaphoreType.DMA],
        compiler_params=pltpu.CompilerParams(vmem_limit_bytes=2 * MIB),
        name="take",
    )(*place, pltpu.with_memory_space_constraint(source, pltpu.HBM), after)


def condition_kernel(sizes, *refs):
    place, (hess, *rest) = refs[:3], refs[3:]
    ids, _, _ = positions(*sizes, place)
    pieces, (_, *outs, right) = rest[: len(ids)], rest[len(ids) :]
    width = pieces[0].shape[1]
    for t, piece in zip(ids, pieces):
        right[:, pl.ds(pl.multiple_of(t * width, width), width)] = piece[...]
    height = hess.shape[0]
    outs[0][...] = lax.dot_general(
        hess[...], right[...], (((1,), (1,)), ((), ())), preferred_element_type=F32
    ).astype(BF16)
    for out in outs[1:]:
        out[:height, :] = outs[0][...]
        if out.shape[0] > height:
            out[height:, :] = jnp.zeros((out.shape[0] - height, out.shape[1]), BF16)


def condition(sizes, place, hess, pieces, after, more):
    rows, queries = hess.shape[0], pieces[0].shape[0]
    shapes = [(rows + count, queries) for count in (0, *more)]
    return pl.pallas_call(
        functools.partial(condition_kernel, sizes),
        out_shape=[pltpu.VMEM(shape, BF16) for shape in shapes],
        in_specs=[SMEM] * 3 + [VMEM] * (1 + len(pieces)) + [ANY],
        out_specs=[VMEM] * len(shapes),
        scratch_shapes=[pltpu.VMEM((queries, hess.shape[1]), BF16)],
        compiler_params=pltpu.CompilerParams(vmem_limit_bytes=12 * MIB),
        name="condition",
    )(*place, hess, *pieces, after)


def score_kernel(sizes, columns, direct, *refs):
    place, (store, *rest) = refs[:3], refs[3:]
    ids, blocks, _ = positions(*sizes, place)
    layers, count = len(blocks), len(ids)
    pieces, (_, *outs, right) = rest[: columns * count], rest[columns * count :]
    rows = store.shape[0] // layers
    depth, width = store.shape[1] // count, pieces[0].shape[1]
    for i, piece in enumerate(pieces):
        at = pl.ds(pl.multiple_of(ids[i % count] * depth, depth), depth)
        right[at, i // count * width : (i // count + 1) * width] = piece[:depth, :]
    for r in reversed(range(layers)) if direct else [*range(1, layers, 2), *range(0, layers, 2)]:
        at = pl.ds(pl.multiple_of(blocks[r] * rows, rows), rows)
        part = jnp.dot(store[at, :], right[...], preferred_element_type=F32)
        if direct:
            outs[r][0] = part.astype(outs[r].dtype)
            continue
        for c in range(columns):
            out = outs[2 * c + 1 - r % 2]
            out[r // 2] = part[:, c * width : (c + 1) * width].astype(out.dtype)


def score(name, sizes, place, store, pieces, after, direct=False):
    width = pieces[0][0].shape[1]
    layers, columns = sizes[2], len(pieces)
    rows = store.shape[0] // layers
    shapes = [((layers // 2, rows, width), t) for t in (BF16, F32)] * columns
    if direct:
        shapes = [((1, rows, columns * width), BF16 if r else F32) for r in range(layers)]
    flat = [x for xs in pieces for x in xs]
    made = pl.pallas_call(
        functools.partial(score_kernel, sizes, columns, direct),
        out_shape=[pltpu.VMEM(*shape) for shape in shapes],
        in_specs=[SMEM] * 3 + [VMEM] * (1 + len(flat)) + [ANY],
        out_specs=[VMEM] * len(shapes),
        scratch_shapes=[pltpu.VMEM((store.shape[1], columns * width), BF16)],
        compiler_params=pltpu.CompilerParams(vmem_limit_bytes=12 * MIB),
        name=name,
    )(*place, store, *flat, after)
    return made if direct else [made[2 * c : 2 * c + 2] for c in range(columns)]


def fold_kernel(keep, got, _, send, left):
    for r in range(keep.shape[0]):
        total = keep[r] + got[r].astype(F32)
        if r % 2:
            send[r // 2] = total.astype(BF16)
        else:
            left[r // 2] = total


def fold(keep, got, after):
    shape = (keep.shape[0] // 2,) + keep.shape[1:]
    return pl.pallas_call(
        fold_kernel,
        out_shape=(pltpu.VMEM(shape, BF16), pltpu.VMEM(shape, F32)),
        in_specs=[VMEM, VMEM, ANY],
        out_specs=(VMEM, VMEM),
        compiler_params=pltpu.CompilerParams(vmem_limit_bytes=4 * MIB),
        name="fold",
    )(keep, got, after)


def finish_kernel(sizes, where, first, *refs):
    place, refs = refs[:3], refs[3 if first else 4 :]
    out, sums, sems = refs[2 * len(where) :]
    _, _, order = positions(*sizes, place)
    copies = []
    for i, (j, low, high) in enumerate(where):
        keep, got = refs[2 * i : 2 * i + 2]
        sums[i] = keep[0] + got[0].astype(F32)
        at = pl.multiple_of(order[j] * (out.shape[1] // len(order)) + low, high - low)
        copies.append(pltpu.make_async_copy(sums.at[i], out.at[:, pl.ds(at, high - low)], sems.at[i]))
        copies[-1].start()
    for copy in copies:
        copy.wait()


def finish(sizes, place, where, parts, queries, out=None):
    _, rows, width = parts[0][0].shape
    old = [] if out is None else [out]
    return pl.pallas_call(
        functools.partial(finish_kernel, sizes, tuple(where), out is None),
        out_shape=jax.ShapeDtypeStruct((rows, queries), F32),
        in_specs=[SMEM] * 3 + [ANY] * len(old) + [VMEM] * (2 * len(parts)),
        out_specs=ANY,
        scratch_shapes=[
            pltpu.VMEM((len(parts), rows, width), F32),
            pltpu.SemaphoreType.DMA((len(parts),)),
        ],
        input_output_aliases={3: 0} if old else {},
        compiler_params=pltpu.CompilerParams(vmem_limit_bytes=12 * MIB),
        name="finish",
    )(*place, *old, *[a for part in parts for a in part])


def shards(groups, ex, layers, queries, hessian, store):
    chips = ex // CORES
    sizes = groups, ex, layers
    total = queries.shape[0]
    place = [lax.axis_index(a).astype(jnp.int32)[None] for a in ("groups", "ex", "layer")]

    def permute(x, axis, perm, what):
        with jax.named_scope(what):
            return lax.ppermute(x, axis, perm)

    def from_chip(x, k, what):
        perm = [(e, (e - k * CORES) % ex) for e in range(ex)]
        return permute(x, "ex", perm, what + "_from_chip")

    def from_core(x, what):
        return permute(x, "ex", [(e, e ^ 1) for e in range(ex)], what + "_from_core")

    def from_group(x, j, what):
        perm = [(g, (g - j) % groups) for g in range(groups)]
        return permute(x, "groups", perm, what + "_from_group")

    def from_layer(x, r, what):
        return permute(x, "layer", [(z, z ^ r) for z in range(layers)], f"{what}_from_layer_{r}")

    def tie(x, *others):
        return lax.optimization_barrier((x, *others))[0]

    def gather_chip(x, what):
        return [from_chip(x, k, what) for k in range(1, chips)]

    def gather_group(x, what):
        return [from_group(x, j, what) for j in range(1, groups)]

    def with_cores(ours, theirs):
        return [x for pair in zip(ours, theirs) for x in pair]

    def flip(xs, what):
        return [from_core(x, what) for x in xs]

    def after(token, xs):
        return [tie(x, token) for x in xs]

    parts = []

    def advance(token, chain=False):
        for i, part in enumerate(parts):
            if part[0].shape[0] > 1:
                if chain and i and parts[i - 1][0].shape[0] == 1:
                    token = tie(token, parts[i - 1][1])
                send, keep = fold(part[0], part[1], token)
                step = layers // keep.shape[0] // 2
                part[:] = keep, from_layer(send, step, f"sum{i}")

    def send_parts(made):
        first = len(parts)
        advance(made[-1][1])
        for send, keep in made:
            parts.append([keep, from_layer(send, 1, f"sum{len(parts)}")])
        return parts[first - 1][0] if first else made[-1][1]

    rows = pltpu.with_memory_space_constraint(store[:, 0, :], pltpu.VMEM)
    width = total // groups // CHUNKS
    q0 = take(0, place, queries[:, 0, :], place[0], width)
    q0_there, q0_core = gather_chip(q0, "q0"), from_core(q0, "q0")
    hess = load(hessian[0], q0)
    q1 = take(1, place, queries[:, 0, :], hess, width)
    q0_there = after(q1, q0_there)
    q0_cores = [q0_core] + flip(q0_there, "q0_there")
    q1_there, q1_core = gather_chip(q1, "q1"), from_core(q1, "q1")
    s0, s0_long, s0_longer = condition(sizes, place, hess, with_cores([q0] + q0_there, q0_cores), q1, (16, 0))
    s0_there, s0_across, s0_core = gather_chip(s0_long, "s0"), gather_group(s0_longer, "s0"), from_core(s0, "s0")
    q1_there = after(s0, q1_there)
    q1_cores = [q1_core] + flip(q1_there, "q1_there")
    s1, s1_long = condition(sizes, place, hess, with_cores([q1] + q1_there, q1_cores), s0, (0,))
    s1_there, s1_core = gather_chip(s1, "s1"), from_core(s1, "s1")
    s0_there, s0_across = after(s1, s0_there), after(s1, s0_across)
    s0_diagonal = [gather_group(x, "s0_there") for x in s0_there]
    s0_cores = [s0_core] + flip(s0_there, "s0_there")
    s0_across_cores = flip(s0_across, "s0_across")
    last = send_parts(score("score0", sizes, place, rows, [with_cores([s0] + s0_there, s0_cores)], s1))
    s0_diagonal = [after(last, xs) for xs in s0_diagonal]
    s0_diagonal_cores = [flip(xs, "s0_diagonal") for xs in s0_diagonal]
    s1_across = gather_group(s1_long, "s1")
    s1_there = after(last, s1_there)
    s1_across = after(last, s1_across)
    s1_across_cores = flip(s1_across, "s1_across")
    s1_diagonal = [gather_group(x, "s1_there") for x in s1_there]
    s1_cores = [s1_core] + flip(s1_there, "s1_there")
    pieces = []
    for j in range(groups - 1):
        ours = [s0_across[j]] + [xs[j] for xs in s0_diagonal]
        theirs = [s0_across_cores[j]] + [xs[j] for xs in s0_diagonal_cores]
        pieces.append(with_cores(ours, theirs))
    pieces.append(with_cores([s1] + s1_there, s1_cores))
    last = send_parts(score("score1", sizes, place, rows, pieces, last))
    s1_across = after(last, s1_across)
    s1_across_cores = flip(s1_across, "s1_across")
    s1_diagonal = [after(last, xs) for xs in s1_diagonal]
    s1_diagonal_cores = [flip(xs, "s1_diagonal") for xs in s1_diagonal]
    pieces = []
    for j in range(groups - 1):
        ours = [s1_across[j]] + [xs[j] for xs in s1_diagonal]
        theirs = [s1_across_cores[j]] + [xs[j] for xs in s1_diagonal_cores]
        pieces.append(with_cores(ours, theirs))
    last = send_parts(score("score2", sizes, place, rows, pieces, last))
    while any(part[0].shape[0] > 1 for part in parts):
        advance(last)
    where = [(i % groups, i // groups * width, (i // groups + 1) * width) for i in range(len(parts))]
    early = [i for i in range(len(parts)) if i % groups == 0]
    late = [i for i in range(len(parts)) if i % groups]
    out = None
    for which in (early, late):
        out = finish(sizes, place, [where[i] for i in which], [parts[i] for i in which], total, out)
    return out


def solution(mesh):
    groups, ex, layers = (mesh.shape[a] for a in ("groups", "ex", "layer"))
    in_specs = (P(None, "layer", "ex"), P("layer", "ex", None), P(("groups", "ex"), "layer", None))
    out_specs = P(("groups", "ex", "layer"), None)
    return jax.shard_map(
        functools.partial(shards, groups, ex, layers),
        mesh=mesh,
        in_specs=in_specs,
        out_specs=out_specs,
        check_vma=False,
    )
```

```python
import functools

import jax
import jax.numpy as jnp
from jax import lax
from jax.experimental import pallas as pl
from jax.experimental.pallas import tpu as pltpu
from jax.sharding import PartitionSpec as P

F32, BF16 = jnp.float32, jnp.bfloat16
CORES = 2
CHUNKS = 2
MIB = 1 << 20
VMEM = pl.BlockSpec(memory_space=pltpu.VMEM)
SMEM = pl.BlockSpec(memory_space=pltpu.SMEM)
ANY = pl.BlockSpec(memory_space=pl.ANY)


HBM = pl.BlockSpec(memory_space=pltpu.HBM)


def positions(groups, ex, layers, place):
    at_group, at_ex, at_layer = (ref[0] for ref in place)
    chips = ex // CORES
    chip, core = at_ex // CORES, lax.rem(at_ex, CORES)
    ids = [lax.rem(chip + k, chips) * CORES + (core ^ s) for k in range(chips) for s in range(CORES)]
    blocks = [at_layer ^ r for r in range(layers)]
    return ids, blocks, [lax.rem(at_group + j, groups) for j in range(groups)]


def load_kernel(source, after, out, sem):
    copy = pltpu.make_async_copy(source, out, sem)
    copy.start()
    copy.wait()


def load(source, after):
    return pl.pallas_call(
        load_kernel,
        out_shape=pltpu.VMEM(source.shape, BF16),
        in_specs=[HBM, ANY],
        out_specs=VMEM,
        scratch_shapes=[pltpu.SemaphoreType.DMA],
        compiler_params=pltpu.CompilerParams(vmem_limit_bytes=2 * MIB),
        name="load",
    )(pltpu.with_memory_space_constraint(source, pltpu.HBM), after)


def take_kernel(chunk, at_group, at_ex, at_layer, source, after, out, sem):
    rows = out.shape[0]
    at = pl.multiple_of((at_group[0] * CHUNKS + chunk) * rows, rows)
    copy = pltpu.make_async_copy(source.at[pl.ds(at, rows), :], out, sem)
    copy.start()
    copy.wait()


def take(chunk, place, source, after, rows):
    return pl.pallas_call(
        functools.partial(take_kernel, chunk),
        out_shape=pltpu.VMEM((rows, source.shape[1]), BF16),
        in_specs=[SMEM] * 3 + [HBM, ANY],
        out_specs=VMEM,
        scratch_shapes=[pltpu.SemaphoreType.DMA],
        compiler_params=pltpu.CompilerParams(vmem_limit_bytes=2 * MIB),
        name="take",
    )(*place, pltpu.with_memory_space_constraint(source, pltpu.HBM), after)


def condition_kernel(sizes, *refs):
    place, (hess, *rest) = refs[:3], refs[3:]
    ids, _, _ = positions(*sizes, place)
    pieces, (_, *outs, right) = rest[: len(ids)], rest[len(ids) :]
    width = pieces[0].shape[1]
    for t, piece in zip(ids, pieces):
        right[:, pl.ds(pl.multiple_of(t * width, width), width)] = piece[...]
    height = hess.shape[0]
    outs[0][...] = lax.dot_general(
        hess[...], right[...], (((1,), (1,)), ((), ())), preferred_element_type=F32
    ).astype(BF16)
    for out in outs[1:]:
        out[:height, :] = outs[0][...]
        if out.shape[0] > height:
            out[height:, :] = jnp.zeros((out.shape[0] - height, out.shape[1]), BF16)


def condition(sizes, place, hess, pieces, after, more):
    rows, queries = hess.shape[0], pieces[0].shape[0]
    shapes = [(rows + count, queries) for count in (0, *more)]
    return pl.pallas_call(
        functools.partial(condition_kernel, sizes),
        out_shape=[pltpu.VMEM(shape, BF16) for shape in shapes],
        in_specs=[SMEM] * 3 + [VMEM] * (1 + len(pieces)) + [ANY],
        out_specs=[VMEM] * len(shapes),
        scratch_shapes=[pltpu.VMEM((queries, hess.shape[1]), BF16)],
        compiler_params=pltpu.CompilerParams(vmem_limit_bytes=12 * MIB),
        name="condition",
    )(*place, hess, *pieces, after)


def score_kernel(sizes, columns, direct, *refs):
    place, (store, *rest) = refs[:3], refs[3:]
    ids, blocks, _ = positions(*sizes, place)
    layers, count = len(blocks), len(ids)
    pieces, (_, *outs, right) = rest[: columns * count], rest[columns * count :]
    rows = store.shape[0] // layers
    depth, width = store.shape[1] // count, pieces[0].shape[1]
    for i, piece in enumerate(pieces):
        at = pl.ds(pl.multiple_of(ids[i % count] * depth, depth), depth)
        right[at, i // count * width : (i // count + 1) * width] = piece[:depth, :]
    for r in reversed(range(layers)) if direct else [*range(1, layers, 2), *range(0, layers, 2)]:
        at = pl.ds(pl.multiple_of(blocks[r] * rows, rows), rows)
        part = jnp.dot(store[at, :], right[...], preferred_element_type=F32)
        if direct:
            outs[r][0] = part.astype(outs[r].dtype)
            continue
        for c in range(columns):
            out = outs[2 * c + 1 - r % 2]
            out[r // 2] = part[:, c * width : (c + 1) * width].astype(out.dtype)


def score(name, sizes, place, store, pieces, after, direct=False):
    width = pieces[0][0].shape[1]
    layers, columns = sizes[2], len(pieces)
    rows = store.shape[0] // layers
    shapes = [((layers // 2, rows, width), t) for t in (BF16, F32)] * columns
    if direct:
        shapes = [((1, rows, columns * width), BF16 if r else F32) for r in range(layers)]
    flat = [x for xs in pieces for x in xs]
    made = pl.pallas_call(
        functools.partial(score_kernel, sizes, columns, direct),
        out_shape=[pltpu.VMEM(*shape) for shape in shapes],
        in_specs=[SMEM] * 3 + [VMEM] * (1 + len(flat)) + [ANY],
        out_specs=[VMEM] * len(shapes),
        scratch_shapes=[pltpu.VMEM((store.shape[1], columns * width), BF16)],
        compiler_params=pltpu.CompilerParams(vmem_limit_bytes=12 * MIB),
        name=name,
    )(*place, store, *flat, after)
    return made if direct else [made[2 * c : 2 * c + 2] for c in range(columns)]


def fold_kernel(keep, got, _, send, left):
    for r in range(keep.shape[0]):
        total = keep[r] + got[r].astype(F32)
        if r % 2:
            send[r // 2] = total.astype(BF16)
        else:
            left[r // 2] = total


def fold(keep, got, after):
    shape = (keep.shape[0] // 2,) + keep.shape[1:]
    return pl.pallas_call(
        fold_kernel,
        out_shape=(pltpu.VMEM(shape, BF16), pltpu.VMEM(shape, F32)),
        in_specs=[VMEM, VMEM, ANY],
        out_specs=(VMEM, VMEM),
        compiler_params=pltpu.CompilerParams(vmem_limit_bytes=4 * MIB),
        name="fold",
    )(keep, got, after)


def finish_kernel(sizes, where, first, *refs):
    place, refs = refs[:3], refs[3 if first else 4 :]
    out, sums, sems = refs[2 * len(where) :]
    _, _, order = positions(*sizes, place)
    copies = []
    for i, (j, low, high) in enumerate(where):
        keep, got = refs[2 * i : 2 * i + 2]
        sums[i] = keep[0] + got[0].astype(F32)
        at = pl.multiple_of(order[j] * (out.shape[1] // len(order)) + low, high - low)
        copies.append(pltpu.make_async_copy(sums.at[i], out.at[:, pl.ds(at, high - low)], sems.at[i]))
        copies[-1].start()
    for copy in copies:
        copy.wait()


def finish(sizes, place, where, parts, queries, out=None):
    _, rows, width = parts[0][0].shape
    old = [] if out is None else [out]
    return pl.pallas_call(
        functools.partial(finish_kernel, sizes, tuple(where), out is None),
        out_shape=jax.ShapeDtypeStruct((rows, queries), F32),
        in_specs=[SMEM] * 3 + [ANY] * len(old) + [VMEM] * (2 * len(parts)),
        out_specs=ANY,
        scratch_shapes=[
            pltpu.VMEM((len(parts), rows, width), F32),
            pltpu.SemaphoreType.DMA((len(parts),)),
        ],
        input_output_aliases={3: 0} if old else {},
        compiler_params=pltpu.CompilerParams(vmem_limit_bytes=12 * MIB),
        name="finish",
    )(*place, *old, *[a for part in parts for a in part])


def shards(groups, ex, layers, queries, hessian, store):
    chips = ex // CORES
    sizes = groups, ex, layers
    total = queries.shape[0]
    place = [lax.axis_index(a).astype(jnp.int32)[None] for a in ("groups", "ex", "layer")]

    def permute(x, axis, perm, what):
        with jax.named_scope(what):
            return lax.ppermute(x, axis, perm)

    def from_chip(x, k, what):
        perm = [(e, (e - k * CORES) % ex) for e in range(ex)]
        return permute(x, "ex", perm, what + "_from_chip")

    def from_core(x, what):
        return permute(x, "ex", [(e, e ^ 1) for e in range(ex)], what + "_from_core")

    def from_group(x, j, what):
        perm = [(g, (g - j) % groups) for g in range(groups)]
        return permute(x, "groups", perm, what + "_from_group")

    def from_layer(x, r, what):
        return permute(x, "layer", [(z, z ^ r) for z in range(layers)], f"{what}_from_layer_{r}")

    def tie(x, *others):
        return lax.optimization_barrier((x, *others))[0]

    def gather_chip(x, what):
        return [from_chip(x, k, what) for k in range(1, chips)]

    def gather_group(x, what):
        return [from_group(x, j, what) for j in range(1, groups)]

    def with_cores(ours, theirs):
        return [x for pair in zip(ours, theirs) for x in pair]

    def flip(xs, what):
        return [from_core(x, what) for x in xs]

    def after(token, xs):
        return [tie(x, token) for x in xs]

    parts = []

    def advance(token, chain=False):
        for i, part in enumerate(parts):
            if part[0].shape[0] > 1:
                if chain and i and parts[i - 1][0].shape[0] == 1:
                    token = tie(token, parts[i - 1][1])
                send, keep = fold(part[0], part[1], token)
                step = layers // keep.shape[0] // 2
                part[:] = keep, from_layer(send, step, f"sum{i}")

    def send_parts(made):
        first = len(parts)
        advance(made[-1][1])
        for send, keep in made:
            parts.append([keep, from_layer(send, 1, f"sum{len(parts)}")])
        return parts[first - 1][0] if first else made[-1][1]

    rows = pltpu.with_memory_space_constraint(store[:, 0, :], pltpu.VMEM)
    width = total // groups // CHUNKS
    q0 = take(0, place, queries[:, 0, :], place[0], width)
    q0_there, q0_core = gather_chip(q0, "q0"), from_core(q0, "q0")
    hess = load(hessian[0], q0)
    q1 = take(1, place, queries[:, 0, :], hess, width)
    q0_there = after(q1, q0_there)
    q0_cores = [q0_core] + flip(q0_there, "q0_there")
    q1_there, q1_core = gather_chip(q1, "q1"), from_core(q1, "q1")
    s0, s0_long, s0_longer = condition(sizes, place, hess, with_cores([q0] + q0_there, q0_cores), q1, (16, 0))
    s0_there, s0_across, s0_core = gather_chip(s0_long, "s0"), gather_group(s0_longer, "s0"), from_core(s0, "s0")
    q1_there = after(s0, q1_there)
    q1_cores = [q1_core] + flip(q1_there, "q1_there")
    s1, s1_long = condition(sizes, place, hess, with_cores([q1] + q1_there, q1_cores), s0, (0,))
    s1_there, s1_core = gather_chip(s1, "s1"), from_core(s1, "s1")
    s0_there, s0_across = after(s1, s0_there), after(s1, s0_across)
    s0_diagonal = [gather_group(x, "s0_there") for x in s0_there]
    s0_cores = [s0_core] + flip(s0_there, "s0_there")
    s0_across_cores = flip(s0_across, "s0_across")
    last = send_parts(score("score0", sizes, place, rows, [with_cores([s0] + s0_there, s0_cores)], s1))
    s0_diagonal = [after(last, xs) for xs in s0_diagonal]
    s0_diagonal_cores = [flip(xs, "s0_diagonal") for xs in s0_diagonal]
    s1_across = gather_group(s1_long, "s1")
    s1_there = after(last, s1_there)
    s1_across = after(last, s1_across)
    s1_across_cores = flip(s1_across, "s1_across")
    s1_diagonal = [gather_group(x, "s1_there") for x in s1_there]
    s1_cores = [s1_core] + flip(s1_there, "s1_there")
    pieces = []
    for j in range(groups - 1):
        ours = [s0_across[j]] + [xs[j] for xs in s0_diagonal]
        theirs = [s0_across_cores[j]] + [xs[j] for xs in s0_diagonal_cores]
        pieces.append(with_cores(ours, theirs))
    pieces.append(with_cores([s1] + s1_there, s1_cores))
    last = send_parts(score("score1", sizes, place, rows, pieces, last))
    s1_across = after(last, s1_across)
    s1_across_cores = flip(s1_across, "s1_across")
    s1_diagonal = [after(last, xs) for xs in s1_diagonal]
    s1_diagonal_cores = [flip(xs, "s1_diagonal") for xs in s1_diagonal]
    pieces = []
    for j in range(groups - 1):
        ours = [s1_across[j]] + [xs[j] for xs in s1_diagonal]
        theirs = [s1_across_cores[j]] + [xs[j] for xs in s1_diagonal_cores]
        pieces.append(with_cores(ours, theirs))
    last = send_parts(score("score2", sizes, place, rows, pieces, last))
    while any(part[0].shape[0] > 1 for part in parts):
        advance(last)
    where = [(i % groups, i // groups * width, (i // groups + 1) * width) for i in range(len(parts))]
    early = [i for i in range(len(parts)) if i % groups == 0]
    late = [i for i in range(len(parts)) if i % groups]
    out = None
    for which in (early, late[:-1], late[-1:]):
        out = finish(sizes, place, [where[i] for i in which], [parts[i] for i in which], total, out)
    return out


def solution(mesh):
    groups, ex, layers = (mesh.shape[a] for a in ("groups", "ex", "layer"))
    in_specs = (P(None, "layer", "ex"), P("layer", "ex", None), P(("groups", "ex"), "layer", None))
    out_specs = P(("groups", "ex", "layer"), None)
    return jax.shard_map(
        functools.partial(shards, groups, ex, layers),
        mesh=mesh,
        in_specs=in_specs,
        out_specs=out_specs,
        check_vma=False,
    )
```
